32 devices in a mesh: row: 4 (over y, core), col: 4 (over z), bin: 2 (over x).
Axes of the slice: x: 2, y: 2, z: 4, core: 2. Of those that a mesh axis runs over, the one named last changes fastest.
Arguments:
- records: bfloat16 [4096, 6656], P('row', 'col'), may hold values from -400 to 400
- offsets: int32 [4], P('col'), may hold values from 0 to 164, as said below
- live_flags: int32 [4096], P('row'), may hold values 0 or 1
Outputs:
- cross_spectra: bfloat16 [32, 2, 4096, 4096], P('bin', None, 'row', 'col')
The draws below stay inside these ranges and needn't reach their ends.
Inputs may be any that keep to these rules, and one draw needn't show every extreme that they name: `offsets`: some window has delay 0 and some has delay 164.
All inputs are finite; a program needn't handle non-finite values. No bound on the sum of `live_flags` on one device may be relied on, other than what follows from the above.
Results may differ from the reference program's by a relative error of at most 0.007.
Values sent between devices are 32-bit elements; how exact they have to be, the bound alone decides.
No kernel may reach another device: no remote copies, remote signals or barrier semaphores. Data moves between devices by JAX's collectives and lax.ppermute only.
A program may use at most 192 MiB of HBM per device.

```python
import math
import jax
import jax.numpy as jnp
from jax import lax

C = 4096
L = 1500
NB = 32
BSTEP = 6
SLACK = 164
WIN_DEV = 1
T_DEV = 1664
TIME = 6656
WINDOWS = 4


def draw_records(key, part):
    key = jax.random.fold_in(key, 11)
    key_noise, key_gain, key_common, key_weight = jax.random.split(key, 4)
    noise_field = jax.random.normal(key_noise, (C, TIME + 1), jnp.float32)
    channel_gain = jnp.exp(jax.random.uniform(key_gain, (C, 1), jnp.float32, 0.0, 2.3))
    shared_part = 0.3
    common = jnp.clip(jax.random.normal(key_common, (1, TIME), jnp.float32), -6.0, 6.0)
    weights = jax.random.uniform(key_weight, (C, 1), jnp.float32, 0.5, 1.5)
    colored = jnp.clip(noise_field[:, 1:], -6.0, 6.0) - 0.95 * jnp.clip(noise_field[:, :-1], -6.0, 6.0)
    return (channel_gain * (colored + shared_part * weights * common)).astype(jnp.bfloat16)


def draw_offsets(key, part):
    key = jax.random.fold_in(key, 5)
    key_values, key_low, key_high = jax.random.split(key, 3)
    values = jax.random.randint(key_values, (WINDOWS,), 0, SLACK + 1)
    low_slot = jax.random.randint(key_low, (), 0, WINDOWS)
    high_slot = (low_slot + 1 + jax.random.randint(key_high, (), 0, WINDOWS - 1)) % WINDOWS
    positions = lax.iota(jnp.int32, WINDOWS)
    values = jnp.where(positions == low_slot, 0, values)
    return jnp.where(positions == high_slot, SLACK, values).astype(jnp.int32)


def touch_ends(values, key, least, top_value):
    extent = values.shape
    spot = [jax.random.randint(jax.random.fold_in(key, axis), (), 0, extent[axis]) for axis in range(len(extent))]
    values = values.at[tuple(spot)].set(least)
    longest = extent.index(max(extent))
    spot[longest] = (spot[longest] + 1) % extent[longest]
    return values.at[tuple(spot)].set(top_value)


def setup_inputs(seed: int = 0) -> dict:
    arg_keys = jax.random.split(jax.random.key(seed), 4)
    records = draw_records(jax.random.fold_in(arg_keys[3], 71), 0)
    offsets = draw_offsets(jax.random.fold_in(arg_keys[3], 71), 0)
    live_flags = touch_ends((jax.random.randint(arg_keys[2], (C,), 0, 8) < 7).astype(jnp.int32), jax.random.fold_in(arg_keys[2], 1), 0, 1)
    return dict(records=records, offsets=offsets, live_flags=live_flags)


epsilon = 1e-05

def make_table(first_bin, bin_count, length, stride):
    bin_ids = (first_bin + lax.iota(jnp.int32, bin_count) + 1) * stride
    sample_ids = lax.iota(jnp.int32, length)
    angles = (bin_ids[:, None] * sample_ids[None, :] % length).astype(jnp.float32) * (2.0 * math.pi / length)
    tapering = 0.5 - 0.5 * jnp.cos(sample_ids.astype(jnp.float32) * (2.0 * math.pi / length))
    return jnp.stack([jnp.cos(angles) * tapering, -jnp.sin(angles) * tapering]).astype(jnp.bfloat16)

def reference(records, offsets, live_flags):
    dft_table = make_table(0, NB, L, BSTEP).reshape(2 * NB, L)

    def one_window(window_id):
        first_sample = window_id // WIN_DEV * T_DEV + window_id % WIN_DEV * L + offsets[window_id]
        segment = lax.dynamic_slice_in_dim(records, first_sample.astype(jnp.int32), L, 1)
        return jnp.dot(dft_table, segment.T, preferred_element_type=jnp.float32).reshape(2, NB, C)
    spectra = lax.map(one_window, lax.iota(jnp.int32, WINDOWS))
    energy = lax.optimization_barrier(jnp.sum(spectra * spectra, axis=(1, 2))) / (2 * NB)
    scaling = live_flags.astype(jnp.float32) / jnp.sqrt(energy + epsilon)
    whitened = spectra * scaling[:, None, None, :]
    highest = lax.Precision.HIGHEST

    def one_bin(bin_id):
        block = lax.dynamic_index_in_dim(whitened, bin_id, 2, keepdims=False)
        real_part = jnp.einsum('wpc,wpd->cd', block, block, precision=highest)
        imag_part = jnp.einsum('wc,wd->cd', block[:, 1], block[:, 0], precision=highest) - jnp.einsum('wc,wd->cd', block[:, 0], block[:, 1], precision=highest)
        return (jnp.stack([real_part, imag_part]) / WINDOWS).astype(jnp.bfloat16)
    return lax.map(one_bin, lax.iota(jnp.int32, NB))
```

```python
import functools
import math

import jax
import jax.numpy as jnp
import numpy as np
from jax import lax
from jax.experimental import pallas as pl
from jax.experimental.pallas import tpu as pltpu
from jax.sharding import PartitionSpec as P

L = 1500
NB = 32
BSTEP = 6
EPSILON = 1e-05
GROUP = 4


def padded_table(width):
    k = (np.arange(NB) + 1) * BSTEP
    n = np.arange(L)
    angle = (k[:, None] * n[None, :] % L) * (2.0 * math.pi / L)
    taper = 0.5 - 0.5 * np.cos(n * (2.0 * math.pi / L))
    parts = np.stack([np.cos(angle) * taper, -np.sin(angle) * taper], axis=1)
    table = np.zeros((2 * NB, width), np.float32)
    table[:, :L] = parts.reshape(2 * NB, L)
    return jnp.asarray(table.astype(jnp.bfloat16))


def whiten_kernel(sizes, place_ref, table_ref, records_ref, live_ref, *refs):
    outs, (shifted, product) = refs[: len(sizes)], refs[len(sizes):]
    samples = records_ref.shape[1]

    @pl.when(pl.program_id(0) == 0)
    def _():
        turned = pltpu.roll(table_ref[...].astype(jnp.float32), place_ref[0], 1)
        shifted[...] = turned[:, :samples].astype(jnp.bfloat16)

    spectra = lax.dot_general(
        shifted[...], records_ref[...], (((1,), (1,)), ((), ())),
        preferred_element_type=jnp.float32,
    )
    product[...] = spectra
    energy = jnp.sum(spectra * spectra, axis=0, keepdims=True) / (2 * NB)
    scaling = live_ref[...].astype(jnp.float32) / jnp.sqrt(energy + EPSILON)
    held = 2 * sum(sizes)
    start = pl.multiple_of(place_ref[1] * held, 8)
    for size, out in zip(sizes, outs):
        out[...] = product[pl.ds(start, 2 * size), :] * scaling
        start = pl.multiple_of(start + 2 * size, 8)


def whiten(records, offset, bin_index, live, sizes):
    channels, samples = records.shape
    block = min(256, channels)
    width = -(-(samples + 128) // 128) * 128
    place = jnp.stack([offset, bin_index])
    return pl.pallas_call(
        functools.partial(whiten_kernel, sizes),
        grid_spec=pltpu.PrefetchScalarGridSpec(
            num_scalar_prefetch=1,
            grid=(channels // block,),
            in_specs=[
                pl.BlockSpec((2 * NB, width), lambda i, s: (0, 0)),
                pl.BlockSpec((block, samples), lambda i, s: (i, 0)),
                pl.BlockSpec((1, block), lambda i, s: (0, i)),
            ],
            out_specs=[pl.BlockSpec((2 * size, block), lambda i, s: (0, i)) for size in sizes],
            scratch_shapes=[
                pltpu.VMEM((2 * NB, samples), jnp.bfloat16),
                pltpu.VMEM((2 * NB, block), jnp.float32),
            ],
        ),
        out_shape=[jax.ShapeDtypeStruct((2 * size, channels), jnp.float32) for size in sizes],
        compiler_params=pltpu.CompilerParams(vmem_limit_bytes=32 * 2**20),
        cost_estimate=pl.CostEstimate(
            flops=4 * NB * samples * channels, bytes_accessed=2 * samples * channels, transcendentals=0
        ),
        name="whiten",
    )(place, padded_table(width), records, live.reshape(1, channels))


def split(values):
    high = values.astype(jnp.bfloat16).astype(jnp.float32)
    return high, values - high


def cross_kernel(windows, size, slots_ref, *refs):
    own, mirror = refs[:windows], refs[windows : 2 * windows]
    out_ref, held, left, right = refs[-4:]
    bin_id = pl.program_id(0)
    rows = 2 * GROUP
    terms = windows * rows
    groups = size // GROUP

    def gather(parts, first):
        for i, part in enumerate(parts):
            slot = slots_ref[first + i]
            for g in range(groups):
                at = pl.multiple_of(g * terms + slot * rows, 8)
                held[pl.ds(at, rows), :] = part[g * rows : (g + 1) * rows, :]

    @pl.when(bin_id == 0)
    def _():
        gather(own, 0)
        for g in range(groups):
            high, low = split(held[g * terms : (g + 1) * terms, :] * (1.0 / windows))
            stacked = jnp.concatenate([high, high, low], axis=0)
            left[g] = stacked.T.astype(jnp.bfloat16)
        gather(mirror, windows)
        for g in range(groups):
            values = held[g * terms : (g + 1) * terms, :]
            part = lax.broadcasted_iota(jnp.int32, values.shape, 0) % 2
            turned = jnp.where(
                part == 0, -pltpu.roll(values, terms - 1, 0), pltpu.roll(values, 1, 0)
            )
            for q, block in enumerate((values, turned)):
                high, low = split(block)
                stacked = jnp.concatenate([high, low, high], axis=0)
                right[g, q] = stacked.astype(jnp.bfloat16)

    group, inner = bin_id // GROUP, bin_id % GROUP
    lane = lax.broadcasted_iota(jnp.int32, (1, 3 * terms), 1)
    mask = jnp.where(lane % rows // 2 == inner, 1.0, 0.0).astype(jnp.bfloat16)
    picked = left[group] * mask
    columns = out_ref.shape[3]
    tile = min(512, columns)
    for q in range(2):
        for first in range(0, columns, tile):
            out_ref[0, q, :, first : first + tile] = jnp.dot(
                picked, right[group, q, :, first : first + tile], preferred_element_type=jnp.float32
            ).astype(jnp.bfloat16)


def cross(own, mirror, slots, so_far, first, size, bins):
    windows = len(own)
    channels = own[0].shape[1]
    terms = windows * 2 * GROUP
    groups = size // GROUP
    whole = pl.BlockSpec((2 * size, channels), lambda f, s: (0, 0))
    previous = [] if so_far is None else [so_far]
    return pl.pallas_call(
        functools.partial(cross_kernel, windows, size),
        grid_spec=pltpu.PrefetchScalarGridSpec(
            num_scalar_prefetch=1,
            grid=(size,),
            in_specs=[whole] * (2 * windows) + [pl.BlockSpec(memory_space=pl.ANY)] * len(previous),
            out_specs=pl.BlockSpec((1, 2, channels, channels), lambda f, s: (f + first, 0, 0, 0)),
            scratch_shapes=[
                pltpu.VMEM((groups * terms, channels), jnp.float32),
                pltpu.VMEM((groups, channels, 3 * terms), jnp.bfloat16),
                pltpu.VMEM((groups, 2, 3 * terms, channels), jnp.bfloat16),
            ],
        ),
        out_shape=jax.ShapeDtypeStruct((bins, 2, channels, channels), jnp.bfloat16),
        input_output_aliases={2 * windows + 1: 0} if previous else {},
        compiler_params=pltpu.CompilerParams(vmem_limit_bytes=48 * 2**20),
        cost_estimate=pl.CostEstimate(
            flops=2 * size * 2 * channels * channels * 256,
            bytes_accessed=4 * size * channels * channels,
            transcendentals=0,
        ),
        name="cross",
    )(slots, *own, *mirror, *previous)


def per_device(records, offsets, live_flags):
    row, col = lax.axis_index("row"), lax.axis_index("col")
    n = lax.axis_size("col")
    bins = NB // lax.axis_size("bin")
    sizes = (GROUP, bins - GROUP)
    spectra = whiten(records, offsets[0], lax.axis_index("bin"), live_flags, sizes)
    steps = jnp.arange(n, dtype=jnp.int32)
    slots = jnp.concatenate([(col - steps) % n, (row - steps) % n])
    moved = []
    for block in spectra:
        own = [block] + [
            lax.ppermute(block, "col", [(c, (c + s) % n) for c in range(n)]) for s in range(1, n)
        ]
        mirror = [
            lax.ppermute(
                block, ("row", "col"),
                [(r * n + w, (w + s) % n * n + r) for r in range(n) for w in range(n)],
            )
            for s in range(n)
        ]
        moved.append((own, mirror))
    out, first = None, 0
    for (own, mirror), size in zip(moved, sizes):
        out = cross(own, mirror, slots, out, first, size, bins)
        first += size
    return out


def solution(mesh):
    in_specs = (P("row", "col"), P("col"), P("row"))
    out_specs = P("bin", None, "row", "col")
    return jax.shard_map(
        per_device, mesh=mesh, in_specs=in_specs, out_specs=out_specs, check_vma=False
    )
```

```python
import functools
import math

import jax
import jax.numpy as jnp
import numpy as np
from jax import lax
from jax.experimental import pallas as pl
from jax.experimental.pallas import tpu as pltpu
from jax.sharding import PartitionSpec as P

L = 1500
NB = 32
BSTEP = 6
EPSILON = 1e-05
GROUP = 4


def padded_table(width):
    k = (np.arange(NB) + 1) * BSTEP
    n = np.arange(L)
    angle = (k[:, None] * n[None, :] % L) * (2.0 * math.pi / L)
    taper = 0.5 - 0.5 * np.cos(n * (2.0 * math.pi / L))
    parts = np.stack([np.cos(angle) * taper, -np.sin(angle) * taper], axis=1)
    table = np.zeros((2 * NB, width), np.float32)
    table[:, :L] = parts.reshape(2 * NB, L)
    return jnp.asarray(table.astype(jnp.bfloat16).astype(np.float32))


def whiten_kernel(sizes, place_ref, table_ref, records_ref, live_ref, *refs):
    outs, (shifted, product) = refs[: len(sizes)], refs[len(sizes):]
    samples = records_ref.shape[1]

    @pl.when(pl.program_id(0) == 0)
    def _():
        turned = pltpu.roll(table_ref[...], place_ref[0], 1)
        shifted[...] = turned[:, :samples].astype(jnp.bfloat16)

    spectra = lax.dot_general(
        shifted[...], records_ref[...], (((1,), (1,)), ((), ())),
        preferred_element_type=jnp.float32,
    )
    product[...] = spectra
    energy = jnp.sum(spectra * spectra, axis=0, keepdims=True) / (2 * NB)
    scaling = live_ref[...].astype(jnp.float32) / jnp.sqrt(energy + EPSILON)
    held = 2 * sum(sizes)
    start = pl.multiple_of(place_ref[1] * held, 8)
    for size, out in zip(sizes, outs):
        out[...] = product[pl.ds(start, 2 * size), :] * scaling
        start = pl.multiple_of(start + 2 * size, 8)


def whiten(records, offset, bin_index, live, sizes):
    channels, samples = records.shape
    block = min(256, channels)
    width = -(-(samples + 128) // 128) * 128
    place = jnp.stack([offset, bin_index])
    return pl.pallas_call(
        functools.partial(whiten_kernel, sizes),
        grid_spec=pltpu.PrefetchScalarGridSpec(
            num_scalar_prefetch=1,
            grid=(channels // block,),
            in_specs=[
                pl.BlockSpec((2 * NB, width), lambda i, s: (0, 0)),
                pl.BlockSpec((block, samples), lambda i, s: (i, 0)),
                pl.BlockSpec((1, block), lambda i, s: (0, i)),
            ],
            out_specs=[pl.BlockSpec((2 * size, block), lambda i, s: (0, i)) for size in sizes],
            scratch_shapes=[
                pltpu.VMEM((2 * NB, samples), jnp.bfloat16),
                pltpu.VMEM((2 * NB, block), jnp.float32),
            ],
        ),
        out_shape=[jax.ShapeDtypeStruct((2 * size, channels), jnp.float32) for size in sizes],
        compiler_params=pltpu.CompilerParams(vmem_limit_bytes=60 * 2**20),
        cost_estimate=pl.CostEstimate(
            flops=4 * NB * samples * channels, bytes_accessed=2 * samples * channels, transcendentals=0
        ),
        name="whiten",
    )(place, padded_table(width), records, live.reshape(1, channels))


def split(values):
    high = values.astype(jnp.bfloat16).astype(jnp.float32)
    return high, values - high


def stack_group(ref, group):
    rows = 2 * GROUP
    parts = [ref[w, group * rows : (group + 1) * rows, :] for w in range(ref.shape[0])]
    return jnp.concatenate(parts, axis=0)


def cross_kernel(size, wide, own, mirror, *refs):
    out_ref, left, right = refs[-3:]
    bin_id = pl.program_id(0)
    windows = own.shape[0]
    rows = 2 * GROUP
    terms = windows * rows

    @pl.when(bin_id == 0)
    def _():
        for g in range(size // GROUP):
            high, low = split(stack_group(own, g) * (1.0 / windows))
            left[g] = jnp.concatenate([high, high, low], axis=0).T.astype(jnp.bfloat16)
            values = stack_group(mirror, g)
            part = lax.broadcasted_iota(jnp.int32, values.shape, 0) % 2
            turned = jnp.where(
                part == 0, -pltpu.roll(values, terms - 1, 0), pltpu.roll(values, 1, 0)
            )
            for q, block in enumerate((values, turned)):
                high, low = split(block)
                right[g, q] = jnp.concatenate([high, low, high], axis=0).astype(jnp.bfloat16)

    group, inner = bin_id // GROUP, bin_id % GROUP
    lane = lax.broadcasted_iota(jnp.int32, (1, 3 * terms), 1)
    mask = jnp.where(lane % rows // 2 == inner, 1.0, 0.0).astype(jnp.bfloat16)
    channels = out_ref.shape[3]
    tile = min(256, channels)
    for q in range(2):
        for first in range(0, channels, tile):
            if wide:
                out_ref[0, q, first : first + tile, :] = jnp.dot(
                    left[group, first : first + tile, :] * mask, right[group, q],
                    preferred_element_type=jnp.float32,
                ).astype(jnp.bfloat16)
            else:
                out_ref[0, q, :, first : first + tile] = jnp.dot(
                    left[group] * mask, right[group, q, :, first : first + tile],
                    preferred_element_type=jnp.float32,
                ).astype(jnp.bfloat16)


def cross(own, mirror, so_far, first, size, bins, wide):
    windows, _, channels = own.shape
    terms = windows * 2 * GROUP
    groups = size // GROUP
    whole = pl.BlockSpec(own.shape, lambda f: (0, 0, 0))
    previous = [] if so_far is None else [so_far]
    return pl.pallas_call(
        functools.partial(cross_kernel, size, wide),
        grid=(size,),
        in_specs=[whole] * 2 + [pl.BlockSpec(memory_space=pl.ANY)] * len(previous),
        out_specs=pl.BlockSpec((1, 2, channels, channels), lambda f: (f + first, 0, 0, 0)),
        scratch_shapes=[
            pltpu.VMEM((groups, channels, 3 * terms), jnp.bfloat16),
            pltpu.VMEM((groups, 2, 3 * terms, channels), jnp.bfloat16),
        ],
        out_shape=jax.ShapeDtypeStruct((bins, 2, channels, channels), jnp.bfloat16),
        input_output_aliases={2: 0} if previous else {},
        compiler_params=pltpu.CompilerParams(vmem_limit_bytes=48 * 2**20),
        cost_estimate=pl.CostEstimate(
            flops=2 * size * 2 * channels * channels * 256,
            bytes_accessed=4 * size * channels * channels,
            transcendentals=0,
        ),
        name="cross",
    )(own, mirror, *previous)


def per_device(records, offsets, live_flags):
    n = lax.axis_size("col")
    bins = NB // lax.axis_size("bin")
    sizes = (GROUP, bins - GROUP)
    spectra = whiten(records, offsets[0], lax.axis_index("bin"), live_flags, sizes)
    swap = [(r * n + w, w * n + r) for r in range(n) for w in range(n)]
    moved = []
    for block in spectra:
        if moved:
            block, _ = lax.optimization_barrier((block, moved[-1][0]))
        other = lax.ppermute(block, ("row", "col"), swap)
        own, mirror = (
            lax.all_to_all(jnp.broadcast_to(x[None], (n, *x.shape)), axis, 0, 0)
            for x, axis in ((block, "col"), (other, "row"))
        )
        moved.append((own, mirror))
    out, first = None, 0
    for (own, mirror), size in zip(moved, sizes):
        out = cross(own, mirror, out, first, size, bins, first > 0)
        first += size
    return out


def solution(mesh):
    in_specs = (P("row", "col"), P("col"), P("row"))
    out_specs = P("bin", None, "row", "col")
    return jax.shard_map(
        per_device, mesh=mesh, in_specs=in_specs, out_specs=out_specs, check_vma=False
    )
```

```python
import functools
import math

import jax
import jax.numpy as jnp
import numpy as np
from jax import lax
from jax.experimental import pallas as pl
from jax.experimental.pallas import tpu as pltpu
from jax.sharding import PartitionSpec as P

L = 1500
NB = 32
BSTEP = 6
EPSILON = 1e-05
GROUP = 4


def padded_table(width):
    k = (np.arange(NB) + 1) * BSTEP
    n = np.arange(L)
    angle = (k[:, None] * n[None, :] % L) * (2.0 * math.pi / L)
    taper = 0.5 - 0.5 * np.cos(n * (2.0 * math.pi / L))
    parts = np.stack([np.cos(angle) * taper, -np.sin(angle) * taper], axis=1)
    table = np.zeros((2 * NB, width), np.float32)
    table[:, :L] = parts.reshape(2 * NB, L)
    return jnp.asarray(table.astype(jnp.bfloat16).astype(np.float32))


def whiten_kernel(
    place_ref, table_hbm, records_hbm, live_hbm, out_ref, table, records, live, shifted, product, sems
):
    pieces, block, samples = records.shape
    copies = [
        pltpu.make_async_copy(table_hbm, table, sems.at[0]),
        pltpu.make_async_copy(live_hbm, live, sems.at[1]),
    ]
    for i in range(pieces):
        source = records_hbm.at[pl.ds(i * block, block)]
        copies.append(pltpu.make_async_copy(source, records.at[i], sems.at[2 + i]))
    for copy in copies:
        copy.start()
    copies[0].wait()
    turned = pltpu.roll(table[...], place_ref[0], 1)
    shifted[...] = turned[:, :samples].astype(jnp.bfloat16)
    copies[1].wait()
    held = out_ref.shape[0]
    start = pl.multiple_of(place_ref[1] * held, 8)
    for i in range(pieces):
        copies[2 + i].wait()
        spectra = lax.dot_general(
            shifted[...], records[i], (((1,), (1,)), ((), ())),
            preferred_element_type=jnp.float32,
        )
        product[...] = spectra
        energy = jnp.sum(spectra * spectra, axis=0, keepdims=True) / (2 * NB)
        columns = slice(i * block, (i + 1) * block)
        scaling = live[:, columns].astype(jnp.float32) / jnp.sqrt(energy + EPSILON)
        out_ref[:, columns] = product[pl.ds(start, held), :] * scaling


def whiten(records, offset, bin_index, live, bins):
    channels, samples = records.shape
    block = min(256, channels)
    pieces = channels // block
    width = -(-(samples + 128) // 128) * 128
    place = jnp.stack([offset, bin_index])
    return pl.pallas_call(
        whiten_kernel,
        in_specs=[pl.BlockSpec(memory_space=pltpu.SMEM)] + [pl.BlockSpec(memory_space=pl.ANY)] * 3,
        out_specs=pl.BlockSpec(memory_space=pltpu.VMEM),
        scratch_shapes=[
            pltpu.VMEM((2 * NB, width), jnp.float32),
            pltpu.VMEM((pieces, block, samples), jnp.bfloat16),
            pltpu.VMEM((1, channels), jnp.int32),
            pltpu.VMEM((2 * NB, samples), jnp.bfloat16),
            pltpu.VMEM((2 * NB, block), jnp.float32),
            pltpu.SemaphoreType.DMA((2 + pieces,)),
        ],
        out_shape=jax.ShapeDtypeStruct((2 * bins, channels), jnp.float32),
        compiler_params=pltpu.CompilerParams(vmem_limit_bytes=61 * 2**20),
        cost_estimate=pl.CostEstimate(
            flops=4 * NB * samples * channels, bytes_accessed=2 * samples * channels, transcendentals=0
        ),
        name="whiten",
    )(place, padded_table(width), records, live.reshape(1, channels))


def split(values):
    high = values.astype(jnp.bfloat16).astype(jnp.float32)
    return high, values - high


def cross_kernel(size, first, turn_ref, own_low, own_high, mirror_low, mirror_high, *refs):
    out_hbm, held, left, right, done, sems = refs[-6:]
    step = pl.program_id(0)
    half = own_low.shape[0]
    windows = 2 * half
    rows = 2 * GROUP
    terms = windows * rows
    channels = out_hbm.shape[3]
    tile = min(256, channels)
    tiles = channels // tile

    def gather(low, high, turn, group):
        for w in range(windows):
            part = (low if w < half else high)[w % half, group * rows : (group + 1) * rows, :]
            held[pl.ds(pl.multiple_of((w ^ turn) * rows, 8), rows), :] = part

    def copy(f, slot, q, t):
        piece = pl.ds(t * tile, tile)
        return pltpu.make_async_copy(
            done.at[slot, q, piece], out_hbm.at[first + f, q, piece], sems.at[slot, q * tiles + t]
        )

    @pl.when(step == 0)
    def _():
        for g in range(size // GROUP):
            gather(own_low, own_high, 0, g)
            high, low = split(held[...] * (1.0 / windows))
            left[g] = jnp.concatenate([high, high, low], axis=0).T.astype(jnp.bfloat16)
            gather(mirror_low, mirror_high, turn_ref[0], g)
            values = held[...]
            part = lax.broadcasted_iota(jnp.int32, values.shape, 0) % 2
            turned = jnp.where(
                part == 0, -pltpu.roll(values, terms - 1, 0), pltpu.roll(values, 1, 0)
            )
            for q, block in enumerate((values, turned)):
                high, low = split(block)
                right[g, q] = jnp.concatenate([high, low, high], axis=0).astype(jnp.bfloat16)

    group, inner = step // GROUP, step % GROUP
    slot = step % 2
    lane = lax.broadcasted_iota(jnp.int32, (1, 3 * terms), 1)
    mask = jnp.where(lane % rows // 2 == inner, 1.0, 0.0).astype(jnp.bfloat16)
    for q in range(2):
        for t in range(tiles):
            @pl.when(step >= 2)
            def _():
                copy(step - 2, slot, q, t).wait()

            done[slot, q, t * tile : (t + 1) * tile, :] = jnp.dot(
                left[group, t * tile : (t + 1) * tile, :] * mask, right[group, q],
                preferred_element_type=jnp.float32,
            ).astype(jnp.bfloat16)
            copy(step, slot, q, t).start()

    @pl.when(step == size - 1)
    def _():
        for f in (size - 2, size - 1):
            for q in range(2):
                for t in range(tiles):
                    copy(f, f % 2, q, t).wait()


def cross(turn, own, mirror, so_far, first, size, bins):
    windows = 2 * own[0].shape[0]
    channels = own[0].shape[2]
    terms = windows * 2 * GROUP
    groups = size // GROUP
    tiles = channels // min(256, channels)
    previous = [] if so_far is None else [so_far]
    return pl.pallas_call(
        functools.partial(cross_kernel, size, first),
        grid_spec=pltpu.PrefetchScalarGridSpec(
            num_scalar_prefetch=1,
            grid=(size,),
            in_specs=[pl.BlockSpec(x.shape, lambda f, s: (0, 0, 0)) for x in (*own, *mirror)]
            + [pl.BlockSpec(memory_space=pl.ANY)] * len(previous),
            out_specs=pl.BlockSpec(memory_space=pl.ANY),
            scratch_shapes=[
                pltpu.VMEM((terms, channels), jnp.float32),
                pltpu.VMEM((groups, channels, 3 * terms), jnp.bfloat16),
                pltpu.VMEM((groups, 2, 3 * terms, channels), jnp.bfloat16),
                pltpu.VMEM((2, 2, channels, channels), jnp.bfloat16),
                pltpu.SemaphoreType.DMA((2, 2 * tiles)),
            ],
        ),
        out_shape=jax.ShapeDtypeStruct((bins, 2, channels, channels), jnp.bfloat16),
        input_output_aliases={5: 0} if previous else {},
        compiler_params=pltpu.CompilerParams(vmem_limit_bytes=48 * 2**20),
        cost_estimate=pl.CostEstimate(
            flops=2 * size * 2 * channels * channels * 256,
            bytes_accessed=4 * size * channels * channels,
            transcendentals=0,
        ),
        name="cross",
    )(turn, *own, *mirror, *previous)


def exchange(block, axis, distance):
    n = lax.axis_size(axis)
    return lax.ppermute(block, axis, [(i, i ^ distance) for i in range(n)])


def double(block, axis):
    held, distance = block[None], 1
    while distance < lax.axis_size(axis) // 2:
        held = jnp.concatenate([held, exchange(held, axis, distance)])
        distance *= 2
    return held


def per_device(records, offsets, live_flags):
    row, col = lax.axis_index("row"), lax.axis_index("col")
    n = lax.axis_size("col")
    bins = NB // lax.axis_size("bin")
    sizes = (GROUP, bins - GROUP)
    whitened = whiten(records, offsets[0], lax.axis_index("bin"), live_flags, bins)
    turn = (row ^ col).reshape(1)
    other = lax.ppermute(
        whitened, ("row", "col"), [(r * n + w, w * n + r) for r in range(n) for w in range(n)]
    )
    own, mirror = double(whitened, "col"), double(other, "row")
    parts, first = [], 0
    for size in sizes:
        rows = slice(2 * first, 2 * (first + size))
        halves = (own[:, rows], mirror[:, rows])
        parts.append([(x, exchange(x, axis, n // 2)) for x, axis in zip(halves, ("col", "row"))])
        first += size
    out, first = None, 0
    for size, (own_pair, mirror_pair) in zip(sizes, parts):
        out = cross(turn, own_pair, mirror_pair, out, first, size, bins)
        first += size
    return out


def solution(mesh):
    in_specs = (P("row", "col"), P("col"), P("row"))
    out_specs = P("bin", None, "row", "col")
    return jax.shard_map(
        per_device, mesh=mesh, in_specs=in_specs, out_specs=out_specs, check_vma=False
    )
```

```python
import functools
import math

import jax
import jax.numpy as jnp
import numpy as np
from jax import lax
from jax.experimental import pallas as pl
from jax.experimental.pallas import tpu as pltpu
from jax.sharding import PartitionSpec as P

L = 1500
NB = 32
BSTEP = 6
EPSILON = 1e-05
GROUP = 4


def padded_table(width):
    k = (np.arange(NB) + 1) * BSTEP
    n = np.arange(L)
    angle = (k[:, None] * n[None, :] % L) * (2.0 * math.pi / L)
    taper = 0.5 - 0.5 * np.cos(n * (2.0 * math.pi / L))
    parts = np.stack([np.cos(angle) * taper, -np.sin(angle) * taper], axis=1)
    table = np.zeros((2 * NB, width), np.float32)
    table[:, :L] = parts.reshape(2 * NB, L)
    return jnp.asarray(table.astype(jnp.bfloat16).astype(np.float32))


def whiten_kernel(
    offset_ref, table_hbm, records_hbm, live_hbm, out_ref, table, records, live, shifted, product, sems
):
    pieces, block, samples = records.shape
    copies = [
        pltpu.make_async_copy(table_hbm, table, sems.at[0]),
        pltpu.make_async_copy(live_hbm, live, sems.at[1]),
    ]
    for i in range(pieces):
        source = records_hbm.at[pl.ds(i * block, block)]
        copies.append(pltpu.make_async_copy(source, records.at[i], sems.at[2 + i]))
    for copy in copies:
        copy.start()
    copies[0].wait()
    turned = pltpu.roll(table[...], offset_ref[0], 1)
    shifted[...] = turned[:, :samples].astype(jnp.bfloat16)
    copies[1].wait()
    held = out_ref.shape[0]
    start = pl.multiple_of(lax.axis_index("bin") * held, 8)
    for i in range(pieces):
        copies[2 + i].wait()
        spectra = lax.dot_general(
            records[i], shifted[...], (((1,), (1,)), ((), ())),
            preferred_element_type=jnp.float32,
        ).T
        product[i] = spectra
        energy = jnp.sum(spectra * spectra, axis=0, keepdims=True) / (2 * NB)
        columns = slice(i * block, (i + 1) * block)
        scaling = live[:, columns].astype(jnp.float32) / jnp.sqrt(energy + EPSILON)
        out_ref[:, columns] = product[i, pl.ds(start, held), :] * scaling


def whiten(records, offsets, live, bins):
    channels, samples = records.shape
    block = min(256, channels)
    pieces = channels // block
    width = -(-(samples + 128) // 128) * 128
    return pl.pallas_call(
        whiten_kernel,
        in_specs=[pl.BlockSpec(memory_space=pltpu.SMEM)] + [pl.BlockSpec(memory_space=pl.ANY)] * 3,
        out_specs=pl.BlockSpec(memory_space=pltpu.VMEM),
        scratch_shapes=[
            pltpu.VMEM((2 * NB, width), jnp.float32),
            pltpu.VMEM((pieces, block, samples), jnp.bfloat16),
            pltpu.VMEM((1, channels), jnp.int32),
            pltpu.VMEM((2 * NB, samples), jnp.bfloat16),
            pltpu.VMEM((pieces, 2 * NB, block), jnp.float32),
            pltpu.SemaphoreType.DMA((2 + pieces,)),
        ],
        out_shape=jax.ShapeDtypeStruct((2 * bins, channels), jnp.float32),
        compiler_params=pltpu.CompilerParams(vmem_limit_bytes=61 * 2**20),
        cost_estimate=pl.CostEstimate(
            flops=4 * NB * samples * channels, bytes_accessed=2 * samples * channels, transcendentals=0
        ),
        name="whiten",
    )(offsets, padded_table(width), records, live.reshape(1, channels))


def split(values):
    high = values.astype(jnp.bfloat16).astype(jnp.float32)
    return high, values - high


def cross_kernel(size, first, wide, turn_ref, own_low, own_high, mirror_low, mirror_high, *refs):
    out_hbm, held, left, right, done, sems = refs[-6:]
    step = pl.program_id(0)
    half = own_low.shape[0]
    windows = 2 * half
    rows = 2 * GROUP
    terms = windows * rows
    channels = out_hbm.shape[3]
    tile = min(256, channels)
    tiles = channels // tile

    def gather(low, high, turn, group):
        for w in range(windows):
            part = (low if w < half else high)[w % half, group * rows : (group + 1) * rows, :]
            held[pl.ds(pl.multiple_of((w ^ turn) * rows, 8), rows), :] = part

    def copy(f, slot, q, t):
        piece = pl.ds(t * tile, tile)
        return pltpu.make_async_copy(
            done.at[slot, q, piece], out_hbm.at[first + f, q, piece], sems.at[slot, q * tiles + t]
        )

    @pl.when(step == 0)
    def _():
        for g in range(size // GROUP):
            gather(own_low, own_high, 0, g)
            high, low = split(held[...] * (1.0 / windows))
            left[g] = jnp.concatenate([high, high, low], axis=0).T.astype(jnp.bfloat16)
            gather(mirror_low, mirror_high, turn_ref[0], g)
            values = held[...]
            part = lax.broadcasted_iota(jnp.int32, values.shape, 0) % 2
            turned = jnp.where(
                part == 0, -pltpu.roll(values, terms - 1, 0), pltpu.roll(values, 1, 0)
            )
            for q, block in enumerate((values, turned)):
                high, low = split(block)
                right[g, q] = jnp.concatenate([high, low, high], axis=0).astype(jnp.bfloat16)

    group, inner = step // GROUP, step % GROUP
    slot = step % 2
    lane = lax.broadcasted_iota(jnp.int32, (1, 3 * terms), 1)
    mask = jnp.where(lane % rows // 2 == inner, 1.0, 0.0).astype(jnp.bfloat16)
    pieces = [(q, t) for q in range(2) for t in range(tiles)]

    @pl.when(step >= 2)
    def _():
        for q, t in pieces:
            copy(step - 2, slot, q, t).wait()

    picked = left[group] * mask
    for q, t in pieces:
        if wide:
            done[slot, q, t * tile : (t + 1) * tile, :] = jnp.dot(
                picked[t * tile : (t + 1) * tile], right[group, q], preferred_element_type=jnp.float32
            ).astype(jnp.bfloat16)
        else:
            done[slot, q, :, t * tile : (t + 1) * tile] = jnp.dot(
                picked, right[group, q, :, t * tile : (t + 1) * tile], preferred_element_type=jnp.float32
            ).astype(jnp.bfloat16)
    for q, t in pieces:
        copy(step, slot, q, t).start()

    @pl.when(step == size - 1)
    def _():
        for f in (size - 2, size - 1):
            for q, t in pieces:
                copy(f, f % 2, q, t).wait()


def cross(turn, own, mirror, so_far, first, size, bins):
    windows = 2 * own[0].shape[0]
    channels = own[0].shape[2]
    terms = windows * 2 * GROUP
    groups = size // GROUP
    tiles = channels // min(256, channels)
    previous = [] if so_far is None else [so_far]
    return pl.pallas_call(
        functools.partial(cross_kernel, size, first, first > 0),
        grid_spec=pltpu.PrefetchScalarGridSpec(
            num_scalar_prefetch=1,
            grid=(size,),
            in_specs=[pl.BlockSpec(x.shape, lambda f, s: (0, 0, 0)) for x in (*own, *mirror)]
            + [pl.BlockSpec(memory_space=pl.ANY)] * len(previous),
            out_specs=pl.BlockSpec(memory_space=pl.ANY),
            scratch_shapes=[
                pltpu.VMEM((terms, channels), jnp.float32),
                pltpu.VMEM((groups, channels, 3 * terms), jnp.bfloat16),
                pltpu.VMEM((groups, 2, 3 * terms, channels), jnp.bfloat16),
                pltpu.VMEM((2, 2, channels, channels), jnp.bfloat16),
                pltpu.SemaphoreType.DMA((2, 2 * tiles)),
            ],
        ),
        out_shape=jax.ShapeDtypeStruct((bins, 2, channels, channels), jnp.bfloat16),
        input_output_aliases={5: 0} if previous else {},
        compiler_params=pltpu.CompilerParams(vmem_limit_bytes=48 * 2**20),
        cost_estimate=pl.CostEstimate(
            flops=2 * size * 2 * channels * channels * 256,
            bytes_accessed=4 * size * channels * channels,
            transcendentals=0,
        ),
        name="cross",
    )(turn, *own, *mirror, *previous)


def exchange(block, axis, distance):
    n = lax.axis_size(axis)
    return lax.ppermute(block, axis, [(i, i ^ distance) for i in range(n)])


def double(block, axis):
    held, distance = block[None], 1
    while distance < lax.axis_size(axis) // 2:
        held = jnp.concatenate([held, exchange(held, axis, distance)])
        distance *= 2
    return held


def per_device(records, offsets, live_flags):
    row, col = lax.axis_index("row"), lax.axis_index("col")
    n = lax.axis_size("col")
    bins = NB // lax.axis_size("bin")
    sizes = (GROUP, bins - GROUP)
    whitened = whiten(records, offsets, live_flags, bins)
    turn = (row ^ col).reshape(1)
    other = lax.ppermute(
        whitened, ("row", "col"), [(r * n + w, w * n + r) for r in range(n) for w in range(n)]
    )
    own, mirror = double(whitened, "col"), double(other, "row")
    parts, first = [], 0
    for size in sizes:
        rows = slice(2 * first, 2 * (first + size))
        halves = (own[:, rows], mirror[:, rows])
        parts.append([(x, exchange(x, axis, n // 2)) for x, axis in zip(halves, ("col", "row"))])
        first += size
    out, first = None, 0
    for size, (own_pair, mirror_pair) in zip(sizes, parts):
        out = cross(turn, own_pair, mirror_pair, out, first, size, bins)
        first += size
    return out


def solution(mesh):
    in_specs = (P("row", "col"), P("col"), P("row"))
    out_specs = P("bin", None, "row", "col")
    return jax.shard_map(
        per_device, mesh=mesh, in_specs=in_specs, out_specs=out_specs, check_vma=False
    )
```

```python
import functools
import math

import jax
import jax.numpy as jnp
import numpy as np
from jax import lax
from jax.experimental import pallas as pl
from jax.experimental.pallas import tpu as pltpu
from jax.sharding import PartitionSpec as P

L = 1500
NB = 32
BSTEP = 6
EPSILON = 1e-05
GROUP = 4
CHUNK = 128
SLOTS = 8


def padded_table(width):
    k = (np.arange(NB) + 1) * BSTEP
    n = np.arange(L)
    angle = (k[:, None] * n[None, :] % L) * (2.0 * math.pi / L)
    taper = 0.5 - 0.5 * np.cos(n * (2.0 * math.pi / L))
    parts = np.stack([np.cos(angle) * taper, -np.sin(angle) * taper], axis=1)
    table = np.zeros((2 * NB, width), np.float32)
    table[:, :L] = parts.reshape(2 * NB, L)
    return jnp.asarray(table.astype(jnp.bfloat16).astype(np.float32))


def whiten_kernel(
    offset_ref, table_hbm, records_hbm, live_hbm, *refs
):
    outs, (table, records, live, shifted, product, sems) = refs[:-6], refs[-6:]
    pieces, block, samples = records.shape
    copies = [
        pltpu.make_async_copy(table_hbm, table, sems.at[0]),
        pltpu.make_async_copy(live_hbm, live, sems.at[1]),
    ]
    for i in range(pieces):
        source = records_hbm.at[pl.ds(i * block, block)]
        copies.append(pltpu.make_async_copy(source, records.at[i], sems.at[2 + i]))
    for copy in copies:
        copy.start()
    copies[0].wait()
    turned = pltpu.roll(table[...], offset_ref[0], 1)
    shifted[...] = turned[:, :samples].astype(jnp.bfloat16)
    copies[1].wait()
    held = sum(out.shape[0] for out in outs)
    start = pl.multiple_of(lax.axis_index("bin") * held, 8)
    for i in range(pieces):
        copies[2 + i].wait()
        spectra = lax.dot_general(
            records[i], shifted[...], (((1,), (1,)), ((), ())),
            preferred_element_type=jnp.float32,
        ).T
        product[i] = spectra
        energy = jnp.sum(spectra * spectra, axis=0, keepdims=True) / (2 * NB)
        columns = slice(i * block, (i + 1) * block)
        scaling = live[:, columns].astype(jnp.float32) / jnp.sqrt(energy + EPSILON)
        at = start
        for out in outs:
            out[:, columns] = product[i, pl.ds(at, out.shape[0]), :] * scaling
            at = pl.multiple_of(at + out.shape[0], 8)


def whiten(records, offsets, live, sizes):
    channels, samples = records.shape
    block = min(256, channels)
    pieces = channels // block
    width = -(-(samples + 128) // 128) * 128
    return pl.pallas_call(
        whiten_kernel,
        in_specs=[pl.BlockSpec(memory_space=pltpu.SMEM)] + [pl.BlockSpec(memory_space=pl.ANY)] * 3,
        out_specs=[pl.BlockSpec(memory_space=pltpu.VMEM)] * len(sizes),
        scratch_shapes=[
            pltpu.VMEM((2 * NB, width), jnp.float32),
            pltpu.VMEM((pieces, block, samples), jnp.bfloat16),
            pltpu.VMEM((1, channels), jnp.int32),
            pltpu.VMEM((2 * NB, samples), jnp.bfloat16),
            pltpu.VMEM((pieces, 2 * NB, block), jnp.float32),
            pltpu.SemaphoreType.DMA((2 + pieces,)),
        ],
        out_shape=[jax.ShapeDtypeStruct((2 * size, channels), jnp.float32) for size in sizes],
        compiler_params=pltpu.CompilerParams(vmem_limit_bytes=32 * 2**20),
        cost_estimate=pl.CostEstimate(
            flops=4 * NB * samples * channels, bytes_accessed=2 * samples * channels, transcendentals=0
        ),
        name="whiten",
    )(offsets, *(
        pltpu.with_memory_space_constraint(x, pltpu.HBM)
        for x in (padded_table(width), records, live.reshape(1, channels))
    ))


def split(values):
    high = values.astype(jnp.bfloat16).astype(jnp.float32)
    return high, values - high


def cross_kernel(size, first, turn_ref, own_low, own_high, mirror_low, mirror_high, *refs):
    out_hbm, held, left, right, picked, done, sems = refs[-7:]
    step = pl.program_id(0)
    half = own_low.shape[0]
    windows = 2 * half
    rows = 2 * GROUP
    terms = windows * rows
    depth, channels = right.shape[1:]
    width = left.shape[1]
    tile = min(256, channels)
    pieces = [(q, t) for q in range(2) for t in range(channels // tile)]
    slot, inner = step % 2, step % GROUP

    def gather(low, high, turn):
        at = pl.multiple_of(step * 2, rows)
        for w in range(windows):
            part = (low if w < half else high)[w % half, pl.ds(at, rows), :]
            held[pl.ds(pl.multiple_of((w ^ turn) * rows, 8), rows), :] = part
        return held[...]

    def copy(f, slot, q, t):
        piece = pl.ds(t * tile, tile)
        return pltpu.make_async_copy(
            done.at[slot, q, piece], out_hbm.at[first + f, q, piece], sems.at[slot, q * (channels // tile) + t]
        )

    @pl.when(step == 0)
    def _():
        picked[...] = jnp.zeros_like(picked)
        right[...] = jnp.zeros_like(right)

    @pl.when(inner == 0)
    def _():
        high, low = split(gather(own_low, own_high, 0) * (1.0 / windows))
        blank = [jnp.zeros((width - 3 * terms, channels), jnp.float32)] if width > 3 * terms else []
        left[...] = jnp.concatenate([high, high, low, *blank], axis=0).T.astype(jnp.bfloat16)
        values = gather(mirror_low, mirror_high, turn_ref[0])
        part = lax.broadcasted_iota(jnp.int32, values.shape, 0) % 2
        turned = jnp.where(part == 0, -pltpu.roll(values, terms - 1, 0), pltpu.roll(values, 1, 0))
        for q, block in enumerate((values, turned)):
            high, low = split(block)
            right[q, : 3 * terms] = jnp.concatenate([high, low, high], axis=0).astype(jnp.bfloat16)

    @pl.when(step >= 2)
    def _():
        for q, t in pieces:
            copy(step - 2, slot, q, t).wait()

    lane = lax.broadcasted_iota(jnp.int32, (1, width), 1)
    mask = jnp.where(lane % rows // 2 == inner, 1.0, 0.0).astype(jnp.bfloat16)
    picked[:, :width] = left[...] * mask

    def multiply(*accs):
        def stage(number):
            n, k = stages[number]
            for q in range(2):
                held_block = right[q, k * 256 : (k + 1) * 256, n * 256 : (n + 1) * 256]
                pltpu.matmul_push_rhs(held_block, number % 2, q)

        def retire(n, j, place):
            for q in range(2):
                done[slot, q, j * CHUNK : (j + 1) * CHUNK, n * 256 : (n + 1) * 256] = pltpu.matmul_pop(
                    accs[q * SLOTS + place]
                ).astype(jnp.bfloat16)

        chunks, deep = channels // CHUNK, depth // 256
        stages = [(n, k) for n in range(channels // 256) for k in range(deep)]
        waiting = []
        stage(0)
        for number, (n, k) in enumerate(stages):
            for j in range(chunks):
                place = (n * chunks + j) % SLOTS
                if k == 0 and len(waiting) > SLOTS // 2:
                    retire(*waiting.pop(0))
                for q in range(2):
                    pltpu.matmul_acc_lhs(
                        accs[q * SLOTS + place],
                        picked[j * CHUNK : (j + 1) * CHUNK, k * 256 : (k + 1) * 256],
                        load_staged_rhs=number % 2 if j == 0 else None,
                    )
                if j == 0 and number + 1 < len(stages):
                    stage(number + 1)
                if k == deep - 1:
                    waiting.append((n, j, place))
        for entry in waiting:
            retire(*entry)

    pl.run_scoped(
        multiply, *(pltpu.ACC(q)((CHUNK, 256), jnp.float32) for q in range(2) for _ in range(SLOTS))
    )
    for q, t in pieces:
        copy(step, slot, q, t).start()

    @pl.when(step == size - 1)
    def _():
        for f in (size - 2, size - 1):
            for q, t in pieces:
                copy(f, f % 2, q, t).wait()


def cross(turn, own, mirror, so_far, first, size, bins):
    windows = 2 * own[0].shape[0]
    channels = own[0].shape[2]
    terms = windows * 2 * GROUP
    width = -(-3 * terms // 128) * 128
    depth = -(-3 * terms // 256) * 256
    tiles = channels // min(256, channels)
    previous = [] if so_far is None else [so_far]
    return pl.pallas_call(
        functools.partial(cross_kernel, size, first),
        grid_spec=pltpu.PrefetchScalarGridSpec(
            num_scalar_prefetch=1,
            grid=(size,),
            in_specs=[pl.BlockSpec(x.shape, lambda f, s: (0, 0, 0)) for x in (*own, *mirror)]
            + [pl.BlockSpec(memory_space=pl.ANY)] * len(previous),
            out_specs=pl.BlockSpec(memory_space=pl.ANY),
            scratch_shapes=[
                pltpu.VMEM((terms, channels), jnp.float32),
                pltpu.VMEM((channels, width), jnp.bfloat16),
                pltpu.VMEM((2, depth, channels), jnp.bfloat16),
                pltpu.VMEM((channels, depth), jnp.bfloat16),
                pltpu.VMEM((2, 2, channels, channels), jnp.bfloat16),
                pltpu.SemaphoreType.DMA((2, 2 * tiles)),
            ],
        ),
        out_shape=jax.ShapeDtypeStruct((bins, 2, channels, channels), jnp.bfloat16),
        input_output_aliases={5: 0} if previous else {},
        compiler_params=pltpu.CompilerParams(vmem_limit_bytes=48 * 2**20),
        cost_estimate=pl.CostEstimate(
            flops=2 * size * 2 * channels * channels * 256,
            bytes_accessed=4 * size * channels * channels,
            transcendentals=0,
        ),
        name="cross",
    )(turn, *own, *mirror, *previous)


def exchange(block, axis, distance):
    n = lax.axis_size(axis)
    return lax.ppermute(block, axis, [(i, i ^ distance) for i in range(n)])


def double(block, axis):
    held, distance = block[None], 1
    while distance < lax.axis_size(axis) // 2:
        held = jnp.concatenate([held, exchange(held, axis, distance)])
        distance *= 2
    return held


def per_device(records, offsets, live_flags):
    row, col = lax.axis_index("row"), lax.axis_index("col")
    n = lax.axis_size("col")
    bins = NB // lax.axis_size("bin")
    sizes = (GROUP, bins - GROUP)
    turn = (row ^ col).reshape(1)
    swap = [(r * n + w, w * n + r) for r in range(n) for w in range(n)]
    parts = []
    for block in whiten(records, offsets, live_flags, sizes):
        other = lax.ppermute(block, ("row", "col"), swap)
        pairs = []
        for x, axis in ((block, "col"), (other, "row")):
            near = double(x, axis)
            pairs.append((near, exchange(near, axis, n // 2)))
        parts.append(pairs)
    out, first = None, 0
    for size, (own, mirror) in zip(sizes, parts):
        out = cross(turn, own, mirror, out, first, size, bins)
        first += size
    return out


def solution(mesh):
    in_specs = (P("row", "col"), P("col"), P("row"))
    out_specs = P("bin", None, "row", "col")
    return jax.shard_map(
        per_device, mesh=mesh, in_specs=in_specs, out_specs=out_specs, check_vma=False
    )
```

```python
import functools
import math

import jax
import jax.numpy as jnp
import numpy as np
from jax import lax
from jax.experimental import pallas as pl
from jax.experimental.pallas import tpu as pltpu
from jax.sharding import PartitionSpec as P

L = 1500
NB = 32
BSTEP = 6
EPSILON = 1e-05
PAD = 168
GROUP = 4
CHUNK = 128
BUFFERS = 4
SLOTS = 8


def padded_table(samples):
    k = (np.arange(NB) + 1) * BSTEP
    n = np.arange(L)
    angle = (k[:, None] * n[None, :] % L) * (2.0 * math.pi / L)
    taper = 0.5 - 0.5 * np.cos(n * (2.0 * math.pi / L))
    parts = np.stack([np.cos(angle) * taper, -np.sin(angle) * taper], axis=1)
    table = np.zeros((PAD + samples, 2 * NB), np.float32)
    table[PAD : PAD + L] = parts.reshape(2 * NB, L).T
    return jnp.asarray(table.astype(jnp.bfloat16).astype(np.float32))


def whiten_kernel(sizes, offset_ref, table_hbm, records_hbm, live_hbm, *refs):
    outs, (table, records, live, shifted, product, sems) = refs[:-6], refs[-6:]
    pieces, block, samples = records.shape
    copies = [
        pltpu.make_async_copy(table_hbm, table, sems.at[0]),
        pltpu.make_async_copy(live_hbm, live, sems.at[1]),
    ]
    for i in range(pieces):
        source = records_hbm.at[pl.ds(i * block, block)]
        copies.append(pltpu.make_async_copy(source, records.at[i], sems.at[2 + i]))
    for copy in copies:
        copy.start()
    copies[0].wait()
    shifted[...] = table[pl.ds(PAD - offset_ref[0], samples), :].astype(jnp.bfloat16)
    copies[1].wait()
    start = pl.multiple_of(lax.axis_index("bin") * (2 * sum(sizes)), 8)
    for i in range(pieces):
        copies[2 + i].wait()
        spectra = jnp.dot(records[i], shifted[...], preferred_element_type=jnp.float32).T
        product[i] = spectra
        energy = jnp.sum(spectra * spectra, axis=0, keepdims=True) / (2 * NB)
        columns = slice(i * block, (i + 1) * block)
        scaling = live[:, columns].astype(jnp.float32) / jnp.sqrt(energy + EPSILON)
        at = 0
        for size, out in zip(sizes, outs):
            rows = pl.ds(pl.multiple_of(start + at, 8), 2 * size)
            out[:, columns] = product[i, rows, :] * scaling
            at += 2 * size


def whiten(records, offsets, live, sizes):
    channels, samples = records.shape
    block = min(256, channels)
    pieces = channels // block
    rows = [2 * size for size in sizes]
    return pl.pallas_call(
        functools.partial(whiten_kernel, sizes),
        in_specs=[pl.BlockSpec(memory_space=pltpu.SMEM)] + [pl.BlockSpec(memory_space=pl.ANY)] * 3,
        out_specs=[pl.BlockSpec(memory_space=pltpu.VMEM)] * len(rows),
        scratch_shapes=[
            pltpu.VMEM((PAD + samples, 2 * NB), jnp.float32),
            pltpu.VMEM((pieces, block, samples), jnp.bfloat16),
            pltpu.VMEM((1, channels), jnp.int32),
            pltpu.VMEM((samples, 2 * NB), jnp.bfloat16),
            pltpu.VMEM((pieces, 2 * NB, block), jnp.float32),
            pltpu.SemaphoreType.DMA((2 + pieces,)),
        ],
        out_shape=[jax.ShapeDtypeStruct((count, channels), jnp.float32) for count in rows],
        compiler_params=pltpu.CompilerParams(vmem_limit_bytes=32 * 2**20),
        cost_estimate=pl.CostEstimate(
            flops=4 * NB * samples * channels, bytes_accessed=2 * samples * channels, transcendentals=0
        ),
        name="whiten",
    )(offsets, *(
        pltpu.with_memory_space_constraint(x, pltpu.HBM)
        for x in (padded_table(samples), records, live.reshape(1, channels))
    ))


def split(values):
    high = values.astype(jnp.bfloat16).astype(jnp.float32)
    return high, values - high


def cross_kernel(size, first, turn_ref, own_low, own_high, mirror_low, mirror_high, *refs):
    out_hbm, held, left, right, picked, done, sems = refs[-7:]
    step = pl.program_id(0)
    half = own_low.shape[0]
    windows = 2 * half
    rows = 2 * GROUP
    terms = windows * rows
    depth, channels = right.shape[1:]
    width = left.shape[1]
    height = done.shape[2]
    tile = min(256, height)
    pieces = [(q, t) for q in range(2) for t in range(height // tile)]
    slot, inner = step % BUFFERS, step // 2 % GROUP
    top = pl.multiple_of(step % 2 * height, height)

    def gather(low, high, turn):
        at = pl.multiple_of(step, rows)
        for w in range(windows):
            part = (low if w < half else high)[w % half, pl.ds(at, rows), :]
            held[pl.ds(pl.multiple_of((w ^ turn) * rows, 8), rows), :] = part
        return held[...]

    def copy(at_step, slot, q, t):
        target = pl.ds(pl.multiple_of(at_step % 2 * height + t * tile, tile), tile)
        return pltpu.make_async_copy(
            done.at[slot, q, pl.ds(t * tile, tile)],
            out_hbm.at[first + at_step // 2, q, target],
            sems.at[slot, q * (height // tile) + t],
        )

    @pl.when(step == 0)
    def _():
        picked[...] = jnp.zeros_like(picked)
        right[...] = jnp.zeros_like(right)

    @pl.when(step % (2 * GROUP) == 0)
    def _():
        high, low = split(gather(own_low, own_high, 0) * (1.0 / windows))
        blank = [jnp.zeros((width - 3 * terms, channels), jnp.float32)] if width > 3 * terms else []
        left[...] = jnp.concatenate([high, high, low, *blank], axis=0).T.astype(jnp.bfloat16)
        values = gather(mirror_low, mirror_high, turn_ref[0])
        part = lax.broadcasted_iota(jnp.int32, values.shape, 0) % 2
        turned = jnp.where(part == 0, -pltpu.roll(values, terms - 1, 0), pltpu.roll(values, 1, 0))
        for q, block in enumerate((values, turned)):
            high, low = split(block)
            right[q, : 3 * terms] = jnp.concatenate([high, low, high], axis=0).astype(jnp.bfloat16)

    @pl.when(step >= BUFFERS)
    def _():
        for q, t in pieces:
            copy(step - BUFFERS, slot, q, t).wait()

    lane = lax.broadcasted_iota(jnp.int32, (1, width), 1)
    mask = jnp.where(lane % rows // 2 == inner, 1.0, 0.0).astype(jnp.bfloat16)
    picked[:, :width] = left[pl.ds(top, height), :] * mask

    def multiply(*accs):
        def stage(number):
            n, k = stages[number]
            for q in range(2):
                held_block = right[q, k * 256 : (k + 1) * 256, n * 256 : (n + 1) * 256]
                pltpu.matmul_push_rhs(held_block, number % 2, q)

        def retire(n, j, place):
            for q in range(2):
                done[slot, q, j * CHUNK : (j + 1) * CHUNK, n * 256 : (n + 1) * 256] = pltpu.matmul_pop(
                    accs[q * SLOTS + place]
                ).astype(jnp.bfloat16)

        chunks, deep = height // CHUNK, depth // 256
        stages = [(n, k) for n in range(channels // 256) for k in range(deep)]
        waiting = []
        stage(0)
        for number, (n, k) in enumerate(stages):
            for j in range(chunks):
                place = (n * chunks + j) % SLOTS
                if k == 0 and len(waiting) > SLOTS // 2:
                    retire(*waiting.pop(0))
                for q in range(2):
                    pltpu.matmul_acc_lhs(
                        accs[q * SLOTS + place],
                        picked[j * CHUNK : (j + 1) * CHUNK, k * 256 : (k + 1) * 256],
                        load_staged_rhs=number % 2 if j == 0 else None,
                    )
                if j == 0 and number + 1 < len(stages):
                    stage(number + 1)
                if k == deep - 1:
                    waiting.append((n, j, place))
        for entry in waiting:
            retire(*entry)

    pl.run_scoped(
        multiply, *(pltpu.ACC(q)((CHUNK, 256), jnp.float32) for q in range(2) for _ in range(SLOTS))
    )
    for q, t in pieces:
        copy(step, slot, q, t).start(priority=t % 2)

    @pl.when(step == 2 * size - 1)
    def _():
        for last in range(2 * size - BUFFERS, 2 * size):
            for q, t in pieces:
                copy(last, last % BUFFERS, q, t).wait()


def cross(turn, own, mirror, so_far, first, size, bins):
    windows = 2 * own[0].shape[0]
    channels = own[0].shape[2]
    terms = windows * 2 * GROUP
    width = -(-3 * terms // 128) * 128
    depth = -(-3 * terms // 256) * 256
    height = channels // 2
    previous = [] if so_far is None else [so_far]
    return pl.pallas_call(
        functools.partial(cross_kernel, size, first),
        grid_spec=pltpu.PrefetchScalarGridSpec(
            num_scalar_prefetch=1,
            grid=(2 * size,),
            in_specs=[pl.BlockSpec(x.shape, lambda f, s: (0, 0, 0)) for x in (*own, *mirror)]
            + [pl.BlockSpec(memory_space=pl.ANY)] * len(previous),
            out_specs=pl.BlockSpec(memory_space=pl.ANY),
            scratch_shapes=[
                pltpu.VMEM((terms, channels), jnp.float32),
                pltpu.VMEM((channels, width), jnp.bfloat16),
                pltpu.VMEM((2, depth, channels), jnp.bfloat16),
                pltpu.VMEM((height, depth), jnp.bfloat16),
                pltpu.VMEM((BUFFERS, 2, height, channels), jnp.bfloat16),
                pltpu.SemaphoreType.DMA((BUFFERS, 2 * (height // min(256, height)))),
            ],
        ),
        out_shape=jax.ShapeDtypeStruct((bins, 2, channels, channels), jnp.bfloat16),
        input_output_aliases={5: 0} if previous else {},
        compiler_params=pltpu.CompilerParams(vmem_limit_bytes=48 * 2**20),
        cost_estimate=pl.CostEstimate(
            flops=2 * size * 2 * channels * channels * 256,
            bytes_accessed=4 * size * channels * channels,
            transcendentals=0,
        ),
        name="cross",
    )(turn, *own, *mirror, *previous)


def exchange(block, axis, distance):
    n = lax.axis_size(axis)
    return lax.ppermute(block, axis, [(i, i ^ distance) for i in range(n)])


def double(held, axis):
    distance = 1
    while distance < lax.axis_size(axis) // 2:
        held = jnp.concatenate([held, exchange(held, axis, distance)])
        distance *= 2
    return held


def per_device(records, offsets, live_flags):
    row, col = lax.axis_index("row"), lax.axis_index("col")
    n = lax.axis_size("col")
    bins = NB // lax.axis_size("bin")
    sizes = (GROUP, bins - GROUP)
    turn = (row ^ col).reshape(1)
    swap = [(r * n + w, w * n + r) for r in range(n) for w in range(n) if r != w]
    parts = []
    for block in whiten(records, offsets, live_flags, sizes):
        other = jnp.where(row == col, block, lax.ppermute(block, ("row", "col"), swap))
        pairs = []
        for x, axis in ((block, "col"), (other, "row")):
            near = double(x[None], axis)
            pairs.append((near, exchange(near, axis, n // 2)))
        parts.append(pairs)
    out, first = None, 0
    for size, (own, mirror) in zip(sizes, parts):
        out = cross(turn, own, mirror, out, first, size, bins)
        first += size
    return out


def solution(mesh):
    in_specs = (P("row", "col"), P("col"), P("row"))
    out_specs = P("bin", None, "row", "col")
    return jax.shard_map(
        per_device, mesh=mesh, in_specs=in_specs, out_specs=out_specs, check_vma=False
    )
```

```python
import functools
import math

import jax
import jax.numpy as jnp
import numpy as np
from jax import lax
from jax.experimental import pallas as pl
from jax.experimental.pallas import tpu as pltpu
from jax.sharding import PartitionSpec as P

L = 1500
NB = 32
BSTEP = 6
EPSILON = 1e-05
PAD = 168
GROUP = 4
CHUNK = 128
BUFFERS = 4
SLOTS = 8


def padded_table(samples):
    k = (np.arange(NB) + 1) * BSTEP
    n = np.arange(L)
    angle = (k[:, None] * n[None, :] % L) * (2.0 * math.pi / L)
    taper = 0.5 - 0.5 * np.cos(n * (2.0 * math.pi / L))
    parts = np.stack([np.cos(angle) * taper, -np.sin(angle) * taper], axis=1)
    table = np.zeros((PAD + samples, 2 * NB), np.float32)
    table[PAD : PAD + L] = parts.reshape(2 * NB, L).T
    return jnp.asarray(table.astype(jnp.bfloat16).astype(np.float32))


def whiten_kernel(sizes, offset_ref, table_hbm, records_hbm, live_hbm, *refs):
    outs, (table, records, live, shifted, product, sems) = refs[:-6], refs[-6:]
    pieces, block, samples = records.shape
    copies = [
        pltpu.make_async_copy(table_hbm, table, sems.at[0]),
        pltpu.make_async_copy(live_hbm, live, sems.at[1]),
    ]
    for i in range(pieces):
        source = records_hbm.at[pl.ds(i * block, block)]
        copies.append(pltpu.make_async_copy(source, records.at[i], sems.at[2 + i]))
    for copy in copies:
        copy.start()
    copies[0].wait()
    shifted[...] = table[pl.ds(PAD - offset_ref[0], samples), :].astype(jnp.bfloat16)
    copies[1].wait()
    start = pl.multiple_of(lax.axis_index("bin") * (2 * sum(sizes)), 8)
    for i in range(pieces):
        copies[2 + i].wait()
        spectra = jnp.dot(records[i], shifted[...], preferred_element_type=jnp.float32).T
        product[i] = spectra
        energy = jnp.sum(spectra * spectra, axis=0, keepdims=True) / (2 * NB)
        columns = slice(i * block, (i + 1) * block)
        scaling = live[:, columns].astype(jnp.float32) / jnp.sqrt(energy + EPSILON)
        at = 0
        for size, out in zip(sizes, outs):
            rows = pl.ds(pl.multiple_of(start + at, 8), 2 * size)
            out[:, columns] = product[i, rows, :] * scaling
            at += 2 * size


def whiten(records, offsets, live, sizes):
    channels, samples = records.shape
    block = min(256, channels)
    pieces = channels // block
    rows = [2 * size for size in sizes]
    return pl.pallas_call(
        functools.partial(whiten_kernel, sizes),
        in_specs=[pl.BlockSpec(memory_space=pltpu.SMEM)] + [pl.BlockSpec(memory_space=pl.ANY)] * 3,
        out_specs=[pl.BlockSpec(memory_space=pltpu.VMEM)] * len(rows),
        scratch_shapes=[
            pltpu.VMEM((PAD + samples, 2 * NB), jnp.float32),
            pltpu.VMEM((pieces, block, samples), jnp.bfloat16),
            pltpu.VMEM((1, channels), jnp.int32),
            pltpu.VMEM((samples, 2 * NB), jnp.bfloat16),
            pltpu.VMEM((pieces, 2 * NB, block), jnp.float32),
            pltpu.SemaphoreType.DMA((2 + pieces,)),
        ],
        out_shape=[jax.ShapeDtypeStruct((count, channels), jnp.float32) for count in rows],
        compiler_params=pltpu.CompilerParams(vmem_limit_bytes=32 * 2**20),
        cost_estimate=pl.CostEstimate(
            flops=4 * NB * samples * channels, bytes_accessed=2 * samples * channels, transcendentals=0
        ),
        name="whiten",
    )(offsets, *(
        pltpu.with_memory_space_constraint(x, pltpu.HBM)
        for x in (padded_table(samples), records, live.reshape(1, channels))
    ))


def split(values):
    high = values.astype(jnp.bfloat16).astype(jnp.float32)
    return high, values - high


def cross_kernel(size, first, turn_ref, own_low, own_high, mirror_low, mirror_high, *refs):
    out_hbm, held, left, right, picked, done, sems = refs[-7:]
    step = pl.program_id(0)
    half = own_low.shape[0]
    windows = 2 * half
    rows = 2 * GROUP
    terms = windows * rows
    depth, channels = right.shape[1:]
    width = left.shape[1]
    height = done.shape[2]
    tile = min(256, height)
    pieces = [(q, t) for q in range(2) for t in range(height // tile)]
    slot, inner = step % BUFFERS, step // 2 % GROUP
    top = pl.multiple_of(step % 2 * height, height)

    def gather(low, high, turn):
        at = pl.multiple_of(step, rows)
        for w in range(windows):
            part = (low if w < half else high)[w % half, pl.ds(at, rows), :]
            held[pl.ds(pl.multiple_of((w ^ turn) * rows, 8), rows), :] = part
        return held[...]

    def copy(at_step, slot, q, t):
        target = pl.ds(pl.multiple_of(at_step % 2 * height + t * tile, tile), tile)
        return pltpu.make_async_copy(
            done.at[slot, q, pl.ds(t * tile, tile)],
            out_hbm.at[first + at_step // 2, q, target],
            sems.at[slot, q * (height // tile) + t],
        )

    @pl.when(step == 0)
    def _():
        picked[...] = jnp.zeros_like(picked)
        right[...] = jnp.zeros_like(right)

    @pl.when(step % (2 * GROUP) == 0)
    def _():
        high, low = split(gather(own_low, own_high, 0) * (1.0 / windows))
        blank = [jnp.zeros((width - 3 * terms, channels), jnp.float32)] if width > 3 * terms else []
        left[...] = jnp.concatenate([high, high, low, *blank], axis=0).T.astype(jnp.bfloat16)
        values = gather(mirror_low, mirror_high, turn_ref[0])
        part = lax.broadcasted_iota(jnp.int32, values.shape, 0) % 2
        turned = jnp.where(part == 0, -pltpu.roll(values, terms - 1, 0), pltpu.roll(values, 1, 0))
        for q, block in enumerate((values, turned)):
            high, low = split(block)
            right[q, : 3 * terms] = jnp.concatenate([high, low, high], axis=0).astype(jnp.bfloat16)

    @pl.when(step >= BUFFERS)
    def _():
        for q, t in pieces:
            copy(step - BUFFERS, slot, q, t).wait()

    lane = lax.broadcasted_iota(jnp.int32, (1, width), 1)
    mask = jnp.where(lane % rows // 2 == inner, 1.0, 0.0).astype(jnp.bfloat16)
    picked[:, :width] = left[pl.ds(top, height), :] * mask

    def multiply(*accs):
        def stage(number):
            n, k = stages[number]
            for q in range(2):
                held_block = right[q, k * 256 : (k + 1) * 256, n * 256 : (n + 1) * 256]
                pltpu.matmul_push_rhs(held_block, number % 2, q)

        def retire(n, j, place):
            for q in range(2):
                done[slot, q, j * CHUNK : (j + 1) * CHUNK, n * 256 : (n + 1) * 256] = pltpu.matmul_pop(
                    accs[q * SLOTS + place]
                ).astype(jnp.bfloat16)

        chunks, deep = height // CHUNK, depth // 256
        stages = [(n, k) for n in range(channels // 256) for k in range(deep)]
        waiting = []
        stage(0)
        for number, (n, k) in enumerate(stages):
            for j in range(chunks):
                place = (n * chunks + j) % SLOTS
                if k == 0 and len(waiting) > SLOTS // 2:
                    retire(*waiting.pop(0))
                for q in range(2):
                    pltpu.matmul_acc_lhs(
                        accs[q * SLOTS + place],
                        picked[j * CHUNK : (j + 1) * CHUNK, k * 256 : (k + 1) * 256],
                        load_staged_rhs=number % 2 if j == 0 else None,
                    )
                if j == 0 and number + 1 < len(stages):
                    stage(number + 1)
                if k == deep - 1:
                    waiting.append((n, j, place))
        for entry in waiting:
            retire(*entry)

    pl.run_scoped(
        multiply, *(pltpu.ACC(q)((CHUNK, 256), jnp.float32) for q in range(2) for _ in range(SLOTS))
    )
    for q, t in pieces:
        copy(step, slot, q, t).start(priority=t % 2)

    @pl.when(step == 2 * size - 1)
    def _():
        for last in range(2 * size - BUFFERS, 2 * size):
            for q, t in pieces:
                copy(last, last % BUFFERS, q, t).wait()


def cross(turn, own, mirror, so_far, first, size, bins):
    windows = 2 * own[0].shape[0]
    channels = own[0].shape[2]
    terms = windows * 2 * GROUP
    width = -(-3 * terms // 128) * 128
    depth = -(-3 * terms // 256) * 256
    height = channels // 2
    previous = [] if so_far is None else [so_far]
    return pl.pallas_call(
        functools.partial(cross_kernel, size, first),
        grid_spec=pltpu.PrefetchScalarGridSpec(
            num_scalar_prefetch=1,
            grid=(2 * size,),
            in_specs=[pl.BlockSpec(x.shape, lambda f, s: (0, 0, 0)) for x in (*own, *mirror)]
            + [pl.BlockSpec(memory_space=pl.ANY)] * len(previous),
            out_specs=pl.BlockSpec(memory_space=pl.ANY),
            scratch_shapes=[
                pltpu.VMEM((terms, channels), jnp.float32),
                pltpu.VMEM((channels, width), jnp.bfloat16),
                pltpu.VMEM((2, depth, channels), jnp.bfloat16),
                pltpu.VMEM((height, depth), jnp.bfloat16),
                pltpu.VMEM((BUFFERS, 2, height, channels), jnp.bfloat16),
                pltpu.SemaphoreType.DMA((BUFFERS, 2 * (height // min(256, height)))),
            ],
        ),
        out_shape=jax.ShapeDtypeStruct((bins, 2, channels, channels), jnp.bfloat16),
        input_output_aliases={5: 0} if previous else {},
        compiler_params=pltpu.CompilerParams(vmem_limit_bytes=48 * 2**20),
        cost_estimate=pl.CostEstimate(
            flops=2 * size * 2 * channels * channels * 256,
            bytes_accessed=4 * size * channels * channels,
            transcendentals=0,
        ),
        name="cross",
    )(turn, *own, *mirror, *previous)


def exchange(block, axis, distance):
    n = lax.axis_size(axis)
    return lax.ppermute(block, axis, [(i, i ^ distance) for i in range(n)])


def double(held, axis):
    distance = 1
    while distance < lax.axis_size(axis) // 2:
        held = jnp.concatenate([held, exchange(held, axis, distance)])
        distance *= 2
    return held


def per_device(records, offsets, live_flags):
    row, col = lax.axis_index("row"), lax.axis_index("col")
    n = lax.axis_size("col")
    bins = NB // lax.axis_size("bin")
    sizes = (GROUP, bins - GROUP)
    across = n // 2
    turn = (row ^ col ^ across).reshape(1)
    swap = [(r * n + w, (w ^ across) * n + r) for r in range(n) for w in range(n)]
    parts = []
    for block in whiten(records, offsets, live_flags, sizes):
        other = lax.ppermute(block, ("row", "col"), swap)
        pairs = []
        for x, axis in ((block, "col"), (other, "row")):
            near = double(x[None], axis)
            pairs.append((near, exchange(near, axis, n // 2)))
        parts.append(pairs)
    out, first = None, 0
    for size, (own, mirror) in zip(sizes, parts):
        out = cross(turn, own, mirror, out, first, size, bins)
        first += size
    return out


def solution(mesh):
    in_specs = (P("row", "col"), P("col"), P("row"))
    out_specs = P("bin", None, "row", "col")
    return jax.shard_map(
        per_device, mesh=mesh, in_specs=in_specs, out_specs=out_specs, check_vma=False
    )
```

```python
import functools
import math

import jax
import jax.numpy as jnp
import numpy as np
from jax import lax
from jax.experimental import pallas as pl
from jax.experimental.pallas import tpu as pltpu
from jax.sharding import PartitionSpec as P

L = 1500
NB = 32
BSTEP = 6
EPSILON = 1e-05
PAD = 168
GROUP = 4
SPLIT = 4
BUFFERS = 8
SLOTS = 8


def padded_table(samples):
    k = (np.arange(NB) + 1) * BSTEP
    n = np.arange(L)
    angle = (k[:, None] * n[None, :] % L) * (2.0 * math.pi / L)
    taper = 0.5 - 0.5 * np.cos(n * (2.0 * math.pi / L))
    parts = np.stack([np.cos(angle) * taper, -np.sin(angle) * taper], axis=1)
    table = np.zeros((PAD + samples, 2 * NB), np.float32)
    table[PAD : PAD + L] = parts.reshape(2 * NB, L).T
    return jnp.asarray(table.astype(jnp.bfloat16).astype(np.float32))


def whiten_kernel(sizes, offset_ref, table_hbm, records_hbm, live_hbm, *refs):
    outs, (table, records, live, shifted, product, sems) = refs[:-6], refs[-6:]
    pieces, block, samples = records.shape
    copies = [
        pltpu.make_async_copy(table_hbm, table, sems.at[0]),
        pltpu.make_async_copy(live_hbm, live, sems.at[1]),
    ]
    for i in range(pieces):
        source = records_hbm.at[pl.ds(i * block, block)]
        copies.append(pltpu.make_async_copy(source, records.at[i], sems.at[2 + i]))
    for copy in copies:
        copy.start()
    copies[0].wait()
    shifted[...] = table[pl.ds(PAD - offset_ref[0], samples), :].astype(jnp.bfloat16)
    copies[1].wait()
    start = pl.multiple_of(lax.axis_index("bin") * (2 * sum(sizes)), 8)
    for i in range(pieces):
        copies[2 + i].wait()
        spectra = jnp.dot(records[i], shifted[...], preferred_element_type=jnp.float32).T
        product[i] = spectra
        energy = jnp.sum(spectra * spectra, axis=0, keepdims=True) / (2 * NB)
        columns = slice(i * block, (i + 1) * block)
        scaling = live[:, columns].astype(jnp.float32) / jnp.sqrt(energy + EPSILON)
        at = 0
        for size, out in zip(sizes, outs):
            rows = pl.ds(pl.multiple_of(start + at, 8), 2 * size)
            out[:, columns] = product[i, rows, :] * scaling
            at += 2 * size


def whiten(records, offsets, live, sizes):
    channels, samples = records.shape
    block = min(256, channels)
    pieces = channels // block
    rows = [2 * size for size in sizes]
    return pl.pallas_call(
        functools.partial(whiten_kernel, sizes),
        in_specs=[pl.BlockSpec(memory_space=pltpu.SMEM)] + [pl.BlockSpec(memory_space=pl.ANY)] * 3,
        out_specs=[pl.BlockSpec(memory_space=pltpu.VMEM)] * len(rows),
        scratch_shapes=[
            pltpu.VMEM((PAD + samples, 2 * NB), jnp.float32),
            pltpu.VMEM((pieces, block, samples), jnp.bfloat16),
            pltpu.VMEM((1, channels), jnp.int32),
            pltpu.VMEM((samples, 2 * NB), jnp.bfloat16),
            pltpu.VMEM((pieces, 2 * NB, block), jnp.float32),
            pltpu.SemaphoreType.DMA((2 + pieces,)),
        ],
        out_shape=[jax.ShapeDtypeStruct((count, channels), jnp.float32) for count in rows],
        compiler_params=pltpu.CompilerParams(vmem_limit_bytes=32 * 2**20),
        cost_estimate=pl.CostEstimate(
            flops=4 * NB * samples * channels, bytes_accessed=2 * samples * channels, transcendentals=0
        ),
        name="whiten",
    )(offsets, *(
        pltpu.with_memory_space_constraint(x, pltpu.HBM)
        for x in (padded_table(samples), records, live.reshape(1, channels))
    ))


def split(values):
    high = values.astype(jnp.bfloat16).astype(jnp.float32)
    return high, values - high


def cross_kernel(size, first, turn_ref, own_low, own_high, mirror_low, mirror_high, *refs):
    out_hbm, held, left, right, picked, done, sems = refs[-7:]
    step = pl.program_id(0)
    half = own_low.shape[0]
    windows = 2 * half
    rows = 2 * GROUP
    terms = windows * rows
    depth, channels = right.shape[1:]
    width = left.shape[1]
    height = done.shape[2]
    tile = min(256, height)
    pieces = [(q, t) for q in range(2) for t in range(height // tile)]
    slot, inner = step % BUFFERS, step // SPLIT % GROUP
    top = pl.multiple_of(step % SPLIT * height, height)
    chunk = min(128, height)

    def gather(low, high, turn):
        at = pl.multiple_of(step // SPLIT * 2, rows)
        for w in range(windows):
            part = (low if w < half else high)[w % half, pl.ds(at, rows), :]
            held[pl.ds(pl.multiple_of((w ^ turn) * rows, 8), rows), :] = part
        return held[...]

    def copy(at_step, slot, q, t):
        target = pl.ds(pl.multiple_of(at_step % SPLIT * height + t * tile, tile), tile)
        return pltpu.make_async_copy(
            done.at[slot, q, pl.ds(t * tile, tile)],
            out_hbm.at[first + at_step // SPLIT, q, target],
            sems.at[slot, q * (height // tile) + t],
        )

    @pl.when(step == 0)
    def _():
        picked[...] = jnp.zeros_like(picked)
        right[...] = jnp.zeros_like(right)

    @pl.when(step % (SPLIT * GROUP) == 0)
    def _():
        high, low = split(gather(own_low, own_high, 0) * (1.0 / windows))
        blank = [jnp.zeros((width - 3 * terms, channels), jnp.float32)] if width > 3 * terms else []
        left[...] = jnp.concatenate([high, high, low, *blank], axis=0).T.astype(jnp.bfloat16)
        values = gather(mirror_low, mirror_high, turn_ref[0])
        part = lax.broadcasted_iota(jnp.int32, values.shape, 0) % 2
        turned = jnp.where(part == 0, -pltpu.roll(values, terms - 1, 0), pltpu.roll(values, 1, 0))
        for q, block in enumerate((values, turned)):
            high, low = split(block)
            right[q, : 3 * terms] = jnp.concatenate([high, low, high], axis=0).astype(jnp.bfloat16)

    @pl.when(step >= BUFFERS)
    def _():
        for q, t in pieces:
            copy(step - BUFFERS, slot, q, t).wait()

    lane = lax.broadcasted_iota(jnp.int32, (1, width), 1)
    mask = jnp.where(lane % rows // 2 == inner, 1.0, 0.0).astype(jnp.bfloat16)
    picked[:, :width] = left[pl.ds(top, height), :] * mask

    def multiply(*accs):
        def stage(number):
            n, k = stages[number]
            for q in range(2):
                held_block = right[q, k * 256 : (k + 1) * 256, n * 256 : (n + 1) * 256]
                pltpu.matmul_push_rhs(held_block, number % 2, q)

        def retire(n, j, place):
            for q in range(2):
                done[slot, q, j * chunk : (j + 1) * chunk, n * 256 : (n + 1) * 256] = pltpu.matmul_pop(
                    accs[q * SLOTS + place]
                ).astype(jnp.bfloat16)

        chunks, deep = height // chunk, depth // 256
        stages = [(n, k) for n in range(channels // 256) for k in range(deep)]
        waiting = []
        stage(0)
        for number, (n, k) in enumerate(stages):
            for j in range(chunks):
                place = (n * chunks + j) % SLOTS
                if k == 0 and len(waiting) > SLOTS // 2:
                    retire(*waiting.pop(0))
                for q in range(2):
                    pltpu.matmul_acc_lhs(
                        accs[q * SLOTS + place],
                        picked[j * chunk : (j + 1) * chunk, k * 256 : (k + 1) * 256],
                        load_staged_rhs=number % 2 if j == 0 else None,
                    )
                if j == 0 and number + 1 < len(stages):
                    stage(number + 1)
                if k == deep - 1:
                    waiting.append((n, j, place))
        for entry in waiting:
            retire(*entry)

    pl.run_scoped(
        multiply, *(pltpu.ACC(q)((chunk, 256), jnp.float32) for q in range(2) for _ in range(SLOTS))
    )
    for q, t in pieces:
        copy(step, slot, q, t).start(priority=q)

    @pl.when(step == SPLIT * size - 1)
    def _():
        for last in range(SPLIT * size - BUFFERS, SPLIT * size):
            for q, t in pieces:
                copy(last, last % BUFFERS, q, t).wait()


def cross(turn, own, mirror, so_far, first, size, bins):
    windows = 2 * own[0].shape[0]
    channels = own[0].shape[2]
    terms = windows * 2 * GROUP
    width = -(-3 * terms // 128) * 128
    depth = -(-3 * terms // 256) * 256
    height = channels // SPLIT
    previous = [] if so_far is None else [so_far]
    return pl.pallas_call(
        functools.partial(cross_kernel, size, first),
        grid_spec=pltpu.PrefetchScalarGridSpec(
            num_scalar_prefetch=1,
            grid=(SPLIT * size,),
            in_specs=[pl.BlockSpec(x.shape, lambda f, s: (0, 0, 0)) for x in (*own, *mirror)]
            + [pl.BlockSpec(memory_space=pl.ANY)] * len(previous),
            out_specs=pl.BlockSpec(memory_space=pl.ANY),
            scratch_shapes=[
                pltpu.VMEM((terms, channels), jnp.float32),
                pltpu.VMEM((channels, width), jnp.bfloat16),
                pltpu.VMEM((2, depth, channels), jnp.bfloat16),
                pltpu.VMEM((height, depth), jnp.bfloat16),
                pltpu.VMEM((BUFFERS, 2, height, channels), jnp.bfloat16),
                pltpu.SemaphoreType.DMA((BUFFERS, 2 * (height // min(256, height)))),
            ],
        ),
        out_shape=jax.ShapeDtypeStruct((bins, 2, channels, channels), jnp.bfloat16),
        input_output_aliases={5: 0} if previous else {},
        compiler_params=pltpu.CompilerParams(vmem_limit_bytes=48 * 2**20),
        cost_estimate=pl.CostEstimate(
            flops=2 * size * 2 * channels * channels * 256,
            bytes_accessed=4 * size * channels * channels,
            transcendentals=0,
        ),
        name="cross",
    )(turn, *own, *mirror, *previous)


def exchange(block, axis, distance):
    n = lax.axis_size(axis)
    return lax.ppermute(block, axis, [(i, i ^ distance) for i in range(n)])


def double(held, axis):
    distance = 1
    while distance < lax.axis_size(axis) // 2:
        held = jnp.concatenate([held, exchange(held, axis, distance)])
        distance *= 2
    return held


def per_device(records, offsets, live_flags):
    row, col = lax.axis_index("row"), lax.axis_index("col")
    n = lax.axis_size("col")
    bins = NB // lax.axis_size("bin")
    sizes = (GROUP, bins - GROUP)
    across = n // 2
    turn = (row ^ col ^ across).reshape(1)
    swap = [(r * n + w, (w ^ across) * n + r) for r in range(n) for w in range(n)]
    blocks = whiten(records, offsets, live_flags, sizes)
    others = [lax.ppermute(blocks[0], ("row", "col"), swap)]
    for block in blocks[1:]:
        block, others[-1] = lax.optimization_barrier((block, others[-1]))
        others.append(lax.ppermute(block, ("row", "col"), swap))
    own = [double(block[None], "col") for block in blocks]
    own_far = [exchange(near, "col", n // 2) for near in own]
    mirror = [double(other[None], "row") for other in others]
    mirror_far = [exchange(near, "row", n // 2) for near in mirror]
    parts = zip(zip(own, own_far), zip(mirror, mirror_far))
    out, first = None, 0
    for size, pairs in zip(sizes, parts):
        out = cross(turn, *pairs, out, first, size, bins)
        first += size
    return out


def solution(mesh):
    in_specs = (P("row", "col"), P("col"), P("row"))
    out_specs = P("bin", None, "row", "col")
    return jax.shard_map(
        per_device, mesh=mesh, in_specs=in_specs, out_specs=out_specs, check_vma=False
    )
```

```python
import functools
import math

import jax
import jax.numpy as jnp
import numpy as np
from jax import lax
from jax.experimental import pallas as pl
from jax.experimental.pallas import tpu as pltpu
from jax.sharding import PartitionSpec as P

L = 1500
NB = 32
BSTEP = 6
EPSILON = 1e-05
PAD = 168
GROUP = 4
SPLIT = 2
BUFFERS = 4
SLOTS = 8


def padded_table(samples):
    k = (np.arange(NB) + 1) * BSTEP
    n = np.arange(L)
    angle = (k[:, None] * n[None, :] % L) * (2.0 * math.pi / L)
    taper = 0.5 - 0.5 * np.cos(n * (2.0 * math.pi / L))
    parts = np.stack([np.cos(angle) * taper, -np.sin(angle) * taper], axis=1)
    table = np.zeros((PAD + samples, 2 * NB), np.float32)
    table[PAD : PAD + L] = parts.reshape(2 * NB, L).T
    return jnp.asarray(table.astype(jnp.bfloat16).astype(np.float32))


def whiten_kernel(sizes, offset_ref, table_hbm, records_hbm, live_hbm, *refs):
    outs, (table, records, live, shifted, product, sems) = refs[:-6], refs[-6:]
    pieces, block, samples = records.shape
    copies = [
        pltpu.make_async_copy(table_hbm, table, sems.at[0]),
        pltpu.make_async_copy(live_hbm, live, sems.at[1]),
    ]
    for i in range(pieces):
        source = records_hbm.at[pl.ds(i * block, block)]
        copies.append(pltpu.make_async_copy(source, records.at[i], sems.at[2 + i]))
    for copy in copies:
        copy.start()
    copies[0].wait()
    shifted[...] = table[pl.ds(PAD - offset_ref[0], samples), :].astype(jnp.bfloat16)
    copies[1].wait()
    start = pl.multiple_of(lax.axis_index("bin") * (2 * sum(sizes)), 8)
    for i in range(pieces):
        copies[2 + i].wait()
        spectra = jnp.dot(records[i], shifted[...], preferred_element_type=jnp.float32).T
        product[i] = spectra
        energy = jnp.sum(spectra * spectra, axis=0, keepdims=True) / (2 * NB)
        columns = slice(i * block, (i + 1) * block)
        scaling = live[:, columns].astype(jnp.float32) / jnp.sqrt(energy + EPSILON)
        at = 0
        for size, out in zip(sizes, outs):
            rows = pl.ds(pl.multiple_of(start + at, 8), 2 * size)
            out[:, columns] = product[i, rows, :] * scaling
            at += 2 * size


def whiten(records, offsets, live, sizes):
    channels, samples = records.shape
    block = min(256, channels)
    pieces = channels // block
    rows = [2 * size for size in sizes]
    return pl.pallas_call(
        functools.partial(whiten_kernel, sizes),
        in_specs=[pl.BlockSpec(memory_space=pltpu.SMEM)] + [pl.BlockSpec(memory_space=pl.ANY)] * 3,
        out_specs=[pl.BlockSpec(memory_space=pltpu.VMEM)] * len(rows),
        scratch_shapes=[
            pltpu.VMEM((PAD + samples, 2 * NB), jnp.float32),
            pltpu.VMEM((pieces, block, samples), jnp.bfloat16),
            pltpu.VMEM((1, channels), jnp.int32),
            pltpu.VMEM((samples, 2 * NB), jnp.bfloat16),
            pltpu.VMEM((pieces, 2 * NB, block), jnp.float32),
            pltpu.SemaphoreType.DMA((2 + pieces,)),
        ],
        out_shape=[jax.ShapeDtypeStruct((count, channels), jnp.float32) for count in rows],
        compiler_params=pltpu.CompilerParams(vmem_limit_bytes=32 * 2**20),
        cost_estimate=pl.CostEstimate(
            flops=4 * NB * samples * channels, bytes_accessed=2 * samples * channels, transcendentals=0
        ),
        name="whiten",
    )(offsets, *(
        pltpu.with_memory_space_constraint(x, pltpu.HBM)
        for x in (padded_table(samples), records, live.reshape(1, channels))
    ))


def split(values):
    high = values.astype(jnp.bfloat16).astype(jnp.float32)
    return high, values - high


def cross_kernel(size, first, turn_ref, own_low, own_high, mirror_low, mirror_high, *refs):
    out_hbm, held, left, right, picked, done, sems = refs[-7:]
    step = pl.program_id(0)
    half = own_low.shape[0]
    windows = 2 * half
    rows = 2 * GROUP
    terms = windows * rows
    depth, channels = right.shape[1:]
    width = left.shape[1]
    height = done.shape[2]
    tile = min(256, height)
    pieces = [(q, t) for q in range(2) for t in range(height // tile)]
    slot, inner = step % BUFFERS, step // SPLIT % GROUP
    top = pl.multiple_of(step % SPLIT * height, height)
    chunk = min(128, height)

    def gather(low, high, turn):
        at = pl.multiple_of(step // SPLIT * 2, rows)
        for w in range(windows):
            part = (low if w < half else high)[w % half, pl.ds(at, rows), :]
            held[pl.ds(pl.multiple_of((w ^ turn) * rows, 8), rows), :] = part
        return held[...]

    def copy(at_step, slot, q, t):
        target = pl.ds(pl.multiple_of(at_step % SPLIT * height + t * tile, tile), tile)
        return pltpu.make_async_copy(
            done.at[slot, q, pl.ds(t * tile, tile)],
            out_hbm.at[first + at_step // SPLIT, q, target],
            sems.at[slot, q * (height // tile) + t],
        )

    @pl.when(step == 0)
    def _():
        picked[...] = jnp.zeros_like(picked)
        right[...] = jnp.zeros_like(right)

    @pl.when(step % (SPLIT * GROUP) == 0)
    def _():
        high, low = split(gather(own_low, own_high, 0) * (1.0 / windows))
        blank = [jnp.zeros((width - 3 * terms, channels), jnp.float32)] if width > 3 * terms else []
        left[...] = jnp.concatenate([high, high, low, *blank], axis=0).T.astype(jnp.bfloat16)
        values = gather(mirror_low, mirror_high, turn_ref[0])
        part = lax.broadcasted_iota(jnp.int32, values.shape, 0) % 2
        turned = jnp.where(part == 0, -pltpu.roll(values, terms - 1, 0), pltpu.roll(values, 1, 0))
        for q, block in enumerate((values, turned)):
            high, low = split(block)
            right[q, : 3 * terms] = jnp.concatenate([high, low, high], axis=0).astype(jnp.bfloat16)

    @pl.when(step >= BUFFERS)
    def _():
        for q, t in pieces:
            copy(step - BUFFERS, slot, q, t).wait()

    lane = lax.broadcasted_iota(jnp.int32, (1, width), 1)
    mask = jnp.where(lane % rows // 2 == inner, 1.0, 0.0).astype(jnp.bfloat16)
    picked[:, :width] = left[pl.ds(top, height), :] * mask

    def multiply(*accs):
        def stage(number):
            n, k = stages[number]
            for q in range(2):
                held_block = right[q, k * 256 : (k + 1) * 256, n * 256 : (n + 1) * 256]
                pltpu.matmul_push_rhs(held_block, number % 2, q)

        def retire(n, j, place):
            for q in range(2):
                done[slot, q, j * chunk : (j + 1) * chunk, n * 256 : (n + 1) * 256] = pltpu.matmul_pop(
                    accs[q * SLOTS + place]
                ).astype(jnp.bfloat16)

        chunks, deep = height // chunk, depth // 256
        stages = [(n, k) for n in range(channels // 256) for k in range(deep)]
        waiting = []
        stage(0)
        for number, (n, k) in enumerate(stages):
            for j in range(chunks):
                place = (n * chunks + j) % SLOTS
                if k == 0 and len(waiting) > SLOTS // 2:
                    retire(*waiting.pop(0))
                for q in range(2):
                    pltpu.matmul_acc_lhs(
                        accs[q * SLOTS + place],
                        picked[j * chunk : (j + 1) * chunk, k * 256 : (k + 1) * 256],
                        load_staged_rhs=number % 2 if j == 0 else None,
                    )
                if j == 0 and number + 1 < len(stages):
                    stage(number + 1)
                if k == deep - 1:
                    waiting.append((n, j, place))
        for entry in waiting:
            retire(*entry)

    pl.run_scoped(
        multiply, *(pltpu.ACC(q)((chunk, 256), jnp.float32) for q in range(2) for _ in range(SLOTS))
    )
    for q, t in pieces:
        copy(step, slot, q, t).start(priority=q)

    @pl.when(step == SPLIT * size - 1)
    def _():
        for last in range(SPLIT * size - BUFFERS, SPLIT * size):
            for q, t in pieces:
                copy(last, last % BUFFERS, q, t).wait()


def cross(turn, own, mirror, so_far, first, size, bins):
    windows = 2 * own[0].shape[0]
    channels = own[0].shape[2]
    terms = windows * 2 * GROUP
    width = -(-3 * terms // 128) * 128
    depth = -(-3 * terms // 256) * 256
    height = channels // SPLIT
    previous = [] if so_far is None else [so_far]
    return pl.pallas_call(
        functools.partial(cross_kernel, size, first),
        grid_spec=pltpu.PrefetchScalarGridSpec(
            num_scalar_prefetch=1,
            grid=(SPLIT * size,),
            in_specs=[pl.BlockSpec(x.shape, lambda f, s: (0, 0, 0)) for x in (*own, *mirror)]
            + [pl.BlockSpec(memory_space=pl.ANY)] * len(previous),
            out_specs=pl.BlockSpec(memory_space=pl.ANY),
            scratch_shapes=[
                pltpu.VMEM((terms, channels), jnp.float32),
                pltpu.VMEM((channels, width), jnp.bfloat16),
                pltpu.VMEM((2, depth, channels), jnp.bfloat16),
                pltpu.VMEM((height, depth), jnp.bfloat16),
                pltpu.VMEM((BUFFERS, 2, height, channels), jnp.bfloat16),
                pltpu.SemaphoreType.DMA((BUFFERS, 2 * (height // min(256, height)))),
            ],
        ),
        out_shape=jax.ShapeDtypeStruct((bins, 2, channels, channels), jnp.bfloat16),
        input_output_aliases={5: 0} if previous else {},
        compiler_params=pltpu.CompilerParams(vmem_limit_bytes=48 * 2**20),
        cost_estimate=pl.CostEstimate(
            flops=2 * size * 2 * channels * channels * 256,
            bytes_accessed=4 * size * channels * channels,
            transcendentals=0,
        ),
        name="cross",
    )(turn, *own, *mirror, *previous)


def exchange(block, axis, distance):
    n = lax.axis_size(axis)
    return lax.ppermute(block, axis, [(i, i ^ distance) for i in range(n)])


def double(block, axis):
    held, distance = block[None], 1
    while distance < lax.axis_size(axis) // 2:
        held = jnp.concatenate([held, exchange(held, axis, distance)])
        distance *= 2
    return held


def per_device(records, offsets, live_flags):
    row, col = lax.axis_index("row"), lax.axis_index("col")
    n = lax.axis_size("col")
    bins = NB // lax.axis_size("bin")
    sizes = (GROUP, bins - GROUP)
    across = n // 2
    turn = (row ^ col ^ across).reshape(1)
    swap = [(r * n + w, (w ^ across) * n + r) for r in range(n) for w in range(n)]
    (whitened,) = whiten(records, offsets, live_flags, (bins,))
    other = lax.ppermute(whitened, ("row", "col"), swap)
    own, mirror = double(whitened, "col"), double(other, "row")
    parts, first = [], 0
    for size in sizes:
        rows = slice(2 * first, 2 * (first + size))
        halves = ((own[:, rows], "col"), (mirror[:, rows], "row"))
        parts.append([(near, exchange(near, axis, n // 2)) for near, axis in halves])
        first += size
    out, first = None, 0
    for size, pairs in zip(sizes, parts):
        out = cross(turn, *pairs, out, first, size, bins)
        first += size
    return out


def solution(mesh):
    in_specs = (P("row", "col"), P("col"), P("row"))
    out_specs = P("bin", None, "row", "col")
    return jax.shard_map(
        per_device, mesh=mesh, in_specs=in_specs, out_specs=out_specs, check_vma=False
    )
```

```python
import functools
import math

import jax
import jax.numpy as jnp
import numpy as np
from jax import lax
from jax.experimental import pallas as pl
from jax.experimental.pallas import tpu as pltpu
from jax.sharding import PartitionSpec as P

L = 1500
NB = 32
BSTEP = 6
EPSILON = 1e-05
PAD = 168
GROUP = 4
CHUNK = 128
BUFFERS = 4
SLOTS = 8


def padded_table(samples):
    k = (np.arange(NB) + 1) * BSTEP
    n = np.arange(L)
    angle = (k[:, None] * n[None, :] % L) * (2.0 * math.pi / L)
    taper = 0.5 - 0.5 * np.cos(n * (2.0 * math.pi / L))
    parts = np.stack([np.cos(angle) * taper, -np.sin(angle) * taper], axis=1)
    table = np.zeros((PAD + samples, 2 * NB), np.float32)
    table[PAD : PAD + L] = parts.reshape(2 * NB, L).T
    return jnp.asarray(table.astype(jnp.bfloat16).astype(np.float32))


def whiten_kernel(sizes, offset_ref, table_hbm, records_hbm, live_hbm, *refs):
    outs, (table, records, live, shifted, product, sems) = refs[:-6], refs[-6:]
    pieces, block, samples = records.shape
    copies = [
        pltpu.make_async_copy(table_hbm, table, sems.at[0]),
        pltpu.make_async_copy(live_hbm, live, sems.at[1]),
    ]
    for i in range(pieces):
        source = records_hbm.at[pl.ds(i * block, block)]
        copies.append(pltpu.make_async_copy(source, records.at[i], sems.at[2 + i]))
    for copy in copies:
        copy.start()
    copies[0].wait()
    shifted[...] = table[pl.ds(PAD - offset_ref[0], samples), :].astype(jnp.bfloat16)
    copies[1].wait()
    start = pl.multiple_of(lax.axis_index("bin") * (2 * sum(sizes)), 8)
    for i in range(pieces):
        copies[2 + i].wait()
        spectra = jnp.dot(records[i], shifted[...], preferred_element_type=jnp.float32).T
        product[i] = spectra
        energy = jnp.sum(spectra * spectra, axis=0, keepdims=True) / (2 * NB)
        columns = slice(i * block, (i + 1) * block)
        scaling = live[:, columns].astype(jnp.float32) / jnp.sqrt(energy + EPSILON)
        at = 0
        for size, out in zip(sizes, outs):
            rows = pl.ds(pl.multiple_of(start + at, 8), 2 * size)
            out[:, columns] = product[i, rows, :] * scaling
            at += 2 * size


def whiten(records, offsets, live, sizes):
    channels, samples = records.shape
    block = min(256, channels)
    pieces = channels // block
    rows = [2 * size for size in sizes]
    return pl.pallas_call(
        functools.partial(whiten_kernel, sizes),
        in_specs=[pl.BlockSpec(memory_space=pltpu.SMEM)] + [pl.BlockSpec(memory_space=pl.ANY)] * 3,
        out_specs=[pl.BlockSpec(memory_space=pltpu.VMEM)] * len(rows),
        scratch_shapes=[
            pltpu.VMEM((PAD + samples, 2 * NB), jnp.float32),
            pltpu.VMEM((pieces, block, samples), jnp.bfloat16),
            pltpu.VMEM((1, channels), jnp.int32),
            pltpu.VMEM((samples, 2 * NB), jnp.bfloat16),
            pltpu.VMEM((pieces, 2 * NB, block), jnp.float32),
            pltpu.SemaphoreType.DMA((2 + pieces,)),
        ],
        out_shape=[jax.ShapeDtypeStruct((count, channels), jnp.float32) for count in rows],
        compiler_params=pltpu.CompilerParams(vmem_limit_bytes=32 * 2**20),
        cost_estimate=pl.CostEstimate(
            flops=4 * NB * samples * channels, bytes_accessed=2 * samples * channels, transcendentals=0
        ),
        name="whiten",
    )(offsets, *(
        pltpu.with_memory_space_constraint(x, pltpu.HBM)
        for x in (padded_table(samples), records, live.reshape(1, channels))
    ))


def split(values):
    high = values.astype(jnp.bfloat16).astype(jnp.float32)
    return high, values - high


def cross_kernel(size, first, turn_ref, own_low, own_high, mirror_low, mirror_high, *refs):
    out_hbm, held, left, right, picked, done, sems = refs[-7:]
    half = own_low.shape[0]
    windows = 2 * half
    rows = 2 * GROUP
    terms = windows * rows
    depth, channels = right.shape[1:]
    width = left.shape[1]
    height = done.shape[2]
    tile = min(256, height)
    pieces = [(q, t) for q in range(2) for t in range(height // tile)]

    def gather(low, high, turn, at):
        for w in range(windows):
            part = (low if w < half else high)[w % half, pl.ds(at, rows), :]
            held[pl.ds(pl.multiple_of((w ^ turn) * rows, 8), rows), :] = part
        return held[...]

    def copy(at_step, slot, q, t):
        target = pl.ds(pl.multiple_of(at_step % 2 * height + t * tile, tile), tile)
        return pltpu.make_async_copy(
            done.at[slot, q, pl.ds(t * tile, tile)],
            out_hbm.at[first + at_step // 2, q, target],
            sems.at[slot, q * (height // tile) + t],
        )

    picked[:, width:] = jnp.zeros((height, depth - width), jnp.bfloat16)
    right[:, 3 * terms :] = jnp.zeros((2, depth - 3 * terms, channels), jnp.bfloat16)

    def prepare(at):
        high, low = split(gather(own_low, own_high, 0, at) * (1.0 / windows))
        blank = [jnp.zeros((width - 3 * terms, channels), jnp.float32)] if width > 3 * terms else []
        left[...] = jnp.concatenate([high, high, low, *blank], axis=0).T.astype(jnp.bfloat16)
        values = gather(mirror_low, mirror_high, turn_ref[0], at)
        part = lax.broadcasted_iota(jnp.int32, values.shape, 0) % 2
        turned = jnp.where(part == 0, -pltpu.roll(values, terms - 1, 0), pltpu.roll(values, 1, 0))
        for q, block in enumerate((values, turned)):
            high, low = split(block)
            right[q, : 3 * terms] = jnp.concatenate([high, low, high], axis=0).astype(jnp.bfloat16)

    def body(step, carry):
        slot, inner = step % BUFFERS, step // 2 % GROUP
        top = pl.multiple_of(step % 2 * height, height)

        @pl.when(step % (2 * GROUP) == 0)
        def _():
            prepare(pl.multiple_of(step, rows))

        @pl.when(step >= BUFFERS)
        def _():
            for q, t in pieces:
                copy(step - BUFFERS, slot, q, t).wait()

        lane = lax.broadcasted_iota(jnp.int32, (1, width), 1)
        mask = jnp.where(lane % rows // 2 == inner, 1.0, 0.0).astype(jnp.bfloat16)
        picked[:, :width] = left[pl.ds(top, height), :] * mask

        def multiply(*accs):
            def stage(number):
                n, k = stages[number]
                for q in range(2):
                    held_block = right[q, k * 256 : (k + 1) * 256, n * 256 : (n + 1) * 256]
                    pltpu.matmul_push_rhs(held_block, number % 2, q)

            def retire(n, j, place):
                for q in range(2):
                    done[slot, q, j * CHUNK : (j + 1) * CHUNK, n * 256 : (n + 1) * 256] = pltpu.matmul_pop(
                        accs[q * SLOTS + place]
                    ).astype(jnp.bfloat16)

            chunks, deep = height // CHUNK, depth // 256
            stages = [(n, k) for n in range(channels // 256) for k in range(deep)]
            waiting = []
            stage(0)
            for number, (n, k) in enumerate(stages):
                for j in range(chunks):
                    place = (n * chunks + j) % SLOTS
                    if k == 0 and len(waiting) > SLOTS // 2:
                        retire(*waiting.pop(0))
                    for q in range(2):
                        pltpu.matmul_acc_lhs(
                            accs[q * SLOTS + place],
                            picked[j * CHUNK : (j + 1) * CHUNK, k * 256 : (k + 1) * 256],
                            load_staged_rhs=number % 2 if j == 0 else None,
                        )
                    if j == 0 and number + 1 < len(stages):
                        stage(number + 1)
                    if k == deep - 1:
                        waiting.append((n, j, place))
            for entry in waiting:
                retire(*entry)

        pl.run_scoped(
            multiply, *(pltpu.ACC(q)((CHUNK, 256), jnp.float32) for q in range(2) for _ in range(SLOTS))
        )
        for q, t in pieces:
            copy(step, slot, q, t).start(priority=t % 2)
        return carry

    lax.fori_loop(0, 2 * size, body, 0)
    for last in range(2 * size - BUFFERS, 2 * size):
        for q, t in pieces:
            copy(last, last % BUFFERS, q, t).wait()


def cross(turn, own, mirror, so_far, first, size, bins):
    windows = 2 * own[0].shape[0]
    channels = own[0].shape[2]
    terms = windows * 2 * GROUP
    width = -(-3 * terms // 128) * 128
    depth = -(-3 * terms // 256) * 256
    height = channels // 2
    previous = [] if so_far is None else [so_far]
    return pl.pallas_call(
        functools.partial(cross_kernel, size, first),
        in_specs=[pl.BlockSpec(memory_space=pltpu.SMEM)]
        + [pl.BlockSpec(memory_space=pltpu.VMEM)] * 4
        + [pl.BlockSpec(memory_space=pl.ANY)] * len(previous),
        out_specs=pl.BlockSpec(memory_space=pl.ANY),
        scratch_shapes=[
            pltpu.VMEM((terms, channels), jnp.float32),
            pltpu.VMEM((channels, width), jnp.bfloat16),
            pltpu.VMEM((2, depth, channels), jnp.bfloat16),
            pltpu.VMEM((height, depth), jnp.bfloat16),
            pltpu.VMEM((BUFFERS, 2, height, channels), jnp.bfloat16),
            pltpu.SemaphoreType.DMA((BUFFERS, 2 * (height // min(256, height)))),
        ],
        out_shape=jax.ShapeDtypeStruct((bins, 2, channels, channels), jnp.bfloat16),
        input_output_aliases={5: 0} if previous else {},
        compiler_params=pltpu.CompilerParams(vmem_limit_bytes=48 * 2**20),
        cost_estimate=pl.CostEstimate(
            flops=2 * size * 2 * channels * channels * 256,
            bytes_accessed=4 * size * channels * channels,
            transcendentals=0,
        ),
        name="cross",
    )(turn, *own, *mirror, *previous)


def exchange(block, axis, distance):
    n = lax.axis_size(axis)
    return lax.ppermute(block, axis, [(i, i ^ distance) for i in range(n)])


def double(held, axis):
    distance = 1
    while distance < lax.axis_size(axis) // 2:
        held = jnp.concatenate([held, exchange(held, axis, distance)])
        distance *= 2
    return held


def per_device(records, offsets, live_flags):
    row, col = lax.axis_index("row"), lax.axis_index("col")
    n = lax.axis_size("col")
    bins = NB // lax.axis_size("bin")
    sizes = (GROUP, bins - GROUP)
    across = n // 2
    turn = (row ^ col ^ across).reshape(1)
    swap = [(r * n + w, (w ^ across) * n + r) for r in range(n) for w in range(n)]
    parts = []
    for block in whiten(records, offsets, live_flags, sizes):
        other = lax.ppermute(block, ("row", "col"), swap)
        pairs = []
        for x, axis in ((block, "col"), (other, "row")):
            near = double(x[None], axis)
            pairs.append((near, exchange(near, axis, n // 2)))
        parts.append(pairs)
    out, first = None, 0
    for size, (own, mirror) in zip(sizes, parts):
        out = cross(turn, own, mirror, out, first, size, bins)
        first += size
    return out


def solution(mesh):
    in_specs = (P("row", "col"), P("col"), P("row"))
    out_specs = P("bin", None, "row", "col")
    return jax.shard_map(
        per_device, mesh=mesh, in_specs=in_specs, out_specs=out_specs, check_vma=False
    )
```

```python
import functools
import math

import jax
import jax.numpy as jnp
import numpy as np
from jax import lax
from jax.experimental import pallas as pl
from jax.experimental.pallas import tpu as pltpu
from jax.sharding import PartitionSpec as P

L = 1500
NB = 32
BSTEP = 6
EPSILON = 1e-05
PAD = 168
GROUP = 4
CHUNK = 128
BUFFERS = 4
SLOTS = 8


def padded_table(samples):
    k = (np.arange(NB) + 1) * BSTEP
    n = np.arange(L)
    angle = (k[:, None] * n[None, :] % L) * (2.0 * math.pi / L)
    taper = 0.5 - 0.5 * np.cos(n * (2.0 * math.pi / L))
    parts = np.stack([np.cos(angle) * taper, -np.sin(angle) * taper], axis=1)
    table = np.zeros((PAD + samples, 2 * NB), np.float32)
    table[PAD : PAD + L] = parts.reshape(2 * NB, L).T
    return jnp.asarray(table.astype(jnp.bfloat16).astype(np.float32))


def whiten_kernel(sizes, offset_ref, table_hbm, records_hbm, live_hbm, *refs):
    outs, (table, records, live, shifted, product, sems) = refs[:-6], refs[-6:]
    pieces, block, samples = records.shape
    copies = [
        pltpu.make_async_copy(table_hbm, table, sems.at[0]),
        pltpu.make_async_copy(live_hbm, live, sems.at[1]),
    ]
    for i in range(pieces):
        source = records_hbm.at[pl.ds(i * block, block)]
        copies.append(pltpu.make_async_copy(source, records.at[i], sems.at[2 + i]))
    for copy in copies:
        copy.start()
    copies[0].wait()
    shifted[...] = table[pl.ds(PAD - offset_ref[0], samples), :].astype(jnp.bfloat16)
    copies[1].wait()
    start = pl.multiple_of(lax.axis_index("bin") * (2 * sum(sizes)), 8)
    for i in range(pieces):
        copies[2 + i].wait()
        spectra = jnp.dot(records[i], shifted[...], preferred_element_type=jnp.float32).T
        product[i] = spectra
        energy = jnp.sum(spectra * spectra, axis=0, keepdims=True) / (2 * NB)
        columns = slice(i * block, (i + 1) * block)
        scaling = live[:, columns].astype(jnp.float32) / jnp.sqrt(energy + EPSILON)
        at = 0
        for size, out in zip(sizes, outs):
            rows = pl.ds(pl.multiple_of(start + at, 8), 2 * size)
            out[:, columns] = product[i, rows, :] * scaling
            at += 2 * size


def whiten(records, offsets, live, sizes):
    channels, samples = records.shape
    block = min(256, channels)
    pieces = channels // block
    rows = [2 * size for size in sizes]
    return pl.pallas_call(
        functools.partial(whiten_kernel, sizes),
        in_specs=[pl.BlockSpec(memory_space=pltpu.SMEM)] + [pl.BlockSpec(memory_space=pl.ANY)] * 3,
        out_specs=[pl.BlockSpec(memory_space=pltpu.VMEM)] * len(rows),
        scratch_shapes=[
            pltpu.VMEM((PAD + samples, 2 * NB), jnp.float32),
            pltpu.VMEM((pieces, block, samples), jnp.bfloat16),
            pltpu.VMEM((1, channels), jnp.int32),
            pltpu.VMEM((samples, 2 * NB), jnp.bfloat16),
            pltpu.VMEM((pieces, 2 * NB, block), jnp.float32),
            pltpu.SemaphoreType.DMA((2 + pieces,)),
        ],
        out_shape=[jax.ShapeDtypeStruct((count, channels), jnp.float32) for count in rows],
        compiler_params=pltpu.CompilerParams(vmem_limit_bytes=32 * 2**20),
        cost_estimate=pl.CostEstimate(
            flops=4 * NB * samples * channels, bytes_accessed=2 * samples * channels, transcendentals=0
        ),
        name="whiten",
    )(offsets, *(
        pltpu.with_memory_space_constraint(x, pltpu.HBM)
        for x in (padded_table(samples), records, live.reshape(1, channels))
    ))


def split(values):
    high = values.astype(jnp.bfloat16).astype(jnp.float32)
    return high, values - high


def cross_kernel(size, first, turn_ref, own_low, own_high, mirror_low, mirror_high, *refs):
    out_hbm, held, left, right, picked, done, sems = refs[-7:]
    half = own_low.shape[0]
    windows = 2 * half
    rows = 2 * GROUP
    terms = windows * rows
    depth, channels = right.shape[1:]
    width = left.shape[1]
    height = done.shape[2]
    tile = min(256, height)
    pieces = [(q, t) for q in range(2) for t in range(height // tile)]

    def gather(low, high, turn, at):
        for w in range(windows):
            part = (low if w < half else high)[w % half, pl.ds(at, rows), :]
            held[pl.ds(pl.multiple_of((w ^ turn) * rows, 8), rows), :] = part
        return held[...]

    def copy(at_step, slot, q, t):
        target = pl.ds(pl.multiple_of(at_step % 2 * height + t * tile, tile), tile)
        return pltpu.make_async_copy(
            done.at[slot, q, pl.ds(t * tile, tile)],
            out_hbm.at[first + at_step // 2, q, target],
            sems.at[slot, q * (height // tile) + t],
        )

    picked[:, width:] = jnp.zeros((height, depth - width), jnp.bfloat16)
    right[:, 3 * terms :] = jnp.zeros((2, depth - 3 * terms, channels), jnp.bfloat16)

    def prepare(at):
        high, low = split(gather(own_low, own_high, 0, at) * (1.0 / windows))
        blank = [jnp.zeros((width - 3 * terms, channels), jnp.float32)] if width > 3 * terms else []
        left[...] = jnp.concatenate([high, high, low, *blank], axis=0).T.astype(jnp.bfloat16)
        values = gather(mirror_low, mirror_high, turn_ref[0], at)
        part = lax.broadcasted_iota(jnp.int32, values.shape, 0) % 2
        turned = jnp.where(part == 0, -pltpu.roll(values, terms - 1, 0), pltpu.roll(values, 1, 0))
        for q, block in enumerate((values, turned)):
            high, low = split(block)
            right[q, : 3 * terms] = jnp.concatenate([high, low, high], axis=0).astype(jnp.bfloat16)

    def body(step, carry):
        slot, inner = step % BUFFERS, step // 2 % GROUP
        top = pl.multiple_of(step % 2 * height, height)

        @pl.when(step % (2 * GROUP) == 0)
        def _():
            prepare(pl.multiple_of(step, rows))

        @pl.when(step >= BUFFERS)
        def _():
            for q, t in pieces:
                copy(step - BUFFERS, slot, q, t).wait()

        lane = lax.broadcasted_iota(jnp.int32, (1, width), 1)
        mask = jnp.where(lane % rows // 2 == inner, 1.0, 0.0).astype(jnp.bfloat16)
        picked[:, :width] = left[pl.ds(top, height), :] * mask

        def multiply(*accs):
            def stage(number):
                n, k = stages[number]
                for q in range(2):
                    held_block = right[q, k * 256 : (k + 1) * 256, n * 256 : (n + 1) * 256]
                    pltpu.matmul_push_rhs(held_block, number % 2, q)

            def retire(n, j, place):
                for q in range(2):
                    done[slot, q, j * CHUNK : (j + 1) * CHUNK, n * 256 : (n + 1) * 256] = pltpu.matmul_pop(
                        accs[q * SLOTS + place]
                    ).astype(jnp.bfloat16)

            chunks, deep = height // CHUNK, depth // 256
            stages = [(n, k) for n in range(channels // 256) for k in range(deep)]
            waiting = []
            stage(0)
            for number, (n, k) in enumerate(stages):
                for j in range(chunks):
                    place = (n * chunks + j) % SLOTS
                    if k == 0 and len(waiting) > SLOTS // 2:
                        retire(*waiting.pop(0))
                    for q in range(2):
                        pltpu.matmul_acc_lhs(
                            accs[q * SLOTS + place],
                            picked[j * CHUNK : (j + 1) * CHUNK, k * 256 : (k + 1) * 256],
                            load_staged_rhs=number % 2 if j == 0 else None,
                        )
                    if j == 0 and number + 1 < len(stages):
                        stage(number + 1)
                    if k == deep - 1:
                        waiting.append((n, j, place))
            for entry in waiting:
                retire(*entry)

        pl.run_scoped(
            multiply, *(pltpu.ACC(q)((CHUNK, 256), jnp.float32) for q in range(2) for _ in range(SLOTS))
        )
        for q, t in pieces:
            copy(step, slot, q, t).start(priority=t % 2)
        return carry

    lax.fori_loop(0, 2 * size, body, 0)
    for last in range(2 * size - BUFFERS, 2 * size):
        for q, t in pieces:
            copy(last, last % BUFFERS, q, t).wait()


def cross(turn, own, mirror, so_far, first, size, bins):
    windows = 2 * own[0].shape[0]
    channels = own[0].shape[2]
    terms = windows * 2 * GROUP
    width = -(-3 * terms // 128) * 128
    depth = -(-3 * terms // 256) * 256
    height = channels // 2
    previous = [] if so_far is None else [so_far]
    return pl.pallas_call(
        functools.partial(cross_kernel, size, first),
        in_specs=[pl.BlockSpec(memory_space=pltpu.SMEM)]
        + [pl.BlockSpec(memory_space=pltpu.VMEM)] * 4
        + [pl.BlockSpec(memory_space=pl.ANY)] * len(previous),
        out_specs=pl.BlockSpec(memory_space=pl.ANY),
        scratch_shapes=[
            pltpu.VMEM((terms, channels), jnp.float32),
            pltpu.VMEM((channels, width), jnp.bfloat16),
            pltpu.VMEM((2, depth, channels), jnp.bfloat16),
            pltpu.VMEM((height, depth), jnp.bfloat16),
            pltpu.VMEM((BUFFERS, 2, height, channels), jnp.bfloat16),
            pltpu.SemaphoreType.DMA((BUFFERS, 2 * (height // min(256, height)))),
        ],
        out_shape=jax.ShapeDtypeStruct((bins, 2, channels, channels), jnp.bfloat16),
        input_output_aliases={5: 0} if previous else {},
        compiler_params=pltpu.CompilerParams(vmem_limit_bytes=48 * 2**20),
        cost_estimate=pl.CostEstimate(
            flops=2 * size * 2 * channels * channels * 256,
            bytes_accessed=4 * size * channels * channels,
            transcendentals=0,
        ),
        name="cross",
    )(turn, *own, *mirror, *previous)


def exchange(block, axis, distance):
    n = lax.axis_size(axis)
    return lax.ppermute(block, axis, [(i, i ^ distance) for i in range(n)])


def double(held, axis):
    distance = 1
    while distance < lax.axis_size(axis) // 2:
        held = jnp.concatenate([held, exchange(held, axis, distance)])
        distance *= 2
    return held


def per_device(records, offsets, live_flags):
    row, col = lax.axis_index("row"), lax.axis_index("col")
    n = lax.axis_size("col")
    bins = NB // lax.axis_size("bin")
    sizes = (GROUP, bins - GROUP)
    across = [n // 4 if (c ^ c >> 1) & 1 else n // 2 for c in range(n)]
    turn = (row ^ col ^ jnp.where((col ^ col >> 1) & 1 == 1, n // 4, n // 2)).reshape(1)
    swap = [(r * n + w, (w ^ across[r]) * n + r) for r in range(n) for w in range(n)]
    parts = []
    for block in whiten(records, offsets, live_flags, sizes):
        other = lax.ppermute(block, ("row", "col"), swap)
        pairs = []
        for x, axis in ((block, "col"), (other, "row")):
            near = double(x[None], axis)
            pairs.append((near, exchange(near, axis, n // 2)))
        parts.append(pairs)
    out, first = None, 0
    for size, (own, mirror) in zip(sizes, parts):
        out = cross(turn, own, mirror, out, first, size, bins)
        first += size
    return out


def solution(mesh):
    in_specs = (P("row", "col"), P("col"), P("row"))
    out_specs = P("bin", None, "row", "col")
    return jax.shard_map(
        per_device, mesh=mesh, in_specs=in_specs, out_specs=out_specs, check_vma=False
    )
```

```python
import functools
import math

import jax
import jax.numpy as jnp
import numpy as np
from jax import lax
from jax.experimental import pallas as pl
from jax.experimental.pallas import tpu as pltpu
from jax.sharding import PartitionSpec as P

L = 1500
NB = 32
BSTEP = 6
EPSILON = 1e-05
PAD = 168
GROUP = 4
CHUNK = 128
BUFFERS = 4
SLOTS = 8


def padded_table(samples):
    k = (np.arange(NB) + 1) * BSTEP
    n = np.arange(L)
    angle = (k[:, None] * n[None, :] % L) * (2.0 * math.pi / L)
    taper = 0.5 - 0.5 * np.cos(n * (2.0 * math.pi / L))
    parts = np.stack([np.cos(angle) * taper, -np.sin(angle) * taper], axis=1)
    table = np.zeros((PAD + samples, 2 * NB), np.float32)
    table[PAD : PAD + L] = parts.reshape(2 * NB, L).T
    return jnp.asarray(table.astype(jnp.bfloat16).astype(np.float32))


def whiten_kernel(sizes, offset_ref, table_hbm, records_hbm, live_hbm, *refs):
    outs, (table, records, live, shifted, product, sems) = refs[:-6], refs[-6:]
    pieces, block, samples = records.shape
    copies = [
        pltpu.make_async_copy(table_hbm, table, sems.at[0]),
        pltpu.make_async_copy(live_hbm, live, sems.at[1]),
    ]
    for i in range(pieces):
        source = records_hbm.at[pl.ds(i * block, block)]
        copies.append(pltpu.make_async_copy(source, records.at[i], sems.at[2 + i]))
    for copy in copies:
        copy.start()
    copies[0].wait()
    shifted[...] = table[pl.ds(PAD - offset_ref[0], samples), :].astype(jnp.bfloat16)
    copies[1].wait()
    start = pl.multiple_of(lax.axis_index("bin") * (2 * sum(sizes)), 8)
    for i in range(pieces):
        copies[2 + i].wait()
        spectra = jnp.dot(records[i], shifted[...], preferred_element_type=jnp.float32).T
        product[i] = spectra
        energy = jnp.sum(spectra * spectra, axis=0, keepdims=True) / (2 * NB)
        columns = slice(i * block, (i + 1) * block)
        scaling = live[:, columns].astype(jnp.float32) / jnp.sqrt(energy + EPSILON)
        at = 0
        for size, out in zip(sizes, outs):
            rows = pl.ds(pl.multiple_of(start + at, 8), 2 * size)
            out[:, columns] = product[i, rows, :] * scaling
            at += 2 * size


def whiten(records, offsets, live, sizes):
    channels, samples = records.shape
    block = min(256, channels)
    pieces = channels // block
    rows = [2 * size for size in sizes]
    return pl.pallas_call(
        functools.partial(whiten_kernel, sizes),
        in_specs=[pl.BlockSpec(memory_space=pltpu.SMEM)] + [pl.BlockSpec(memory_space=pl.ANY)] * 3,
        out_specs=[pl.BlockSpec(memory_space=pltpu.VMEM)] * len(rows),
        scratch_shapes=[
            pltpu.VMEM((PAD + samples, 2 * NB), jnp.float32),
            pltpu.VMEM((pieces, block, samples), jnp.bfloat16),
            pltpu.VMEM((1, channels), jnp.int32),
            pltpu.VMEM((samples, 2 * NB), jnp.bfloat16),
            pltpu.VMEM((pieces, 2 * NB, block), jnp.float32),
            pltpu.SemaphoreType.DMA((2 + pieces,)),
        ],
        out_shape=[jax.ShapeDtypeStruct((count, channels), jnp.float32) for count in rows],
        compiler_params=pltpu.CompilerParams(vmem_limit_bytes=32 * 2**20),
        cost_estimate=pl.CostEstimate(
            flops=4 * NB * samples * channels, bytes_accessed=2 * samples * channels, transcendentals=0
        ),
        name="whiten",
    )(offsets, *(
        pltpu.with_memory_space_constraint(x, pltpu.HBM)
        for x in (padded_table(samples), records, live.reshape(1, channels))
    ))


def split(values):
    high = values.astype(jnp.bfloat16).astype(jnp.float32)
    return high, values - high


def cross_kernel(size, first, turn_ref, own_low, own_high, mirror_low, mirror_high, *refs):
    out_hbm, held, left, right, picked, done, sems = refs[-7:]
    half = own_low.shape[0]
    windows = 2 * half
    rows = 2 * GROUP
    terms = windows * rows
    depth, channels = right.shape[1:]
    width = left.shape[1]
    height = done.shape[2]
    tile = min(256, height)
    pieces = [(q, t) for q in range(2) for t in range(height // tile)]

    def gather(low, high, turn, at):
        for w in range(windows):
            part = (low if w < half else high)[w % half, pl.ds(at, rows), :]
            held[pl.ds(pl.multiple_of((w ^ turn) * rows, 8), rows), :] = part
        return held[...]

    def copy(at_step, slot, q, t):
        target = pl.ds(pl.multiple_of(at_step % 2 * height + t * tile, tile), tile)
        return pltpu.make_async_copy(
            done.at[slot, q, pl.ds(t * tile, tile)],
            out_hbm.at[first + at_step // 2, q, target],
            sems.at[slot, q * (height // tile) + t],
        )

    picked[:, width:] = jnp.zeros((height, depth - width), jnp.bfloat16)
    right[:, 3 * terms :] = jnp.zeros((2, depth - 3 * terms, channels), jnp.bfloat16)

    def prepare(at):
        high, low = split(gather(own_low, own_high, 0, at) * (1.0 / windows))
        blank = [jnp.zeros((width - 3 * terms, channels), jnp.float32)] if width > 3 * terms else []
        left[...] = jnp.concatenate([high, high, low, *blank], axis=0).T.astype(jnp.bfloat16)
        values = gather(mirror_low, mirror_high, turn_ref[0], at)
        part = lax.broadcasted_iota(jnp.int32, values.shape, 0) % 2
        turned = jnp.where(part == 0, -pltpu.roll(values, terms - 1, 0), pltpu.roll(values, 1, 0))
        for q, block in enumerate((values, turned)):
            high, low = split(block)
            right[q, : 3 * terms] = jnp.concatenate([high, low, high], axis=0).astype(jnp.bfloat16)

    def body(step, carry):
        slot, inner = step % BUFFERS, step // 2 % GROUP
        top = pl.multiple_of(step % 2 * height, height)

        @pl.when(step % (2 * GROUP) == 0)
        def _():
            prepare(pl.multiple_of(step, rows))

        @pl.when(step >= BUFFERS)
        def _():
            for q, t in pieces:
                copy(step - BUFFERS, slot, q, t).wait()

        lane = lax.broadcasted_iota(jnp.int32, (1, width), 1)
        mask = jnp.where(lane % rows // 2 == inner, 1.0, 0.0).astype(jnp.bfloat16)
        picked[:, :width] = left[pl.ds(top, height), :] * mask

        def multiply(*accs):
            def stage(number):
                n, k = stages[number]
                for q in range(2):
                    held_block = right[q, k * 256 : (k + 1) * 256, n * 256 : (n + 1) * 256]
                    pltpu.matmul_push_rhs(held_block, number % 2, q)

            def retire(n, j, place):
                for q in range(2):
                    done[slot, q, j * CHUNK : (j + 1) * CHUNK, n * 256 : (n + 1) * 256] = pltpu.matmul_pop(
                        accs[q * SLOTS + place]
                    ).astype(jnp.bfloat16)

            chunks, deep = height // CHUNK, depth // 256
            stages = [(n, k) for n in range(channels // 256) for k in range(deep)]
            waiting = []
            stage(0)
            for number, (n, k) in enumerate(stages):
                for j in range(chunks):
                    place = (n * chunks + j) % SLOTS
                    if k == 0 and len(waiting) > SLOTS // 2:
                        retire(*waiting.pop(0))
                    for q in range(2):
                        pltpu.matmul_acc_lhs(
                            accs[q * SLOTS + place],
                            picked[j * CHUNK : (j + 1) * CHUNK, k * 256 : (k + 1) * 256],
                            load_staged_rhs=number % 2 if j == 0 else None,
                        )
                    if j == 0 and number + 1 < len(stages):
                        stage(number + 1)
                    if k == deep - 1:
                        waiting.append((n, j, place))
            for entry in waiting:
                retire(*entry)

        pl.run_scoped(
            multiply, *(pltpu.ACC(q)((CHUNK, 256), jnp.float32) for q in range(2) for _ in range(SLOTS))
        )
        for q, t in pieces:
            copy(step, slot, q, t).start(priority=t % 2)
        return carry

    lax.fori_loop(0, 2 * size, body, 0)
    for last in range(2 * size - BUFFERS, 2 * size):
        for q, t in pieces:
            copy(last, last % BUFFERS, q, t).wait()


def cross(turn, own, mirror, so_far, first, size, bins):
    windows = 2 * own[0].shape[0]
    channels = own[0].shape[2]
    terms = windows * 2 * GROUP
    width = -(-3 * terms // 128) * 128
    depth = -(-3 * terms // 256) * 256
    height = channels // 2
    previous = [] if so_far is None else [so_far]
    return pl.pallas_call(
        functools.partial(cross_kernel, size, first),
        in_specs=[pl.BlockSpec(memory_space=pltpu.SMEM)]
        + [pl.BlockSpec(memory_space=pltpu.VMEM)] * 4
        + [pl.BlockSpec(memory_space=pl.ANY)] * len(previous),
        out_specs=pl.BlockSpec(memory_space=pl.ANY),
        scratch_shapes=[
            pltpu.VMEM((terms, channels), jnp.float32),
            pltpu.VMEM((channels, width), jnp.bfloat16),
            pltpu.VMEM((2, depth, channels), jnp.bfloat16),
            pltpu.VMEM((height, depth), jnp.bfloat16),
            pltpu.VMEM((BUFFERS, 2, height, channels), jnp.bfloat16),
            pltpu.SemaphoreType.DMA((BUFFERS, 2 * (height // min(256, height)))),
        ],
        out_shape=jax.ShapeDtypeStruct((bins, 2, channels, channels), jnp.bfloat16),
        input_output_aliases={5: 0} if previous else {},
        compiler_params=pltpu.CompilerParams(vmem_limit_bytes=48 * 2**20),
        cost_estimate=pl.CostEstimate(
            flops=2 * size * 2 * channels * channels * 256,
            bytes_accessed=4 * size * channels * channels,
            transcendentals=0,
        ),
        name="cross",
    )(turn, *own, *mirror, *previous)


def exchange(block, axis, distance):
    n = lax.axis_size(axis)
    return lax.ppermute(block, axis, [(i, i ^ distance) for i in range(n)])


def double(held, axis):
    distance = 1
    while distance < lax.axis_size(axis) // 2:
        held = jnp.concatenate([held, exchange(held, axis, distance)])
        distance *= 2
    return held


def per_device(records, offsets, live_flags):
    row, col = lax.axis_index("row"), lax.axis_index("col")
    n = lax.axis_size("col")
    bins = NB // lax.axis_size("bin")
    sizes = (GROUP, bins - GROUP)
    across = [n // 4 if (c ^ c >> 1) & 1 else n // 2 for c in range(n)]
    turn = (row ^ col ^ jnp.where((col ^ col >> 1) & 1 == 1, n // 4, n // 2)).reshape(1)
    swap = [(r * n + w, (w ^ across[r]) * n + r) for r in range(n) for w in range(n)]
    (whitened,) = whiten(records, offsets, live_flags, (bins,))
    other = lax.ppermute(whitened, ("row", "col"), swap)
    own, mirror = double(whitened[None], "col"), double(other[None], "row")
    parts, first = [], 0
    for size in sizes:
        rows = slice(2 * first, 2 * (first + size))
        near = own[:, rows]
        if parts:
            near, parts[-1] = lax.optimization_barrier((near, parts[-1]))
        right = mirror[:, rows]
        parts.append(([near, exchange(near, "col", n // 2)], [right, exchange(right, "row", n // 2)]))
        first += size
    out, first = None, 0
    for size, (own, mirror) in zip(sizes, parts):
        out = cross(turn, own, mirror, out, first, size, bins)
        first += size
    return out


def solution(mesh):
    in_specs = (P("row", "col"), P("col"), P("row"))
    out_specs = P("bin", None, "row", "col")
    return jax.shard_map(
        per_device, mesh=mesh, in_specs=in_specs, out_specs=out_specs, check_vma=False
    )
```

```python
import functools
import math

import jax
import jax.numpy as jnp
import numpy as np
from jax import lax
from jax.experimental import pallas as pl
from jax.experimental.pallas import tpu as pltpu
from jax.sharding import PartitionSpec as P

L = 1500
NB = 32
BSTEP = 6
EPSILON = 1e-05
PAD = 168
GROUP = 4
CHUNK = 128
BUFFERS = 4
SLOTS = 8


def padded_table(samples):
    k = (np.arange(NB) + 1) * BSTEP
    n = np.arange(L)
    angle = (k[:, None] * n[None, :] % L) * (2.0 * math.pi / L)
    taper = 0.5 - 0.5 * np.cos(n * (2.0 * math.pi / L))
    parts = np.stack([np.cos(angle) * taper, -np.sin(angle) * taper], axis=1)
    table = np.zeros((PAD + samples, 2 * NB), np.float32)
    table[PAD : PAD + L] = parts.reshape(2 * NB, L).T
    return jnp.asarray(table.astype(jnp.bfloat16).astype(np.float32))


def whiten_kernel(sizes, offset_ref, table_hbm, records_hbm, live_hbm, *refs):
    outs, (table, records, live, shifted, product, sems) = refs[:-6], refs[-6:]
    pieces, block, samples = records.shape
    copies = [
        pltpu.make_async_copy(table_hbm, table, sems.at[0]),
        pltpu.make_async_copy(live_hbm, live, sems.at[1]),
    ]
    for i in range(pieces):
        source = records_hbm.at[pl.ds(i * block, block)]
        copies.append(pltpu.make_async_copy(source, records.at[i], sems.at[2 + i]))
    for copy in copies:
        copy.start()
    copies[0].wait()
    shifted[...] = table[pl.ds(PAD - offset_ref[0], samples), :].astype(jnp.bfloat16)
    copies[1].wait()
    start = pl.multiple_of(lax.axis_index("bin") * (2 * sum(sizes)), 8)
    for i in range(pieces):
        copies[2 + i].wait()
        spectra = jnp.dot(records[i], shifted[...], preferred_element_type=jnp.float32).T
        product[i] = spectra
        energy = jnp.sum(spectra * spectra, axis=0, keepdims=True) / (2 * NB)
        columns = slice(i * block, (i + 1) * block)
        scaling = live[:, columns].astype(jnp.float32) / jnp.sqrt(energy + EPSILON)
        at = 0
        for size, out in zip(sizes, outs):
            rows = pl.ds(pl.multiple_of(start + at, 8), 2 * size)
            out[:, columns] = product[i, rows, :] * scaling
            at += 2 * size


def whiten(records, offsets, live, sizes):
    channels, samples = records.shape
    block = min(256, channels)
    pieces = channels // block
    rows = [2 * size for size in sizes]
    return pl.pallas_call(
        functools.partial(whiten_kernel, sizes),
        in_specs=[pl.BlockSpec(memory_space=pltpu.SMEM)] + [pl.BlockSpec(memory_space=pl.ANY)] * 3,
        out_specs=[pl.BlockSpec(memory_space=pltpu.VMEM)] * len(rows),
        scratch_shapes=[
            pltpu.VMEM((PAD + samples, 2 * NB), jnp.float32),
            pltpu.VMEM((pieces, block, samples), jnp.bfloat16),
            pltpu.VMEM((1, channels), jnp.int32),
            pltpu.VMEM((samples, 2 * NB), jnp.bfloat16),
            pltpu.VMEM((pieces, 2 * NB, block), jnp.float32),
            pltpu.SemaphoreType.DMA((2 + pieces,)),
        ],
        out_shape=[jax.ShapeDtypeStruct((count, channels), jnp.float32) for count in rows],
        compiler_params=pltpu.CompilerParams(vmem_limit_bytes=32 * 2**20),
        cost_estimate=pl.CostEstimate(
            flops=4 * NB * samples * channels, bytes_accessed=2 * samples * channels, transcendentals=0
        ),
        name="whiten",
    )(offsets, *(
        pltpu.with_memory_space_constraint(x, pltpu.HBM)
        for x in (padded_table(samples), records, live.reshape(1, channels))
    ))


def split(values):
    high = values.astype(jnp.bfloat16).astype(jnp.float32)
    return high, values - high


def cross_kernel(size, first, turn_ref, own_low, own_high, mirror_low, mirror_high, *refs):
    out_hbm, held, left, right, picked, done, sems = refs[-7:]
    half = own_low.shape[0]
    windows = 2 * half
    rows = 2 * GROUP
    terms = windows * rows
    depth, channels = right.shape[1:]
    width = left.shape[1]
    height = done.shape[2]
    tile = min(256, height)
    pieces = [(q, t) for q in range(2) for t in range(height // tile)]

    def gather(low, high, turn, at):
        for w in range(windows):
            part = (low if w < half else high)[w % half, pl.ds(at, rows), :]
            held[pl.ds(pl.multiple_of((w ^ turn) * rows, 8), rows), :] = part
        return held[...]

    def copy(at_step, slot, q, t):
        target = pl.ds(pl.multiple_of(at_step % 2 * height + t * tile, tile), tile)
        return pltpu.make_async_copy(
            done.at[slot, q, pl.ds(t * tile, tile)],
            out_hbm.at[first + at_step // 2, q, target],
            sems.at[slot, q * (height // tile) + t],
        )

    picked[:, width:] = jnp.zeros((height, depth - width), jnp.bfloat16)
    right[:, 3 * terms :] = jnp.zeros((2, depth - 3 * terms, channels), jnp.bfloat16)

    def prepare(at):
        high, low = split(gather(own_low, own_high, 0, at) * (1.0 / windows))
        blank = [jnp.zeros((width - 3 * terms, channels), jnp.float32)] if width > 3 * terms else []
        left[...] = jnp.concatenate([high, high, low, *blank], axis=0).T.astype(jnp.bfloat16)
        values = gather(mirror_low, mirror_high, turn_ref[0], at)
        part = lax.broadcasted_iota(jnp.int32, values.shape, 0) % 2
        turned = jnp.where(part == 0, -pltpu.roll(values, terms - 1, 0), pltpu.roll(values, 1, 0))
        for q, block in enumerate((values, turned)):
            high, low = split(block)
            right[q, : 3 * terms] = jnp.concatenate([high, low, high], axis=0).astype(jnp.bfloat16)

    def body(step, carry):
        slot, inner = step % BUFFERS, step // 2 % GROUP
        top = pl.multiple_of(step % 2 * height, height)

        @pl.when(step % (2 * GROUP) == 0)
        def _():
            prepare(pl.multiple_of(step, rows))

        @pl.when(step >= BUFFERS)
        def _():
            for q, t in pieces:
                copy(step - BUFFERS, slot, q, t).wait()

        lane = lax.broadcasted_iota(jnp.int32, (1, width), 1)
        mask = jnp.where(lane % rows // 2 == inner, 1.0, 0.0).astype(jnp.bfloat16)
        picked[:, :width] = left[pl.ds(top, height), :] * mask

        def multiply(*accs):
            def stage(number):
                n, k = stages[number]
                for q in range(2):
                    held_block = right[q, k * 256 : (k + 1) * 256, n * 256 : (n + 1) * 256]
                    pltpu.matmul_push_rhs(held_block, number % 2, q)

            def retire(n, j, place):
                for q in range(2):
                    done[slot, q, j * CHUNK : (j + 1) * CHUNK, n * 256 : (n + 1) * 256] = pltpu.matmul_pop(
                        accs[q * SLOTS + place]
                    ).astype(jnp.bfloat16)

            chunks, deep = height // CHUNK, depth // 256
            stages = [(n, k) for n in range(channels // 256) for k in range(deep)]
            waiting = []
            stage(0)
            for number, (n, k) in enumerate(stages):
                for j in range(chunks):
                    place = (n * chunks + j) % SLOTS
                    if k == 0 and len(waiting) > SLOTS // 2:
                        retire(*waiting.pop(0))
                    for q in range(2):
                        pltpu.matmul_acc_lhs(
                            accs[q * SLOTS + place],
                            picked[j * CHUNK : (j + 1) * CHUNK, k * 256 : (k + 1) * 256],
                            load_staged_rhs=number % 2 if j == 0 else None,
                        )
                    if j == 0 and number + 1 < len(stages):
                        stage(number + 1)
                    if k == deep - 1:
                        waiting.append((n, j, place))
            for entry in waiting:
                retire(*entry)

        pl.run_scoped(
            multiply, *(pltpu.ACC(q)((CHUNK, 256), jnp.float32) for q in range(2) for _ in range(SLOTS))
        )
        for q, t in pieces:
            copy(step, slot, q, t).start(priority=t % 2)
        return carry

    lax.fori_loop(0, 2 * size, body, 0)
    for last in range(2 * size - BUFFERS, 2 * size):
        for q, t in pieces:
            copy(last, last % BUFFERS, q, t).wait()


def cross(turn, own, mirror, so_far, first, size, bins):
    windows = 2 * own[0].shape[0]
    channels = own[0].shape[2]
    terms = windows * 2 * GROUP
    width = -(-3 * terms // 128) * 128
    depth = -(-3 * terms // 256) * 256
    height = channels // 2
    previous = [] if so_far is None else [so_far]
    return pl.pallas_call(
        functools.partial(cross_kernel, size, first),
        in_specs=[pl.BlockSpec(memory_space=pltpu.SMEM)]
        + [pl.BlockSpec(memory_space=pltpu.VMEM)] * 4
        + [pl.BlockSpec(memory_space=pl.ANY)] * len(previous),
        out_specs=pl.BlockSpec(memory_space=pl.ANY),
        scratch_shapes=[
            pltpu.VMEM((terms, channels), jnp.float32),
            pltpu.VMEM((channels, width), jnp.bfloat16),
            pltpu.VMEM((2, depth, channels), jnp.bfloat16),
            pltpu.VMEM((height, depth), jnp.bfloat16),
            pltpu.VMEM((BUFFERS, 2, height, channels), jnp.bfloat16),
            pltpu.SemaphoreType.DMA((BUFFERS, 2 * (height // min(256, height)))),
        ],
        out_shape=jax.ShapeDtypeStruct((bins, 2, channels, channels), jnp.bfloat16),
        input_output_aliases={5: 0} if previous else {},
        compiler_params=pltpu.CompilerParams(vmem_limit_bytes=48 * 2**20),
        cost_estimate=pl.CostEstimate(
            flops=2 * size * 2 * channels * channels * 256,
            bytes_accessed=4 * size * channels * channels,
            transcendentals=0,
        ),
        name="cross",
    )(turn, *own, *mirror, *previous)


def exchange(block, axis, distance):
    n = lax.axis_size(axis)
    return lax.ppermute(block, axis, [(i, i ^ distance) for i in range(n)])


def double(held, axis):
    distance = lax.axis_size(axis) // 2
    while distance > 1:
        held = jnp.concatenate([held, exchange(held, axis, distance)])
        distance //= 2
    return held


def per_device(records, offsets, live_flags):
    row, col = lax.axis_index("row"), lax.axis_index("col")
    n = lax.axis_size("col")
    bins = NB // lax.axis_size("bin")
    sizes = (GROUP, bins - GROUP)
    across = [n // 4 if (c ^ c >> 1) & 1 else n // 2 for c in range(n)]
    away = row ^ col ^ jnp.where((col ^ col >> 1) & 1 == 1, n // 4, n // 2)
    bits = n.bit_length() - 1
    turn = sum((away >> i & 1) << (bits - 1 - i) for i in range(bits)).reshape(1)
    swap = [(r * n + w, (w ^ across[r]) * n + r) for r in range(n) for w in range(n)]
    parts = []
    for block in whiten(records, offsets, live_flags, sizes):
        other = lax.ppermute(block, ("row", "col"), swap)
        pairs = []
        for x, axis in ((block, "col"), (other, "row")):
            near = double(x[None], axis)
            pairs.append((near, exchange(near, axis, 1)))
        parts.append(pairs)
    out, first = None, 0
    for size, (own, mirror) in zip(sizes, parts):
        out = cross(turn, own, mirror, out, first, size, bins)
        first += size
    return out


def solution(mesh):
    in_specs = (P("row", "col"), P("col"), P("row"))
    out_specs = P("bin", None, "row", "col")
    return jax.shard_map(
        per_device, mesh=mesh, in_specs=in_specs, out_specs=out_specs, check_vma=False
    )
```

```python
import functools
import math

import jax
import jax.numpy as jnp
import numpy as np
from jax import lax
from jax.experimental import pallas as pl
from jax.experimental.pallas import tpu as pltpu
from jax.sharding import PartitionSpec as P

L = 1500
NB = 32
BSTEP = 6
EPSILON = 1e-05
PAD = 168
GROUP = 4
CHUNK = 128
BUFFERS = 4
SLOTS = 8


def padded_table(samples):
    k = (np.arange(NB) + 1) * BSTEP
    n = np.arange(L)
    angle = (k[:, None] * n[None, :] % L) * (2.0 * math.pi / L)
    taper = 0.5 - 0.5 * np.cos(n * (2.0 * math.pi / L))
    parts = np.stack([np.cos(angle) * taper, -np.sin(angle) * taper], axis=1)
    table = np.zeros((PAD + samples, 2 * NB), np.float32)
    table[PAD : PAD + L] = parts.reshape(2 * NB, L).T
    return jnp.asarray(table.astype(jnp.bfloat16).astype(np.float32))


def whiten_kernel(sizes, offset_ref, table_hbm, records_hbm, live_hbm, *refs):
    outs, (table, records, live, shifted, product, sems) = refs[:-6], refs[-6:]
    pieces, block, samples = records.shape
    copies = [
        pltpu.make_async_copy(table_hbm, table, sems.at[0]),
        pltpu.make_async_copy(live_hbm, live, sems.at[1]),
    ]
    for i in range(pieces):
        source = records_hbm.at[pl.ds(i * block, block)]
        copies.append(pltpu.make_async_copy(source, records.at[i], sems.at[2 + i]))
    for copy in copies:
        copy.start()
    copies[0].wait()
    shifted[...] = table[pl.ds(PAD - offset_ref[0], samples), :].astype(jnp.bfloat16)
    copies[1].wait()
    start = pl.multiple_of(lax.axis_index("bin") * (2 * sum(sizes)), 8)
    for i in range(pieces):
        copies[2 + i].wait()
        spectra = jnp.dot(records[i], shifted[...], preferred_element_type=jnp.float32).T
        product[i] = spectra
        energy = jnp.sum(spectra * spectra, axis=0, keepdims=True) / (2 * NB)
        columns = slice(i * block, (i + 1) * block)
        scaling = live[:, columns].astype(jnp.float32) / jnp.sqrt(energy + EPSILON)
        at = 0
        for size, out in zip(sizes, outs):
            rows = pl.ds(pl.multiple_of(start + at, 8), 2 * size)
            out[:, columns] = product[i, rows, :] * scaling
            at += 2 * size


def whiten(records, offsets, live, sizes):
    channels, samples = records.shape
    block = min(256, channels)
    pieces = channels // block
    rows = [2 * size for size in sizes]
    return pl.pallas_call(
        functools.partial(whiten_kernel, sizes),
        in_specs=[pl.BlockSpec(memory_space=pltpu.SMEM)] + [pl.BlockSpec(memory_space=pl.ANY)] * 3,
        out_specs=[pl.BlockSpec(memory_space=pltpu.VMEM)] * len(rows),
        scratch_shapes=[
            pltpu.VMEM((PAD + samples, 2 * NB), jnp.float32),
            pltpu.VMEM((pieces, block, samples), jnp.bfloat16),
            pltpu.VMEM((1, channels), jnp.int32),
            pltpu.VMEM((samples, 2 * NB), jnp.bfloat16),
            pltpu.VMEM((pieces, 2 * NB, block), jnp.float32),
            pltpu.SemaphoreType.DMA((2 + pieces,)),
        ],
        out_shape=[jax.ShapeDtypeStruct((count, channels), jnp.float32) for count in rows],
        compiler_params=pltpu.CompilerParams(vmem_limit_bytes=32 * 2**20),
        cost_estimate=pl.CostEstimate(
            flops=4 * NB * samples * channels, bytes_accessed=2 * samples * channels, transcendentals=0
        ),
        name="whiten",
    )(offsets, *(
        pltpu.with_memory_space_constraint(x, pltpu.HBM)
        for x in (padded_table(samples), records, live.reshape(1, channels))
    ))


def split(values):
    high = values.astype(jnp.bfloat16).astype(jnp.float32)
    return high, values - high


def cross_kernel(size, first, orders, turn_ref, own_low, own_high, mirror_low, mirror_high, *refs):
    out_hbm, held, left, right, picked, done, sems = refs[-7:]
    half = own_low.shape[0]
    windows = 2 * half
    rows = 2 * GROUP
    terms = windows * rows
    depth, channels = right.shape[1:]
    width = left.shape[1]
    height = done.shape[2]
    tile = min(256, height)
    pieces = [(q, t) for q in range(2) for t in range(height // tile)]

    def gather(low, high, order, turn, at):
        for w, distance in enumerate(order):
            part = (low if w < half else high)[w % half, pl.ds(at, rows), :]
            held[pl.ds(pl.multiple_of((distance ^ turn) * rows, 8), rows), :] = part
        return held[...]

    def copy(at_step, slot, q, t):
        target = pl.ds(pl.multiple_of(at_step % 2 * height + t * tile, tile), tile)
        return pltpu.make_async_copy(
            done.at[slot, q, pl.ds(t * tile, tile)],
            out_hbm.at[first + at_step // 2, q, target],
            sems.at[slot, q * (height // tile) + t],
        )

    picked[:, width:] = jnp.zeros((height, depth - width), jnp.bfloat16)
    right[:, 3 * terms :] = jnp.zeros((2, depth - 3 * terms, channels), jnp.bfloat16)

    def prepare(at):
        high, low = split(gather(own_low, own_high, orders[0], 0, at) * (1.0 / windows))
        blank = [jnp.zeros((width - 3 * terms, channels), jnp.float32)] if width > 3 * terms else []
        left[...] = jnp.concatenate([high, high, low, *blank], axis=0).T.astype(jnp.bfloat16)
        values = gather(mirror_low, mirror_high, orders[1], turn_ref[0], at)
        part = lax.broadcasted_iota(jnp.int32, values.shape, 0) % 2
        turned = jnp.where(part == 0, -pltpu.roll(values, terms - 1, 0), pltpu.roll(values, 1, 0))
        for q, block in enumerate((values, turned)):
            high, low = split(block)
            right[q, : 3 * terms] = jnp.concatenate([high, low, high], axis=0).astype(jnp.bfloat16)

    def body(step, carry):
        slot, inner = step % BUFFERS, step // 2 % GROUP
        top = pl.multiple_of(step % 2 * height, height)

        @pl.when(step % (2 * GROUP) == 0)
        def _():
            prepare(pl.multiple_of(step, rows))

        @pl.when(step >= BUFFERS)
        def _():
            for q, t in pieces:
                copy(step - BUFFERS, slot, q, t).wait()

        lane = lax.broadcasted_iota(jnp.int32, (1, width), 1)
        mask = jnp.where(lane % rows // 2 == inner, 1.0, 0.0).astype(jnp.bfloat16)
        picked[:, :width] = left[pl.ds(top, height), :] * mask

        def multiply(*accs):
            def stage(number):
                n, k = stages[number]
                for q in range(2):
                    held_block = right[q, k * 256 : (k + 1) * 256, n * 256 : (n + 1) * 256]
                    pltpu.matmul_push_rhs(held_block, number % 2, q)

            def retire(n, j, place):
                for q in range(2):
                    done[slot, q, j * CHUNK : (j + 1) * CHUNK, n * 256 : (n + 1) * 256] = pltpu.matmul_pop(
                        accs[q * SLOTS + place]
                    ).astype(jnp.bfloat16)

            chunks, deep = height // CHUNK, depth // 256
            stages = [(n, k) for n in range(channels // 256) for k in range(deep)]
            waiting = []
            stage(0)
            for number, (n, k) in enumerate(stages):
                for j in range(chunks):
                    place = (n * chunks + j) % SLOTS
                    if k == 0 and len(waiting) > SLOTS // 2:
                        retire(*waiting.pop(0))
                    for q in range(2):
                        pltpu.matmul_acc_lhs(
                            accs[q * SLOTS + place],
                            picked[j * CHUNK : (j + 1) * CHUNK, k * 256 : (k + 1) * 256],
                            load_staged_rhs=number % 2 if j == 0 else None,
                        )
                    if j == 0 and number + 1 < len(stages):
                        stage(number + 1)
                    if k == deep - 1:
                        waiting.append((n, j, place))
            for entry in waiting:
                retire(*entry)

        pl.run_scoped(
            multiply, *(pltpu.ACC(q)((CHUNK, 256), jnp.float32) for q in range(2) for _ in range(SLOTS))
        )
        for q, t in pieces:
            copy(step, slot, q, t).start(priority=t % 2)
        return carry

    lax.fori_loop(0, 2 * size, body, 0)
    for last in range(2 * size - BUFFERS, 2 * size):
        for q, t in pieces:
            copy(last, last % BUFFERS, q, t).wait()


def cross(turn, own, mirror, so_far, first, size, bins):
    (own, own_order), (mirror, mirror_order) = own, mirror
    windows = 2 * own[0].shape[0]
    channels = own[0].shape[2]
    terms = windows * 2 * GROUP
    width = -(-3 * terms // 128) * 128
    depth = -(-3 * terms // 256) * 256
    height = channels // 2
    previous = [] if so_far is None else [so_far]
    return pl.pallas_call(
        functools.partial(cross_kernel, size, first, (own_order, mirror_order)),
        in_specs=[pl.BlockSpec(memory_space=pltpu.SMEM)]
        + [pl.BlockSpec(memory_space=pltpu.VMEM)] * 4
        + [pl.BlockSpec(memory_space=pl.ANY)] * len(previous),
        out_specs=pl.BlockSpec(memory_space=pl.ANY),
        scratch_shapes=[
            pltpu.VMEM((terms, channels), jnp.float32),
            pltpu.VMEM((channels, width), jnp.bfloat16),
            pltpu.VMEM((2, depth, channels), jnp.bfloat16),
            pltpu.VMEM((height, depth), jnp.bfloat16),
            pltpu.VMEM((BUFFERS, 2, height, channels), jnp.bfloat16),
            pltpu.SemaphoreType.DMA((BUFFERS, 2 * (height // min(256, height)))),
        ],
        out_shape=jax.ShapeDtypeStruct((bins, 2, channels, channels), jnp.bfloat16),
        input_output_aliases={5: 0} if previous else {},
        compiler_params=pltpu.CompilerParams(vmem_limit_bytes=48 * 2**20),
        cost_estimate=pl.CostEstimate(
            flops=2 * size * 2 * channels * channels * 256,
            bytes_accessed=4 * size * channels * channels,
            transcendentals=0,
        ),
        name="cross",
    )(turn, *own, *mirror, *previous)


def exchange(block, axis, distance):
    n = lax.axis_size(axis)
    return lax.ppermute(block, axis, [(i, i ^ distance) for i in range(n)])


def gathered(block, axis, distances):
    held, order = block[None], [0]
    for distance in distances[:-1]:
        held = jnp.concatenate([held, exchange(held, axis, distance)])
        order += [d ^ distance for d in order]
    order += [d ^ distances[-1] for d in order]
    return (held, exchange(held, axis, distances[-1])), tuple(order)


def per_device(records, offsets, live_flags):
    row, col = lax.axis_index("row"), lax.axis_index("col")
    n = lax.axis_size("col")
    bins = NB // lax.axis_size("bin")
    sizes = (GROUP, bins - GROUP)
    across = [n // 4 if (c ^ c >> 1) & 1 else n // 2 for c in range(n)]
    turn = (row ^ col ^ jnp.where((col ^ col >> 1) & 1 == 1, n // 4, n // 2)).reshape(1)
    swap = [(r * n + w, (w ^ across[r]) * n + r) for r in range(n) for w in range(n)]
    rising = [1 << i for i in range(n.bit_length() - 1)]
    parts = []
    for block in whiten(records, offsets, live_flags, sizes):
        other = lax.ppermute(block, ("row", "col"), swap)
        own = gathered(block, "col", rising if parts else rising[::-1])
        parts.append((own, gathered(other, "row", rising)))
    out, first = None, 0
    for size, (own, mirror) in zip(sizes, parts):
        out = cross(turn, own, mirror, out, first, size, bins)
        first += size
    return out


def solution(mesh):
    in_specs = (P("row", "col"), P("col"), P("row"))
    out_specs = P("bin", None, "row", "col")
    return jax.shard_map(
        per_device, mesh=mesh, in_specs=in_specs, out_specs=out_specs, check_vma=False
    )
```

```python
import functools
import math

import jax
import jax.numpy as jnp
import numpy as np
from jax import lax
from jax.experimental import pallas as pl
from jax.experimental.pallas import tpu as pltpu
from jax.sharding import PartitionSpec as P

L = 1500
NB = 32
BSTEP = 6
EPSILON = 1e-05
PAD = 168
GROUP = 4
CHUNK = 128
BUFFERS = 4
SLOTS = 8


def padded_table(samples):
    k = (np.arange(NB) + 1) * BSTEP
    n = np.arange(L)
    angle = (k[:, None] * n[None, :] % L) * (2.0 * math.pi / L)
    taper = 0.5 - 0.5 * np.cos(n * (2.0 * math.pi / L))
    parts = np.stack([np.cos(angle) * taper, -np.sin(angle) * taper], axis=1)
    table = np.zeros((PAD + samples, 2 * NB), np.float32)
    table[PAD : PAD + L] = parts.reshape(2 * NB, L).T
    table = np.concatenate([table[: PAD + samples // 2], table[samples // 2 :]], axis=1)
    return jnp.asarray(table.astype(jnp.bfloat16).astype(np.float32))


def whiten_kernel(sizes, offset_ref, table_hbm, records_hbm, live_hbm, *refs):
    outs, (table, records, live, shifted, product, sems) = refs[:-6], refs[-6:]
    pieces, block, samples = records.shape
    copies = [
        pltpu.make_async_copy(table_hbm, table, sems.at[0]),
        pltpu.make_async_copy(live_hbm, live, sems.at[1]),
    ]
    for i in range(pieces):
        source = records_hbm.at[pl.ds(i * block, block)]
        copies.append(pltpu.make_async_copy(source, records.at[i], sems.at[2 + i]))
    for copy in copies:
        copy.start()
    copies[0].wait()
    turned = table[pl.ds(PAD - offset_ref[0], samples // 2), :].astype(jnp.bfloat16)
    shifted[: samples // 2] = turned[:, : 2 * NB]
    shifted[samples // 2 :] = turned[:, 2 * NB :]
    copies[1].wait()
    start = pl.multiple_of(lax.axis_index("bin") * (2 * sum(sizes)), 8)
    for i in range(pieces):
        copies[2 + i].wait()
        spectra = jnp.dot(records[i], shifted[...], preferred_element_type=jnp.float32).T
        product[i] = spectra
        energy = jnp.sum(spectra * spectra, axis=0, keepdims=True) / (2 * NB)
        columns = slice(i * block, (i + 1) * block)
        scaling = live[:, columns].astype(jnp.float32) / jnp.sqrt(energy + EPSILON)
        at = 0
        for size, out in zip(sizes, outs):
            rows = pl.ds(pl.multiple_of(start + at, 8), 2 * size)
            out[:, columns] = product[i, rows, :] * scaling
            at += 2 * size


def whiten(records, offsets, live, sizes):
    channels, samples = records.shape
    block = min(256, channels)
    pieces = channels // block
    rows = [2 * size for size in sizes]
    return pl.pallas_call(
        functools.partial(whiten_kernel, sizes),
        in_specs=[pl.BlockSpec(memory_space=pltpu.SMEM)] + [pl.BlockSpec(memory_space=pl.ANY)] * 3,
        out_specs=[pl.BlockSpec(memory_space=pltpu.VMEM)] * len(rows),
        scratch_shapes=[
            pltpu.VMEM((PAD + samples // 2, 4 * NB), jnp.float32),
            pltpu.VMEM((pieces, block, samples), jnp.bfloat16),
            pltpu.VMEM((1, channels), jnp.int32),
            pltpu.VMEM((samples, 2 * NB), jnp.bfloat16),
            pltpu.VMEM((pieces, 2 * NB, block), jnp.float32),
            pltpu.SemaphoreType.DMA((2 + pieces,)),
        ],
        out_shape=[jax.ShapeDtypeStruct((count, channels), jnp.float32) for count in rows],
        compiler_params=pltpu.CompilerParams(vmem_limit_bytes=32 * 2**20),
        cost_estimate=pl.CostEstimate(
            flops=4 * NB * samples * channels, bytes_accessed=2 * samples * channels, transcendentals=0
        ),
        name="whiten",
    )(offsets, *(
        pltpu.with_memory_space_constraint(x, pltpu.HBM)
        for x in (padded_table(samples), records, live.reshape(1, channels))
    ))


def split(values):
    high = values.astype(jnp.bfloat16).astype(jnp.float32)
    return high, values - high


def cross_kernel(size, first, turn_ref, own_low, own_high, mirror_low, mirror_high, *refs):
    out_hbm, held, left, right, picked, done, sems = refs[-7:]
    half = own_low.shape[0]
    windows = 2 * half
    rows = 2 * GROUP
    terms = windows * rows
    depth, channels = right.shape[1:]
    width = left.shape[1]
    height = done.shape[2]
    tile = min(256, height)
    pieces = [(q, t) for q in range(2) for t in range(height // tile)]

    def gather(low, high, turn, at):
        for w in range(windows):
            part = (low if w < half else high)[w % half, pl.ds(at, rows), :]
            held[pl.ds(pl.multiple_of((w ^ turn) * rows, 8), rows), :] = part
        return held[...]

    def copy(at_step, slot, q, t):
        target = pl.ds(pl.multiple_of(at_step % 2 * height + t * tile, tile), tile)
        return pltpu.make_async_copy(
            done.at[slot, q, pl.ds(t * tile, tile)],
            out_hbm.at[first + at_step // 2, q, target],
            sems.at[slot, q * (height // tile) + t],
        )

    picked[:, width:] = jnp.zeros((height, depth - width), jnp.bfloat16)
    right[:, 3 * terms :] = jnp.zeros((2, depth - 3 * terms, channels), jnp.bfloat16)

    def prepare(at):
        high, low = split(gather(own_low, own_high, 0, at) * (1.0 / windows))
        blank = [jnp.zeros((width - 3 * terms, channels), jnp.float32)] if width > 3 * terms else []
        left[...] = jnp.concatenate([high, high, low, *blank], axis=0).T.astype(jnp.bfloat16)
        values = gather(mirror_low, mirror_high, turn_ref[0], at)
        part = lax.broadcasted_iota(jnp.int32, values.shape, 0) % 2
        turned = jnp.where(part == 0, -pltpu.roll(values, terms - 1, 0), pltpu.roll(values, 1, 0))
        for q, block in enumerate((values, turned)):
            high, low = split(block)
            right[q, : 3 * terms] = jnp.concatenate([high, low, high], axis=0).astype(jnp.bfloat16)

    def body(step, carry, cuts=1):
        slot, inner = step % BUFFERS, step // 2 % GROUP
        top = pl.multiple_of(step % 2 * height, height)

        @pl.when(step % (2 * GROUP) == 0)
        def _():
            prepare(pl.multiple_of(step, rows))

        @pl.when(step >= BUFFERS)
        def _():
            for q, t in pieces:
                copy(step - BUFFERS, slot, q, t).wait()

        lane = lax.broadcasted_iota(jnp.int32, (1, width), 1)
        mask = jnp.where(lane % rows // 2 == inner, 1.0, 0.0).astype(jnp.bfloat16)
        picked[:, :width] = left[pl.ds(top, height), :] * mask

        def multiply(cut, *accs):
            def stage(number):
                n, k = stages[number]
                for q in range(2):
                    held_block = right[q, k * 256 : (k + 1) * 256, n * 256 : (n + 1) * 256]
                    pltpu.matmul_push_rhs(held_block, number % 2, q)

            def retire(n, j, place):
                for q in range(2):
                    done[slot, q, j * CHUNK : (j + 1) * CHUNK, n * 256 : (n + 1) * 256] = pltpu.matmul_pop(
                        accs[q * SLOTS + place]
                    ).astype(jnp.bfloat16)

            chunks, deep = height // CHUNK // cuts, depth // 256
            stages = [(n, k) for n in range(channels // 256) for k in range(deep)]
            waiting = []
            stage(0)
            for number, (n, k) in enumerate(stages):
                for j in range(cut * chunks, (cut + 1) * chunks):
                    place = (n * chunks + j) % SLOTS
                    if k == 0 and len(waiting) > SLOTS // 2:
                        retire(*waiting.pop(0))
                    for q in range(2):
                        pltpu.matmul_acc_lhs(
                            accs[q * SLOTS + place],
                            picked[j * CHUNK : (j + 1) * CHUNK, k * 256 : (k + 1) * 256],
                            load_staged_rhs=number % 2 if j == cut * chunks else None,
                        )
                    if j == cut * chunks and number + 1 < len(stages):
                        stage(number + 1)
                    if k == deep - 1:
                        waiting.append((n, j, place))
            for entry in waiting:
                retire(*entry)

        accs = [pltpu.ACC(q)((CHUNK, 256), jnp.float32) for q in range(2) for _ in range(SLOTS)]
        share = len(pieces) // 2 // cuts
        for cut in range(cuts):
            pl.run_scoped(functools.partial(multiply, cut), *accs)
            for q, t in pieces:
                if t // share == cut:
                    copy(step, slot, q, t).start(priority=t % 2)
        return carry

    body(jnp.int32(0), 0, height // tile)
    lax.fori_loop(1, 2 * size, body, 0)
    for last in range(2 * size - BUFFERS, 2 * size):
        for q, t in pieces:
            copy(last, last % BUFFERS, q, t).wait()


def cross(turn, own, mirror, so_far, first, size, bins):
    windows = 2 * own[0].shape[0]
    channels = own[0].shape[2]
    terms = windows * 2 * GROUP
    width = -(-3 * terms // 128) * 128
    depth = -(-3 * terms // 256) * 256
    height = channels // 2
    previous = [] if so_far is None else [so_far]
    return pl.pallas_call(
        functools.partial(cross_kernel, size, first),
        in_specs=[pl.BlockSpec(memory_space=pltpu.SMEM)]
        + [pl.BlockSpec(memory_space=pltpu.VMEM)] * 4
        + [pl.BlockSpec(memory_space=pl.ANY)] * len(previous),
        out_specs=pl.BlockSpec(memory_space=pl.ANY),
        scratch_shapes=[
            pltpu.VMEM((terms, channels), jnp.float32),
            pltpu.VMEM((channels, width), jnp.bfloat16),
            pltpu.VMEM((2, depth, channels), jnp.bfloat16),
            pltpu.VMEM((height, depth), jnp.bfloat16),
            pltpu.VMEM((BUFFERS, 2, height, channels), jnp.bfloat16),
            pltpu.SemaphoreType.DMA((BUFFERS, 2 * (height // min(256, height)))),
        ],
        out_shape=jax.ShapeDtypeStruct((bins, 2, channels, channels), jnp.bfloat16),
        input_output_aliases={5: 0} if previous else {},
        compiler_params=pltpu.CompilerParams(vmem_limit_bytes=48 * 2**20),
        cost_estimate=pl.CostEstimate(
            flops=2 * size * 2 * channels * channels * 256,
            bytes_accessed=4 * size * channels * channels,
            transcendentals=0,
        ),
        name="cross",
    )(turn, *own, *mirror, *previous)


def exchange(block, axis, distance):
    n = lax.axis_size(axis)
    return lax.ppermute(block, axis, [(i, i ^ distance) for i in range(n)])


def double(held, axis):
    distance = 1
    while distance < lax.axis_size(axis) // 2:
        held = jnp.concatenate([held, exchange(held, axis, distance)])
        distance *= 2
    return held


def per_device(records, offsets, live_flags):
    row, col = lax.axis_index("row"), lax.axis_index("col")
    n = lax.axis_size("col")
    bins = NB // lax.axis_size("bin")
    sizes = (GROUP, bins - GROUP)
    across = [n // 4 if (c ^ c >> 1) & 1 else n // 2 for c in range(n)]
    turn = (row ^ col ^ jnp.where((col ^ col >> 1) & 1 == 1, n // 4, n // 2)).reshape(1)
    swap = [(r * n + w, (w ^ across[r]) * n + r) for r in range(n) for w in range(n)]
    parts = []
    for block in whiten(records, offsets, live_flags, sizes):
        other = lax.ppermute(block, ("row", "col"), swap)
        pairs = []
        for x, axis in ((block, "col"), (other, "row")):
            near = double(x[None], axis)
            pairs.append((near, exchange(near, axis, n // 2)))
        parts.append(pairs)
    out, first = None, 0
    for size, (own, mirror) in zip(sizes, parts):
        out = cross(turn, own, mirror, out, first, size, bins)
        first += size
    return out


def solution(mesh):
    in_specs = (P("row", "col"), P("col"), P("row"))
    out_specs = P("bin", None, "row", "col")
    return jax.shard_map(
        per_device, mesh=mesh, in_specs=in_specs, out_specs=out_specs, check_vma=False
    )
```

```python
import functools
import math

import jax
import jax.numpy as jnp
import numpy as np
from jax import lax
from jax.experimental import pallas as pl
from jax.experimental.pallas import tpu as pltpu
from jax.sharding import PartitionSpec as P

L = 1500
NB = 32
BSTEP = 6
EPSILON = 1e-05
PAD = 168
GROUP = 4
CHUNK = 128
BUFFERS = 4
SLOTS = 8


def padded_table(samples):
    k = (np.arange(NB) + 1) * BSTEP
    n = np.arange(L)
    angle = (k[:, None] * n[None, :] % L) * (2.0 * math.pi / L)
    taper = 0.5 - 0.5 * np.cos(n * (2.0 * math.pi / L))
    parts = np.stack([np.cos(angle) * taper, -np.sin(angle) * taper], axis=1)
    table = np.zeros((PAD + samples, 2 * NB), np.float32)
    table[PAD : PAD + L] = parts.reshape(2 * NB, L).T
    table = np.concatenate([table[: PAD + samples // 2], table[samples // 2 :]], axis=1)
    return jnp.asarray(table.astype(jnp.bfloat16).astype(np.float32))


def whiten_kernel(sizes, offset_ref, table_hbm, records_hbm, live_hbm, *refs):
    outs, (table, records, live, shifted, product, sems) = refs[:-6], refs[-6:]
    pieces, block, samples = records.shape
    copies = [
        pltpu.make_async_copy(table_hbm, table, sems.at[0]),
        pltpu.make_async_copy(live_hbm, live, sems.at[1]),
    ]
    for i in range(pieces):
        source = records_hbm.at[pl.ds(i * block, block)]
        copies.append(pltpu.make_async_copy(source, records.at[i], sems.at[2 + i]))
    for copy in copies:
        copy.start()
    copies[0].wait()
    turned = table[pl.ds(PAD - offset_ref[0], samples // 2), :].astype(jnp.bfloat16)
    shifted[: samples // 2] = turned[:, : 2 * NB]
    shifted[samples // 2 :] = turned[:, 2 * NB :]
    copies[1].wait()
    start = pl.multiple_of(lax.axis_index("bin") * (2 * sum(sizes)), 8)
    for i in range(pieces):
        copies[2 + i].wait()
        spectra = jnp.dot(records[i], shifted[...], preferred_element_type=jnp.float32).T
        product[i] = spectra
        energy = jnp.sum(spectra * spectra, axis=0, keepdims=True) / (2 * NB)
        columns = slice(i * block, (i + 1) * block)
        scaling = live[:, columns].astype(jnp.float32) / jnp.sqrt(energy + EPSILON)
        at = 0
        for size, out in zip(sizes, outs):
            rows = pl.ds(pl.multiple_of(start + at, 8), 2 * size)
            out[:, columns] = product[i, rows, :] * scaling
            at += 2 * size


def whiten(records, offsets, live, sizes):
    channels, samples = records.shape
    block = min(256, channels)
    pieces = channels // block
    rows = [2 * size for size in sizes]
    return pl.pallas_call(
        functools.partial(whiten_kernel, sizes),
        in_specs=[pl.BlockSpec(memory_space=pltpu.SMEM)] + [pl.BlockSpec(memory_space=pl.ANY)] * 3,
        out_specs=[pl.BlockSpec(memory_space=pltpu.VMEM)] * len(rows),
        scratch_shapes=[
            pltpu.VMEM((PAD + samples // 2, 4 * NB), jnp.float32),
            pltpu.VMEM((pieces, block, samples), jnp.bfloat16),
            pltpu.VMEM((1, channels), jnp.int32),
            pltpu.VMEM((samples, 2 * NB), jnp.bfloat16),
            pltpu.VMEM((pieces, 2 * NB, block), jnp.float32),
            pltpu.SemaphoreType.DMA((2 + pieces,)),
        ],
        out_shape=[jax.ShapeDtypeStruct((count, channels), jnp.float32) for count in rows],
        compiler_params=pltpu.CompilerParams(vmem_limit_bytes=32 * 2**20),
        cost_estimate=pl.CostEstimate(
            flops=4 * NB * samples * channels, bytes_accessed=2 * samples * channels, transcendentals=0
        ),
        name="whiten",
    )(offsets, *(
        pltpu.with_memory_space_constraint(x, pltpu.HBM)
        for x in (padded_table(samples), records, live.reshape(1, channels))
    ))


def split(values):
    high = values.astype(jnp.bfloat16).astype(jnp.float32)
    return high, values - high


def cross_kernel(size, first, turn_ref, own_low, own_high, mirror_low, mirror_high, *refs):
    out_hbm, held, left, right, picked, done, sems = refs[-7:]
    half = own_low.shape[0]
    windows = 2 * half
    rows = 2 * GROUP
    terms = windows * rows
    depth, channels = right.shape[1:]
    width = left.shape[1]
    height = done.shape[2]
    tile = min(256, height)
    pieces = [(q, t) for q in range(2) for t in range(height // tile)]

    def gather(low, high, turn, at):
        for w in range(windows):
            part = (low if w < half else high)[w % half, pl.ds(at, rows), :]
            held[pl.ds(pl.multiple_of((w ^ turn) * rows, 8), rows), :] = part
        return held[...]

    def copy(at_step, slot, q, t):
        target = pl.ds(pl.multiple_of(at_step % 2 * height + t * tile, tile), tile)
        return pltpu.make_async_copy(
            done.at[slot, q, pl.ds(t * tile, tile)],
            out_hbm.at[first + at_step // 2, q, target],
            sems.at[slot, q * (height // tile) + t],
        )

    picked[:, width:] = jnp.zeros((height, depth - width), jnp.bfloat16)
    right[:, 3 * terms :] = jnp.zeros((2, depth - 3 * terms, channels), jnp.bfloat16)

    def prepare(at):
        high, low = split(gather(own_low, own_high, 0, at) * (1.0 / windows))
        blank = [jnp.zeros((width - 3 * terms, channels), jnp.float32)] if width > 3 * terms else []
        left[...] = jnp.concatenate([high, high, low, *blank], axis=0).T.astype(jnp.bfloat16)
        values = gather(mirror_low, mirror_high, turn_ref[0], at)
        part = lax.broadcasted_iota(jnp.int32, values.shape, 0) % 2
        turned = jnp.where(part == 0, -pltpu.roll(values, terms - 1, 0), pltpu.roll(values, 1, 0))
        for q, block in enumerate((values, turned)):
            high, low = split(block)
            right[q, : 3 * terms] = jnp.concatenate([high, low, high], axis=0).astype(jnp.bfloat16)

    def body(step, carry, cuts=1):
        slot, inner = step % BUFFERS, step // 2 % GROUP
        top = pl.multiple_of(step % 2 * height, height)

        @pl.when(step % (2 * GROUP) == 0)
        def _():
            prepare(pl.multiple_of(step, rows))

        @pl.when(step >= BUFFERS)
        def _():
            for q, t in pieces:
                copy(step - BUFFERS, slot, q, t).wait()

        lane = lax.broadcasted_iota(jnp.int32, (1, width), 1)
        mask = jnp.where(lane % rows // 2 == inner, 1.0, 0.0).astype(jnp.bfloat16)
        picked[:, :width] = left[pl.ds(top, height), :] * mask

        def multiply(cut, *accs):
            def stage(number):
                n, k = stages[number]
                for q in range(2):
                    held_block = right[q, k * 256 : (k + 1) * 256, n * 256 : (n + 1) * 256]
                    pltpu.matmul_push_rhs(held_block, number % 2, q)

            def retire(n, j, place):
                for q in range(2):
                    done[slot, q, j * CHUNK : (j + 1) * CHUNK, n * 256 : (n + 1) * 256] = pltpu.matmul_pop(
                        accs[q * SLOTS + place]
                    ).astype(jnp.bfloat16)

            chunks, deep = height // CHUNK // cuts, depth // 256
            stages = [(n, k) for n in range(channels // 256) for k in range(deep)]
            waiting = []
            stage(0)
            for number, (n, k) in enumerate(stages):
                for j in range(cut * chunks, (cut + 1) * chunks):
                    place = (n * chunks + j) % SLOTS
                    if k == 0 and len(waiting) > SLOTS // 2:
                        retire(*waiting.pop(0))
                    for q in range(2):
                        pltpu.matmul_acc_lhs(
                            accs[q * SLOTS + place],
                            picked[j * CHUNK : (j + 1) * CHUNK, k * 256 : (k + 1) * 256],
                            load_staged_rhs=number % 2 if j == cut * chunks else None,
                        )
                    if j == cut * chunks and number + 1 < len(stages):
                        stage(number + 1)
                    if k == deep - 1:
                        waiting.append((n, j, place))
            for entry in waiting:
                retire(*entry)

        accs = [pltpu.ACC(q)((CHUNK, 256), jnp.float32) for q in range(2) for _ in range(SLOTS)]
        share = len(pieces) // 2 // cuts
        for cut in range(cuts):
            pl.run_scoped(functools.partial(multiply, cut), *accs)
            for q, t in pieces:
                if t // share == cut:
                    copy(step, slot, q, t).start(priority=t % 2)
        return carry

    body(jnp.int32(0), 0, height // tile)
    lax.fori_loop(1, 2 * size, body, 0)
    for last in range(2 * size - BUFFERS, 2 * size):
        for q, t in pieces:
            copy(last, last % BUFFERS, q, t).wait()


def cross(turn, own, mirror, so_far, first, size, bins):
    windows = 2 * own[0].shape[0]
    channels = own[0].shape[2]
    terms = windows * 2 * GROUP
    width = -(-3 * terms // 128) * 128
    depth = -(-3 * terms // 256) * 256
    height = channels // 2
    previous = [] if so_far is None else [so_far]
    return pl.pallas_call(
        functools.partial(cross_kernel, size, first),
        in_specs=[pl.BlockSpec(memory_space=pltpu.SMEM)]
        + [pl.BlockSpec(memory_space=pltpu.VMEM)] * 4
        + [pl.BlockSpec(memory_space=pl.ANY)] * len(previous),
        out_specs=pl.BlockSpec(memory_space=pl.ANY),
        scratch_shapes=[
            pltpu.VMEM((terms, channels), jnp.float32),
            pltpu.VMEM((channels, width), jnp.bfloat16),
            pltpu.VMEM((2, depth, channels), jnp.bfloat16),
            pltpu.VMEM((height, depth), jnp.bfloat16),
            pltpu.VMEM((BUFFERS, 2, height, channels), jnp.bfloat16),
            pltpu.SemaphoreType.DMA((BUFFERS, 2 * (height // min(256, height)))),
        ],
        out_shape=jax.ShapeDtypeStruct((bins, 2, channels, channels), jnp.bfloat16),
        input_output_aliases={5: 0} if previous else {},
        compiler_params=pltpu.CompilerParams(vmem_limit_bytes=48 * 2**20),
        cost_estimate=pl.CostEstimate(
            flops=2 * size * 2 * channels * channels * 256,
            bytes_accessed=4 * size * channels * channels,
            transcendentals=0,
        ),
        name="cross",
    )(turn, *own, *mirror, *previous)


def exchange(block, axis, distance):
    n = lax.axis_size(axis)
    return lax.ppermute(block, axis, [(i, i ^ distance) for i in range(n)])


def double(held, axis):
    distance = 1
    while distance < lax.axis_size(axis) // 2:
        held = jnp.concatenate([held, exchange(held, axis, distance)])
        distance *= 2
    return held


def per_device(records, offsets, live_flags):
    row, col = lax.axis_index("row"), lax.axis_index("col")
    n = lax.axis_size("col")
    bins = NB // lax.axis_size("bin")
    sizes = (GROUP, bins - GROUP)
    across = [n // 2 if (c ^ c >> 1) & 1 else n // 4 for c in range(n)]
    turn = (row ^ col ^ jnp.where((col ^ col >> 1) & 1 == 1, n // 2, n // 4)).reshape(1)
    swap = [(r * n + w, (w ^ across[r]) * n + r) for r in range(n) for w in range(n)]
    parts = []
    for block in whiten(records, offsets, live_flags, sizes):
        other = lax.ppermute(block, ("row", "col"), swap)
        pairs = []
        for x, axis in ((block, "col"), (other, "row")):
            near = double(x[None], axis)
            pairs.append((near, exchange(near, axis, n // 2)))
        parts.append(pairs)
    out, first = None, 0
    for size, (own, mirror) in zip(sizes, parts):
        out = cross(turn, own, mirror, out, first, size, bins)
        first += size
    return out


def solution(mesh):
    in_specs = (P("row", "col"), P("col"), P("row"))
    out_specs = P("bin", None, "row", "col")
    return jax.shard_map(
        per_device, mesh=mesh, in_specs=in_specs, out_specs=out_specs, check_vma=False
    )
```

```python
import functools
import math

import jax
import jax.numpy as jnp
import numpy as np
from jax import lax
from jax.experimental import pallas as pl
from jax.experimental.pallas import tpu as pltpu
from jax.sharding import PartitionSpec as P

L = 1500
NB = 32
BSTEP = 6
EPSILON = 1e-05
PAD = 168
GROUP = 4
CHUNK = 128
BUFFERS = 3
SLOTS = 8


def padded_table(samples):
    k = (np.arange(NB) + 1) * BSTEP
    n = np.arange(L)
    angle = (k[:, None] * n[None, :] % L) * (2.0 * math.pi / L)
    taper = 0.5 - 0.5 * np.cos(n * (2.0 * math.pi / L))
    parts = np.stack([np.cos(angle) * taper, -np.sin(angle) * taper], axis=1)
    table = np.zeros((PAD + samples, 2 * NB), np.float32)
    table[PAD : PAD + L] = parts.reshape(2 * NB, L).T
    table = np.concatenate([table[: PAD + samples // 2], table[samples // 2 :]], axis=1)
    return jnp.asarray(table.astype(jnp.bfloat16).astype(np.float32))


def whiten_kernel(sizes, offset_ref, table_hbm, records_hbm, live_hbm, *refs):
    outs, (table, records, live, shifted, product, sems) = refs[:-6], refs[-6:]
    pieces, block, samples = records.shape
    copies = [
        pltpu.make_async_copy(table_hbm, table, sems.at[0]),
        pltpu.make_async_copy(live_hbm, live, sems.at[1]),
    ]
    for i in range(pieces):
        source = records_hbm.at[pl.ds(i * block, block)]
        copies.append(pltpu.make_async_copy(source, records.at[i], sems.at[2 + i]))
    for copy in copies:
        copy.start()
    copies[0].wait()
    turned = table[pl.ds(PAD - offset_ref[0], samples // 2), :].astype(jnp.bfloat16)
    shifted[: samples // 2] = turned[:, : 2 * NB]
    shifted[samples // 2 :] = turned[:, 2 * NB :]
    copies[1].wait()
    start = pl.multiple_of(lax.axis_index("bin") * (2 * sum(sizes)), 8)
    for i in range(pieces):
        copies[2 + i].wait()
        spectra = jnp.dot(records[i], shifted[...], preferred_element_type=jnp.float32).T
        product[i] = spectra
        energy = jnp.sum(spectra * spectra, axis=0, keepdims=True) / (2 * NB)
        columns = slice(i * block, (i + 1) * block)
        scaling = live[:, columns].astype(jnp.float32) / jnp.sqrt(energy + EPSILON)
        at = 0
        for size, out in zip(sizes, outs):
            rows = pl.ds(pl.multiple_of(start + at, 8), 2 * size)
            out[:, columns] = product[i, rows, :] * scaling
            at += 2 * size


def whiten(records, offsets, live, sizes):
    channels, samples = records.shape
    block = min(256, channels)
    pieces = channels // block
    rows = [2 * size for size in sizes]
    return pl.pallas_call(
        functools.partial(whiten_kernel, sizes),
        in_specs=[pl.BlockSpec(memory_space=pltpu.SMEM)] + [pl.BlockSpec(memory_space=pl.ANY)] * 3,
        out_specs=[pl.BlockSpec(memory_space=pltpu.VMEM)] * len(rows),
        scratch_shapes=[
            pltpu.VMEM((PAD + samples // 2, 4 * NB), jnp.float32),
            pltpu.VMEM((pieces, block, samples), jnp.bfloat16),
            pltpu.VMEM((1, channels), jnp.int32),
            pltpu.VMEM((samples, 2 * NB), jnp.bfloat16),
            pltpu.VMEM((pieces, 2 * NB, block), jnp.float32),
            pltpu.SemaphoreType.DMA((2 + pieces,)),
        ],
        out_shape=[jax.ShapeDtypeStruct((count, channels), jnp.float32) for count in rows],
        compiler_params=pltpu.CompilerParams(vmem_limit_bytes=32 * 2**20),
        cost_estimate=pl.CostEstimate(
            flops=4 * NB * samples * channels, bytes_accessed=2 * samples * channels, transcendentals=0
        ),
        name="whiten",
    )(offsets, *(
        pltpu.with_memory_space_constraint(x, pltpu.HBM)
        for x in (padded_table(samples), records, live.reshape(1, channels))
    ))


def split(values):
    high = values.astype(jnp.bfloat16).astype(jnp.float32)
    return high, values - high


def cross_kernel(size, first, turn_ref, own_low, own_high, mirror_low, mirror_high, *refs):
    out_hbm, held, left, right, picked, done, sems = refs[-7:]
    half = own_low.shape[0]
    windows = 2 * half
    rows = 2 * GROUP
    terms = windows * rows
    depth, channels = right.shape[1:]
    width = left.shape[1]
    height = done.shape[2]
    tile = min(256, height)
    pieces = [(q, t) for q in range(2) for t in range(height // tile)]

    def gather(low, high, turn, at):
        for w in range(windows):
            part = (low if w < half else high)[w % half, pl.ds(at, rows), :]
            held[pl.ds(pl.multiple_of((w ^ turn) * rows, 8), rows), :] = part
        return held[...]

    def copy(at_step, slot, q, t):
        piece = pl.ds(t * tile, tile)
        return pltpu.make_async_copy(
            done.at[slot, q, piece],
            out_hbm.at[first + at_step, q, piece],
            sems.at[slot, q * (height // tile) + t],
        )

    picked[:, width:] = jnp.zeros((height, depth - width), jnp.bfloat16)
    right[:, 3 * terms :] = jnp.zeros((2, depth - 3 * terms, channels), jnp.bfloat16)

    def prepare(at):
        high, low = split(gather(own_low, own_high, 0, at) * (1.0 / windows))
        blank = [jnp.zeros((width - 3 * terms, channels), jnp.float32)] if width > 3 * terms else []
        left[...] = jnp.concatenate([high, high, low, *blank], axis=0).T.astype(jnp.bfloat16)
        values = gather(mirror_low, mirror_high, turn_ref[0], at)
        part = lax.broadcasted_iota(jnp.int32, values.shape, 0) % 2
        turned = jnp.where(part == 0, -pltpu.roll(values, terms - 1, 0), pltpu.roll(values, 1, 0))
        for q, block in enumerate((values, turned)):
            high, low = split(block)
            right[q, : 3 * terms] = jnp.concatenate([high, low, high], axis=0).astype(jnp.bfloat16)

    def body(step, carry, cuts=1):
        slot, inner = step % BUFFERS, step % GROUP

        @pl.when(inner == 0)
        def _():
            prepare(pl.multiple_of(step * 2, rows))

        @pl.when(step >= BUFFERS)
        def _():
            for q, t in pieces:
                copy(step - BUFFERS, slot, q, t).wait()

        lane = lax.broadcasted_iota(jnp.int32, (1, width), 1)
        mask = jnp.where(lane % rows // 2 == inner, 1.0, 0.0).astype(jnp.bfloat16)
        picked[:, :width] = left[...] * mask

        def multiply(cut, *accs):
            def stage(number):
                n, k = stages[number]
                for q in range(2):
                    held_block = right[q, k * 256 : (k + 1) * 256, n * 256 : (n + 1) * 256]
                    pltpu.matmul_push_rhs(held_block, number % 2, q)

            def retire(n, j, place):
                for q in range(2):
                    done[slot, q, j * CHUNK : (j + 1) * CHUNK, n * 256 : (n + 1) * 256] = pltpu.matmul_pop(
                        accs[q * SLOTS + place]
                    ).astype(jnp.bfloat16)

            chunks, deep = height // CHUNK // cuts, depth // 256
            stages = [(n, k) for n in range(channels // 256) for k in range(deep)]
            waiting = []
            stage(0)
            for number, (n, k) in enumerate(stages):
                for j in range(cut * chunks, (cut + 1) * chunks):
                    place = (n * chunks + j) % SLOTS
                    if k == 0 and len(waiting) > SLOTS // 2:
                        retire(*waiting.pop(0))
                    for q in range(2):
                        pltpu.matmul_acc_lhs(
                            accs[q * SLOTS + place],
                            picked[j * CHUNK : (j + 1) * CHUNK, k * 256 : (k + 1) * 256],
                            load_staged_rhs=number % 2 if j == cut * chunks else None,
                        )
                    if j == cut * chunks and number + 1 < len(stages):
                        stage(number + 1)
                    if k == deep - 1:
                        waiting.append((n, j, place))
            for entry in waiting:
                retire(*entry)

        accs = [pltpu.ACC(q)((CHUNK, 256), jnp.float32) for q in range(2) for _ in range(SLOTS)]
        share = len(pieces) // 2 // cuts
        for cut in range(cuts):
            pl.run_scoped(functools.partial(multiply, cut), *accs)
            for q, t in pieces:
                if t // share == cut:
                    copy(step, slot, q, t).start(priority=t % 2)
        return carry

    body(jnp.int32(0), 0, height // tile)
    lax.fori_loop(1, size, body, 0)
    for last in range(size - BUFFERS, size):
        for q, t in pieces:
            copy(last, last % BUFFERS, q, t).wait()


def cross(turn, own, mirror, so_far, first, size, bins):
    windows = 2 * own[0].shape[0]
    channels = own[0].shape[2]
    terms = windows * 2 * GROUP
    width = -(-3 * terms // 128) * 128
    depth = -(-3 * terms // 256) * 256
    height = channels
    previous = [] if so_far is None else [so_far]
    return pl.pallas_call(
        functools.partial(cross_kernel, size, first),
        in_specs=[pl.BlockSpec(memory_space=pltpu.SMEM)]
        + [pl.BlockSpec(memory_space=pltpu.VMEM)] * 4
        + [pl.BlockSpec(memory_space=pl.ANY)] * len(previous),
        out_specs=pl.BlockSpec(memory_space=pl.ANY),
        scratch_shapes=[
            pltpu.VMEM((terms, channels), jnp.float32),
            pltpu.VMEM((channels, width), jnp.bfloat16),
            pltpu.VMEM((2, depth, channels), jnp.bfloat16),
            pltpu.VMEM((height, depth), jnp.bfloat16),
            pltpu.VMEM((BUFFERS, 2, height, channels), jnp.bfloat16),
            pltpu.SemaphoreType.DMA((BUFFERS, 2 * (height // min(256, height)))),
        ],
        out_shape=jax.ShapeDtypeStruct((bins, 2, channels, channels), jnp.bfloat16),
        input_output_aliases={5: 0} if previous else {},
        compiler_params=pltpu.CompilerParams(vmem_limit_bytes=48 * 2**20),
        cost_estimate=pl.CostEstimate(
            flops=2 * size * 2 * channels * channels * 256,
            bytes_accessed=4 * size * channels * channels,
            transcendentals=0,
        ),
        name="cross",
    )(turn, *own, *mirror, *previous)


def exchange(block, axis, distance):
    n = lax.axis_size(axis)
    return lax.ppermute(block, axis, [(i, i ^ distance) for i in range(n)])


def double(held, axis):
    distance = 1
    while distance < lax.axis_size(axis) // 2:
        held = jnp.concatenate([held, exchange(held, axis, distance)])
        distance *= 2
    return held


def per_device(records, offsets, live_flags):
    row, col = lax.axis_index("row"), lax.axis_index("col")
    n = lax.axis_size("col")
    bins = NB // lax.axis_size("bin")
    sizes = (GROUP, bins - GROUP)
    across = [n // 4 if (c ^ c >> 1) & 1 else n // 2 for c in range(n)]
    turn = (row ^ col ^ jnp.where((col ^ col >> 1) & 1 == 1, n // 4, n // 2)).reshape(1)
    swap = [(r * n + w, (w ^ across[r]) * n + r) for r in range(n) for w in range(n)]
    parts = []
    for block in whiten(records, offsets, live_flags, sizes):
        other = lax.ppermute(block, ("row", "col"), swap)
        pairs = []
        for x, axis in ((block, "col"), (other, "row")):
            near = double(x[None], axis)
            pairs.append((near, exchange(near, axis, n // 2)))
        parts.append(pairs)
    out, first = None, 0
    for size, (own, mirror) in zip(sizes, parts):
        out = cross(turn, own, mirror, out, first, size, bins)
        first += size
    return out


def solution(mesh):
    in_specs = (P("row", "col"), P("col"), P("row"))
    out_specs = P("bin", None, "row", "col")
    return jax.shard_map(
        per_device, mesh=mesh, in_specs=in_specs, out_specs=out_specs, check_vma=False
    )
```

```python
import functools
import math

import jax
import jax.numpy as jnp
import numpy as np
from jax import lax
from jax.experimental import pallas as pl
from jax.experimental.pallas import tpu as pltpu
from jax.sharding import PartitionSpec as P

L = 1500
NB = 32
BSTEP = 6
EPSILON = 1e-05
PAD = 168
GROUP = 4
CHUNK = 128
BUFFERS = 3
SLOTS = 8


def padded_table(samples):
    k = (np.arange(NB) + 1) * BSTEP
    n = np.arange(L)
    angle = (k[:, None] * n[None, :] % L) * (2.0 * math.pi / L)
    taper = 0.5 - 0.5 * np.cos(n * (2.0 * math.pi / L))
    parts = np.stack([np.cos(angle) * taper, -np.sin(angle) * taper], axis=1)
    table = np.zeros((PAD + samples, 2 * NB), np.float32)
    table[PAD : PAD + L] = parts.reshape(2 * NB, L).T
    table = np.concatenate([table[: PAD + samples // 2], table[samples // 2 :]], axis=1)
    return jnp.asarray(table.astype(jnp.bfloat16).astype(np.float32))


def whiten_kernel(sizes, offset_ref, table_hbm, records_hbm, live_hbm, *refs):
    outs, (table, records, live, shifted, product, sems) = refs[:-6], refs[-6:]
    pieces, block, samples = records.shape
    copies = [
        pltpu.make_async_copy(table_hbm, table, sems.at[0]),
        pltpu.make_async_copy(live_hbm, live, sems.at[1]),
    ]
    for i in range(pieces):
        source = records_hbm.at[pl.ds(i * block, block)]
        copies.append(pltpu.make_async_copy(source, records.at[i], sems.at[2 + i]))
    for copy in copies:
        copy.start()
    copies[0].wait()
    turned = table[pl.ds(PAD - offset_ref[0], samples // 2), :].astype(jnp.bfloat16)
    shifted[: samples // 2] = turned[:, : 2 * NB]
    shifted[samples // 2 :] = turned[:, 2 * NB :]
    copies[1].wait()
    start = pl.multiple_of(lax.axis_index("bin") * (2 * sum(sizes)), 8)
    for i in range(pieces):
        copies[2 + i].wait()
        spectra = jnp.dot(records[i], shifted[...], preferred_element_type=jnp.float32).T
        product[i] = spectra
        energy = jnp.sum(spectra * spectra, axis=0, keepdims=True) / (2 * NB)
        columns = slice(i * block, (i + 1) * block)
        scaling = live[:, columns].astype(jnp.float32) / jnp.sqrt(energy + EPSILON)
        at = 0
        for size, out in zip(sizes, outs):
            rows = pl.ds(pl.multiple_of(start + at, 8), 2 * size)
            out[:, columns] = product[i, rows, :] * scaling
            at += 2 * size


def whiten(records, offsets, live, sizes):
    channels, samples = records.shape
    block = min(256, channels)
    pieces = channels // block
    rows = [2 * size for size in sizes]
    return pl.pallas_call(
        functools.partial(whiten_kernel, sizes),
        in_specs=[pl.BlockSpec(memory_space=pltpu.SMEM)] + [pl.BlockSpec(memory_space=pl.ANY)] * 3,
        out_specs=[pl.BlockSpec(memory_space=pltpu.VMEM)] * len(rows),
        scratch_shapes=[
            pltpu.VMEM((PAD + samples // 2, 4 * NB), jnp.float32),
            pltpu.VMEM((pieces, block, samples), jnp.bfloat16),
            pltpu.VMEM((1, channels), jnp.int32),
            pltpu.VMEM((samples, 2 * NB), jnp.bfloat16),
            pltpu.VMEM((pieces, 2 * NB, block), jnp.float32),
            pltpu.SemaphoreType.DMA((2 + pieces,)),
        ],
        out_shape=[jax.ShapeDtypeStruct((count, channels), jnp.float32) for count in rows],
        compiler_params=pltpu.CompilerParams(vmem_limit_bytes=32 * 2**20),
        cost_estimate=pl.CostEstimate(
            flops=4 * NB * samples * channels, bytes_accessed=2 * samples * channels, transcendentals=0
        ),
        name="whiten",
    )(offsets, *(
        pltpu.with_memory_space_constraint(x, pltpu.HBM)
        for x in (padded_table(samples), records, live.reshape(1, channels))
    ))


def split(values):
    high = values.astype(jnp.bfloat16).astype(jnp.float32)
    return high, values - high


def cross_kernel(size, first, turn_ref, own_low, own_high, mirror_low, mirror_high, *refs):
    out_hbm, held, left, right, picked, done, sems = refs[-7:]
    half = own_low.shape[0]
    windows = 2 * half
    rows = 2 * GROUP
    terms = windows * rows
    depth, channels = right.shape[1:]
    width = left.shape[1]
    height = done.shape[2]
    tile = min(256, height)
    pieces = [(q, t) for q in range(2) for t in range(height // tile)]

    def gather(low, high, turn, at):
        for w in range(windows):
            part = (low if w < half else high)[w % half, pl.ds(at, rows), :]
            held[pl.ds(pl.multiple_of((w ^ turn) * rows, 8), rows), :] = part
        return held[...]

    def copy(at_step, slot, q, t):
        piece = pl.ds(t * tile, tile)
        return pltpu.make_async_copy(
            done.at[slot, q, piece],
            out_hbm.at[first + at_step, q, piece],
            sems.at[slot, q * (height // tile) + t],
        )

    picked[:, width:] = jnp.zeros((height, depth - width), jnp.bfloat16)
    right[:, 3 * terms :] = jnp.zeros((2, depth - 3 * terms, channels), jnp.bfloat16)

    def prepare(at):
        high, low = split(gather(own_low, own_high, 0, at) * (1.0 / windows))
        blank = [jnp.zeros((width - 3 * terms, channels), jnp.float32)] if width > 3 * terms else []
        left[...] = jnp.concatenate([high, high, low, *blank], axis=0).T.astype(jnp.bfloat16)
        values = gather(mirror_low, mirror_high, turn_ref[0], at)
        part = lax.broadcasted_iota(jnp.int32, values.shape, 0) % 2
        turned = jnp.where(part == 0, -pltpu.roll(values, terms - 1, 0), pltpu.roll(values, 1, 0))
        for q, block in enumerate((values, turned)):
            high, low = split(block)
            right[q, : 3 * terms] = jnp.concatenate([high, low, high], axis=0).astype(jnp.bfloat16)

    def body(step, carry, cuts=1):
        slot, inner = step % BUFFERS, step % GROUP

        @pl.when(inner == 0)
        def _():
            prepare(pl.multiple_of(step * 2, rows))

        @pl.when(step >= BUFFERS)
        def _():
            for q, t in pieces:
                copy(step - BUFFERS, slot, q, t).wait()

        lane = lax.broadcasted_iota(jnp.int32, (1, width), 1)
        mask = jnp.where(lane % rows // 2 == inner, 1.0, 0.0).astype(jnp.bfloat16)
        picked[:, :width] = left[...] * mask

        def multiply(cut, *accs):
            def stage(number):
                n, k = stages[number]
                for q in range(2):
                    held_block = right[q, k * 256 : (k + 1) * 256, n * 256 : (n + 1) * 256]
                    pltpu.matmul_push_rhs(held_block, number % 2, q)

            def retire(n, j, place):
                for q in range(2):
                    done[slot, q, j * CHUNK : (j + 1) * CHUNK, n * 256 : (n + 1) * 256] = pltpu.matmul_pop(
                        accs[q * SLOTS + place]
                    ).astype(jnp.bfloat16)

            chunks, deep = height // CHUNK // cuts, depth // 256
            stages = [(n, k) for n in range(channels // 256) for k in range(deep)]
            waiting = []
            stage(0)
            for number, (n, k) in enumerate(stages):
                for j in range(cut * chunks, (cut + 1) * chunks):
                    place = (n * chunks + j) % SLOTS
                    if k == 0 and len(waiting) > SLOTS // 2:
                        retire(*waiting.pop(0))
                    for q in range(2):
                        pltpu.matmul_acc_lhs(
                            accs[q * SLOTS + place],
                            picked[j * CHUNK : (j + 1) * CHUNK, k * 256 : (k + 1) * 256],
                            load_staged_rhs=number % 2 if j == cut * chunks else None,
                        )
                    if j == cut * chunks and number + 1 < len(stages):
                        stage(number + 1)
                    if k == deep - 1:
                        waiting.append((n, j, place))
            for entry in waiting:
                retire(*entry)

        accs = [pltpu.ACC(q)((CHUNK, 256), jnp.float32) for q in range(2) for _ in range(SLOTS)]
        share = len(pieces) // 2 // cuts
        for cut in range(cuts):
            pl.run_scoped(functools.partial(multiply, cut), *accs)
            for q, t in pieces:
                if t // share == cut:
                    copy(step, slot, q, t).start(priority=t % 2)
        return carry

    lax.fori_loop(0, size - 1, body, 0)
    body(jnp.int32(size - 1), 0, min(2, height // tile))
    for last in range(size - BUFFERS, size):
        for q, t in pieces:
            copy(last, last % BUFFERS, q, t).wait()


def cross(turn, own, mirror, so_far, first, size, bins):
    windows = 2 * own[0].shape[0]
    channels = own[0].shape[2]
    terms = windows * 2 * GROUP
    width = -(-3 * terms // 128) * 128
    depth = -(-3 * terms // 256) * 256
    height = channels
    previous = [] if so_far is None else [so_far]
    return pl.pallas_call(
        functools.partial(cross_kernel, size, first),
        in_specs=[pl.BlockSpec(memory_space=pltpu.SMEM)]
        + [pl.BlockSpec(memory_space=pltpu.VMEM)] * 4
        + [pl.BlockSpec(memory_space=pl.ANY)] * len(previous),
        out_specs=pl.BlockSpec(memory_space=pl.ANY),
        scratch_shapes=[
            pltpu.VMEM((terms, channels), jnp.float32),
            pltpu.VMEM((channels, width), jnp.bfloat16),
            pltpu.VMEM((2, depth, channels), jnp.bfloat16),
            pltpu.VMEM((height, depth), jnp.bfloat16),
            pltpu.VMEM((BUFFERS, 2, height, channels), jnp.bfloat16),
            pltpu.SemaphoreType.DMA((BUFFERS, 2 * (height // min(256, height)))),
        ],
        out_shape=jax.ShapeDtypeStruct((bins, 2, channels, channels), jnp.bfloat16),
        input_output_aliases={5: 0} if previous else {},
        compiler_params=pltpu.CompilerParams(vmem_limit_bytes=48 * 2**20),
        cost_estimate=pl.CostEstimate(
            flops=2 * size * 2 * channels * channels * 256,
            bytes_accessed=4 * size * channels * channels,
            transcendentals=0,
        ),
        name="cross",
    )(turn, *own, *mirror, *previous)


def exchange(block, axis, distance):
    n = lax.axis_size(axis)
    return lax.ppermute(block, axis, [(i, i ^ distance) for i in range(n)])


def double(held, axis):
    distance = 1
    while distance < lax.axis_size(axis) // 2:
        held = jnp.concatenate([held, exchange(held, axis, distance)])
        distance *= 2
    return held


def per_device(records, offsets, live_flags):
    row, col = lax.axis_index("row"), lax.axis_index("col")
    n = lax.axis_size("col")
    bins = NB // lax.axis_size("bin")
    sizes = (GROUP, bins - GROUP)
    across = [n // 2 if (c ^ c >> 1) & 1 else n // 4 for c in range(n)]
    turn = (row ^ col ^ jnp.where((col ^ col >> 1) & 1 == 1, n // 2, n // 4)).reshape(1)
    swap = [(r * n + w, (w ^ across[r]) * n + r) for r in range(n) for w in range(n)]
    parts = []
    for block in whiten(records, offsets, live_flags, sizes):
        other = lax.ppermute(block, ("row", "col"), swap)
        pairs = []
        for x, axis in ((block, "col"), (other, "row")):
            near = double(x[None], axis)
            pairs.append((near, exchange(near, axis, n // 2)))
        parts.append(pairs)
    out, first = None, 0
    for size, (own, mirror) in zip(sizes, parts):
        out = cross(turn, own, mirror, out, first, size, bins)
        first += size
    return out


def solution(mesh):
    in_specs = (P("row", "col"), P("col"), P("row"))
    out_specs = P("bin", None, "row", "col")
    return jax.shard_map(
        per_device, mesh=mesh, in_specs=in_specs, out_specs=out_specs, check_vma=False
    )
```

```python
import functools
import math

import jax
import jax.numpy as jnp
import numpy as np
from jax import lax
from jax.experimental import pallas as pl
from jax.experimental.pallas import tpu as pltpu
from jax.sharding import PartitionSpec as P

L = 1500
NB = 32
BSTEP = 6
EPSILON = 1e-05
PAD = 168
GROUP = 4
CHUNK = 128
BUFFERS = 3
SLOTS = 8


def padded_table(samples):
    k = (np.arange(NB) + 1) * BSTEP
    n = np.arange(L)
    angle = (k[:, None] * n[None, :] % L) * (2.0 * math.pi / L)
    taper = 0.5 - 0.5 * np.cos(n * (2.0 * math.pi / L))
    parts = np.stack([np.cos(angle) * taper, -np.sin(angle) * taper], axis=1)
    table = np.zeros((PAD + samples, 2 * NB), np.float32)
    table[PAD : PAD + L] = parts.reshape(2 * NB, L).T
    table = np.concatenate([table[: PAD + samples // 2], table[samples // 2 :]], axis=1)
    return jnp.asarray(table.astype(jnp.bfloat16).astype(np.float32))


def whiten_kernel(sizes, offset_ref, table_hbm, records_hbm, live_hbm, *refs):
    outs, (table, records, live, shifted, product, sems) = refs[:-6], refs[-6:]
    pieces, block, samples = records.shape
    copies = [
        pltpu.make_async_copy(table_hbm, table, sems.at[0]),
        pltpu.make_async_copy(live_hbm, live, sems.at[1]),
    ]
    for i in range(pieces):
        source = records_hbm.at[pl.ds(i * block, block)]
        copies.append(pltpu.make_async_copy(source, records.at[i], sems.at[2 + i]))
    for copy in copies:
        copy.start()
    copies[0].wait()
    turned = table[pl.ds(PAD - offset_ref[0], samples // 2), :].astype(jnp.bfloat16)
    shifted[: samples // 2] = turned[:, : 2 * NB]
    shifted[samples // 2 :] = turned[:, 2 * NB :]
    copies[1].wait()
    start = pl.multiple_of(lax.axis_index("bin") * (2 * sum(sizes)), 8)
    for i in range(pieces):
        copies[2 + i].wait()
        spectra = jnp.dot(records[i], shifted[...], preferred_element_type=jnp.float32).T
        product[i] = spectra
        energy = jnp.sum(spectra * spectra, axis=0, keepdims=True) / (2 * NB)
        columns = slice(i * block, (i + 1) * block)
        scaling = live[:, columns].astype(jnp.float32) / jnp.sqrt(energy + EPSILON)
        at = 0
        for size, out in zip(sizes, outs):
            rows = pl.ds(pl.multiple_of(start + at, 8), 2 * size)
            out[:, columns] = product[i, rows, :] * scaling
            at += 2 * size


def whiten(records, offsets, live, sizes):
    channels, samples = records.shape
    block = min(256, channels)
    pieces = channels // block
    rows = [2 * size for size in sizes]
    return pl.pallas_call(
        functools.partial(whiten_kernel, sizes),
        in_specs=[pl.BlockSpec(memory_space=pltpu.SMEM)] + [pl.BlockSpec(memory_space=pl.ANY)] * 3,
        out_specs=[pl.BlockSpec(memory_space=pltpu.VMEM)] * len(rows),
        scratch_shapes=[
            pltpu.VMEM((PAD + samples // 2, 4 * NB), jnp.float32),
            pltpu.VMEM((pieces, block, samples), jnp.bfloat16),
            pltpu.VMEM((1, channels), jnp.int32),
            pltpu.VMEM((samples, 2 * NB), jnp.bfloat16),
            pltpu.VMEM((pieces, 2 * NB, block), jnp.float32),
            pltpu.SemaphoreType.DMA((2 + pieces,)),
        ],
        out_shape=[jax.ShapeDtypeStruct((count, channels), jnp.float32) for count in rows],
        compiler_params=pltpu.CompilerParams(vmem_limit_bytes=32 * 2**20),
        cost_estimate=pl.CostEstimate(
            flops=4 * NB * samples * channels, bytes_accessed=2 * samples * channels, transcendentals=0
        ),
        name="whiten",
    )(offsets, *(
        pltpu.with_memory_space_constraint(x, pltpu.HBM)
        for x in (padded_table(samples), records, live.reshape(1, channels))
    ))


def split(values):
    high = values.astype(jnp.bfloat16).astype(jnp.float32)
    return high, values - high


def cross_kernel(size, first, turn_ref, own_low, own_high, mirror_low, mirror_high, *refs):
    out_hbm, held, left, right, picked, done, sems = refs[-7:]
    half = own_low.shape[0]
    windows = 2 * half
    rows = 2 * GROUP
    terms = windows * rows
    depth, channels = right.shape[1:]
    width = left.shape[1]
    height = done.shape[2]
    tile = min(256, height)
    pieces = [(q, t) for q in range(2) for t in range(height // tile)]

    def gather(low, high, turn, at):
        for w in range(windows):
            part = (low if w < half else high)[w % half, pl.ds(at, rows), :]
            held[pl.ds(pl.multiple_of((w ^ turn) * rows, 8), rows), :] = part
        return held[...]

    def copy(at_step, slot, q, t):
        piece = pl.ds(t * tile, tile)
        return pltpu.make_async_copy(
            done.at[slot, q, piece],
            out_hbm.at[first + at_step, q, piece],
            sems.at[slot, q * (height // tile) + t],
        )

    picked[:, :, width:] = jnp.zeros((2, height, depth - width), jnp.bfloat16)
    right[:, 3 * terms :] = jnp.zeros((2, depth - 3 * terms, channels), jnp.bfloat16)

    def prepare(at):
        high, low = split(gather(own_low, own_high, 0, at) * (1.0 / windows))
        blank = [jnp.zeros((width - 3 * terms, channels), jnp.float32)] if width > 3 * terms else []
        left[...] = jnp.concatenate([high, high, low, *blank], axis=0).T.astype(jnp.bfloat16)
        values = gather(mirror_low, mirror_high, turn_ref[0], at)
        part = lax.broadcasted_iota(jnp.int32, values.shape, 0) % 2
        turned = jnp.where(part == 0, -pltpu.roll(values, terms - 1, 0), pltpu.roll(values, 1, 0))
        for q, block in enumerate((values, turned)):
            high, low = split(block)
            right[q, : 3 * terms] = jnp.concatenate([high, low, high], axis=0).astype(jnp.bfloat16)

    def pick(at_step, inner):
        lane = lax.broadcasted_iota(jnp.int32, (1, width), 1)
        mask = jnp.where(lane % rows // 2 == inner, 1.0, 0.0).astype(jnp.bfloat16)
        picked[at_step % 2, :, :width] = left[...] * mask

    def body(step, carry, cuts=1):
        slot, inner = step % BUFFERS, step % GROUP

        @pl.when(inner == 0)
        def _():
            prepare(pl.multiple_of(step * 2, rows))
            pick(step, 0)

        @pl.when(step >= BUFFERS)
        def _():
            for q, t in pieces:
                copy(step - BUFFERS, slot, q, t).wait()

        def multiply(cut, *accs):
            def stage(number):
                n, k = stages[number]
                for q in range(2):
                    held_block = right[q, k * 256 : (k + 1) * 256, n * 256 : (n + 1) * 256]
                    pltpu.matmul_push_rhs(held_block, number % 2, q)

            def retire(n, j, place):
                for q in range(2):
                    done[slot, q, j * CHUNK : (j + 1) * CHUNK, n * 256 : (n + 1) * 256] = pltpu.matmul_pop(
                        accs[q * SLOTS + place]
                    ).astype(jnp.bfloat16)

            chunks, deep = height // CHUNK // cuts, depth // 256
            stages = [(n, k) for n in range(channels // 256) for k in range(deep)]
            waiting = []
            stage(0)
            for number, (n, k) in enumerate(stages):
                for j in range(cut * chunks, (cut + 1) * chunks):
                    place = (n * chunks + j) % SLOTS
                    if k == 0 and len(waiting) > SLOTS // 2:
                        retire(*waiting.pop(0))
                    for q in range(2):
                        pltpu.matmul_acc_lhs(
                            accs[q * SLOTS + place],
                            picked[step % 2, j * CHUNK : (j + 1) * CHUNK, k * 256 : (k + 1) * 256],
                            load_staged_rhs=number % 2 if j == cut * chunks else None,
                        )
                    if j == cut * chunks and number + 1 < len(stages):
                        stage(number + 1)
                    if k == deep - 1:
                        waiting.append((n, j, place))
            if cut == cuts - 1:
                pick(step + 1, inner + 1)
            for entry in waiting:
                retire(*entry)

        accs = [pltpu.ACC(q)((CHUNK, 256), jnp.float32) for q in range(2) for _ in range(SLOTS)]
        share = len(pieces) // 2 // cuts
        for cut in range(cuts):
            pl.run_scoped(functools.partial(multiply, cut), *accs)
            for q, t in pieces:
                if t // share == cut:
                    copy(step, slot, q, t).start(priority=t % 2)
        return carry

    body(jnp.int32(0), 0, height // tile)
    lax.fori_loop(1, size, body, 0)
    for last in range(size - BUFFERS, size):
        for q, t in pieces:
            copy(last, last % BUFFERS, q, t).wait()


def cross(turn, own, mirror, so_far, first, size, bins):
    windows = 2 * own[0].shape[0]
    channels = own[0].shape[2]
    terms = windows * 2 * GROUP
    width = -(-3 * terms // 128) * 128
    depth = -(-3 * terms // 256) * 256
    height = channels
    previous = [] if so_far is None else [so_far]
    return pl.pallas_call(
        functools.partial(cross_kernel, size, first),
        in_specs=[pl.BlockSpec(memory_space=pltpu.SMEM)]
        + [pl.BlockSpec(memory_space=pltpu.VMEM)] * 4
        + [pl.BlockSpec(memory_space=pl.ANY)] * len(previous),
        out_specs=pl.BlockSpec(memory_space=pl.ANY),
        scratch_shapes=[
            pltpu.VMEM((terms, channels), jnp.float32),
            pltpu.VMEM((channels, width), jnp.bfloat16),
            pltpu.VMEM((2, depth, channels), jnp.bfloat16),
            pltpu.VMEM((2, height, depth), jnp.bfloat16),
            pltpu.VMEM((BUFFERS, 2, height, channels), jnp.bfloat16),
            pltpu.SemaphoreType.DMA((BUFFERS, 2 * (height // min(256, height)))),
        ],
        out_shape=jax.ShapeDtypeStruct((bins, 2, channels, channels), jnp.bfloat16),
        input_output_aliases={5: 0} if previous else {},
        compiler_params=pltpu.CompilerParams(vmem_limit_bytes=48 * 2**20),
        cost_estimate=pl.CostEstimate(
            flops=2 * size * 2 * channels * channels * 256,
            bytes_accessed=4 * size * channels * channels,
            transcendentals=0,
        ),
        name="cross",
    )(turn, *own, *mirror, *previous)


def exchange(block, axis, distance):
    n = lax.axis_size(axis)
    return lax.ppermute(block, axis, [(i, i ^ distance) for i in range(n)])


def double(held, axis):
    distance = 1
    while distance < lax.axis_size(axis) // 2:
        held = jnp.concatenate([held, exchange(held, axis, distance)])
        distance *= 2
    return held


def per_device(records, offsets, live_flags):
    row, col = lax.axis_index("row"), lax.axis_index("col")
    n = lax.axis_size("col")
    bins = NB // lax.axis_size("bin")
    sizes = (GROUP, bins - GROUP)
    across = [n // 4 if (c ^ c >> 1) & 1 else n // 2 for c in range(n)]
    turn = (row ^ col ^ jnp.where((col ^ col >> 1) & 1 == 1, n // 4, n // 2)).reshape(1)
    swap = [(r * n + w, (w ^ across[r]) * n + r) for r in range(n) for w in range(n)]
    parts = []
    for block in whiten(records, offsets, live_flags, sizes):
        other = lax.ppermute(block, ("row", "col"), swap)
        pairs = []
        for x, axis in ((block, "col"), (other, "row")):
            near = double(x[None], axis)
            pairs.append((near, exchange(near, axis, n // 2)))
        parts.append(pairs)
    out, first = None, 0
    for size, (own, mirror) in zip(sizes, parts):
        out = cross(turn, own, mirror, out, first, size, bins)
        first += size
    return out


def solution(mesh):
    in_specs = (P("row", "col"), P("col"), P("row"))
    out_specs = P("bin", None, "row", "col")
    return jax.shard_map(
        per_device, mesh=mesh, in_specs=in_specs, out_specs=out_specs, check_vma=False
    )
```
